32 devices in a mesh: rep: 2 (over y), section: 2 (over core), seq: 8 (over z, x).
Axes of the slice: x: 2, y: 2, z: 4, core: 2. Of those that a mesh axis runs over, the one named last changes fastest.
Arguments:
- qkv_all: bfloat16 [2, 2, 128, 12288], P(None, 'section', ('rep', 'seq')), parts along dimension 2, may hold values from -120 to 120
- context_kv: bfloat16 [128, 8192], P(('rep', 'section', 'seq')), parts along dimension 0, may hold values from -6 to 6
Outputs:
- attended: bfloat16 [2, 2, 128, 4096], P(None, 'section', ('rep', 'seq')), parts along dimension 2
The draws below stay inside these ranges and needn't reach their ends.
There are 2 independent parts, one for each index of `rep`. The reference program is written for one: setup_inputs(seed, part) draws one part's arguments, and reference() takes and returns one part's arrays. A program takes and returns all parts, laid end to end along the dimension named above; each array names one. Nothing has to cross between parts.
All inputs are finite; a program needn't handle non-finite values.
Results may differ from the reference program's by a relative error of at most 0.005.
Values may be sent and summed in bfloat16 or wider, within the bound.
No kernel may reach another device: no remote copies, remote signals or barrier semaphores. Data moves between devices by JAX's collectives and lax.ppermute only.
A program may use at most 64 MiB of HBM per device.

```python
import jax
import jax.numpy as jnp
from jax import lax

HD = 128
HEADS = 32
STEPS = 2
TOKENS = 64
CTX_TOK = 64
N_SECTION = 2


def draw_qkv_all(key, part):
    shape = (STEPS, N_SECTION, TOKENS, HEADS, 3, HD)
    seeds = jax.random.split(key, 1)
    roles = jnp.array([2.5, 1.0, 1.0], jnp.float32).reshape(1, 1, 1, 1, 3, 1)
    base = jnp.clip(jax.random.normal(seeds[0], shape, jnp.float32), -6.0, 6.0) * roles
    return base.reshape(STEPS, N_SECTION, TOKENS, HEADS * 3 * HD).astype(jnp.bfloat16)


def block_levels(own_key, extent, cuts, least, top_value):
    gain = 1.0
    for position, blocks in cuts:
        draws = jax.random.uniform(jax.random.fold_in(jax.random.fold_in(own_key, 6), position), (blocks,), jnp.float32, least / len(cuts), top_value / len(cuts))
        gain = gain * jnp.repeat(jnp.exp(draws), extent[position] // blocks).reshape((-1,) + (1,) * (len(extent) - 1 - position))
    return gain


def centred(own_key, shape, spread, bound, pieces=(), held_as=jnp.bfloat16):
    values = spread * jax.random.normal(own_key, shape, jnp.float32)
    if pieces:
        values = values * block_levels(own_key, shape, pieces, -0.22, 0.18)
    return jnp.clip(values, -bound, bound).astype(held_as)


def setup_inputs(seed: int = 0, part: int = 0) -> dict:
    key_list = jax.random.split(jax.random.key(seed), 3)
    part_keys = jax.random.split(jax.random.fold_in(key_list[2], part), 3)
    qkv_all = draw_qkv_all(jax.random.fold_in(jax.random.fold_in(key_list[2], part), 71), part)
    context_kv = centred(part_keys[1], (CTX_TOK, HEADS * 2 * HD), 1.0, 6.0, ((0, 16),))
    return dict(qkv_all=qkv_all, context_kv=context_kv)


def attention(queries, keys, values):
    def one_head(operands):
        q_head, k_head, v_head = operands
        scores = jnp.dot(q_head, k_head.T, preferred_element_type=jnp.float32) * (HD ** -0.5)
        weights = jnp.exp(scores - jnp.max(scores, axis=1, keepdims=True))
        total = jnp.sum(weights, axis=1, keepdims=True)
        mixed = jnp.dot(weights.astype(jnp.bfloat16), v_head, preferred_element_type=jnp.float32)
        return (mixed / total).astype(jnp.bfloat16)

    heads_out = lax.map(one_head, (queries.transpose(1, 0, 2), keys.transpose(1, 0, 2), values.transpose(1, 0, 2)))
    return heads_out.transpose(1, 0, 2).reshape(TOKENS, HEADS * HD)


def reference(qkv_all, context_kv):
    context = context_kv.reshape(CTX_TOK, HEADS, 2, HD)
    earlier_keys = [context[:, :, 0]]
    earlier_vals = [context[:, :, 1]]
    results = []
    for step in range(STEPS):
        per_section = []
        for section in range(N_SECTION):
            frames = qkv_all[step, section].reshape(TOKENS, HEADS, 3, HD)
            keys = jnp.concatenate(earlier_keys + [frames[:, :, 1]], axis=0)
            values = jnp.concatenate(earlier_vals + [frames[:, :, 2]], axis=0)
            per_section.append(attention(frames[:, :, 0], keys, values))
        results.append(jnp.stack(per_section))
        last_frames = qkv_all[step, N_SECTION - 1].reshape(TOKENS, HEADS, 3, HD)
        earlier_keys = earlier_keys + [last_frames[:, :, 1]]
        earlier_vals = earlier_vals + [last_frames[:, :, 2]]
    return jnp.stack(results)
```

```python
import functools

import jax
import jax.numpy as jnp
from jax import lax
from jax.experimental import pallas as pl
from jax.experimental.pallas import tpu as pltpu
from jax.sharding import PartitionSpec as P

HEADS = 32
AXES = ("section", "seq")


def softmax_mix(queries, keys, values, scale):
    scores = (
        lax.dot_general(
            queries, keys, (((1,), (1,)), ((), ())), preferred_element_type=jnp.float32
        )
        * scale
    )
    weights = jnp.exp(scores - jnp.max(scores, axis=1, keepdims=True))
    total = jnp.sum(weights, axis=1, keepdims=True)
    mixed = jnp.dot(weights.astype(jnp.bfloat16), values, preferred_element_type=jnp.float32)
    return (mixed / total).astype(jnp.bfloat16)


def attend_kernel(
    steps, sections, heads, tok_rows, ctx_rows, head_dim, scale, got_ref, out_ref
):
    sources = got_ref.shape[0]
    per_section = sources // sections
    ctx_base = steps * heads * 3 * tok_rows

    def part(step, section, head, role):
        base = ((step * heads + head) * 3 + role) * tok_rows
        block = got_ref[section * per_section : (section + 1) * per_section, base : base + tok_rows]
        return block.reshape(per_section * tok_rows, head_dim)

    ctx_all = got_ref[:, ctx_base:]

    def context(head, role):
        base = (head * 2 + role) * ctx_rows
        return ctx_all[:, base : base + ctx_rows].reshape(sources * ctx_rows, head_dim)

    for head in range(heads):
        earlier_keys = [context(head, 0)]
        earlier_vals = [context(head, 1)]
        for step in range(steps):
            own = [(part(step, s, head, 1), part(step, s, head, 2)) for s in range(sections)]
            for s in range(sections):
                keys = jnp.concatenate(earlier_keys + [own[s][0]], axis=0)
                vals = jnp.concatenate(earlier_vals + [own[s][1]], axis=0)
                mixed = softmax_mix(part(step, s, head, 0), keys, vals, scale)
                base = (step * heads + head) * tok_rows
                out_ref[s * per_section : (s + 1) * per_section, base : base + tok_rows] = (
                    mixed.reshape(per_section, tok_rows, head_dim)
                )
            earlier_keys.append(own[sections - 1][0])
            earlier_vals.append(own[sections - 1][1])


def shards(qkv_all, context_kv):
    sections = lax.axis_size("section")
    peers = sections * lax.axis_size("seq")
    groups = min(peers, HEADS)
    copies = peers // groups
    heads = HEADS // groups
    steps, _, tok_rows, width = qkv_all.shape
    head_dim = width // (3 * HEADS)
    ctx_rows = context_kv.shape[0]
    scale = head_dim ** (-0.5)
    if copies > 1:
        return shards_copied(qkv_all, context_kv, sections, groups, copies, heads, scale)

    blocks = qkv_all[:, 0].reshape(steps, tok_rows, groups, heads * 3, head_dim)
    blocks = blocks.transpose(2, 0, 3, 1, 4).reshape(groups, -1, head_dim)
    ctx = context_kv.reshape(ctx_rows, groups, heads * 2, head_dim)
    ctx = ctx.transpose(1, 2, 0, 3).reshape(groups, -1, head_dim)
    sent = jnp.concatenate([blocks, ctx], axis=1)
    got = lax.all_to_all(sent, AXES, split_axis=0, concat_axis=0, tiled=True)
    mixed = pl.pallas_call(
        functools.partial(
            attend_kernel, steps, sections, heads, tok_rows, ctx_rows, head_dim, scale
        ),
        out_shape=jax.ShapeDtypeStruct((peers, steps * heads * tok_rows, head_dim), jnp.bfloat16),
        in_specs=[pl.BlockSpec(memory_space=pltpu.VMEM)],
        out_specs=pl.BlockSpec(memory_space=pltpu.VMEM),
        compiler_params=pltpu.CompilerParams(vmem_limit_bytes=32 * 1024 * 1024),
    )(got)
    back = lax.all_to_all(mixed, AXES, split_axis=0, concat_axis=0, tiled=True)
    back = back.reshape(groups, steps, heads, tok_rows, head_dim).transpose(1, 3, 0, 2, 4)
    return back.reshape(steps, 1, tok_rows, HEADS * head_dim)


def shards_copied(qkv_all, context_kv, sections, groups, copies, heads, scale):
    steps, _, tok_rows, width = qkv_all.shape
    head_dim = width // (3 * HEADS)
    peers = groups * copies
    share = tok_rows // copies
    ctx_rows = context_kv.shape[0]
    frames = qkv_all[:, 0].reshape(steps, tok_rows, groups, heads, 3, head_dim)
    queries = frames[..., 0, :].reshape(steps, copies, share, groups, heads, head_dim)
    queries = queries.transpose(3, 1, 0, 4, 2, 5).reshape(peers, -1, head_dim)
    key_vals = frames[..., 1:, :].transpose(2, 0, 3, 4, 1, 5).reshape(groups, -1, head_dim)
    ctx = context_kv.reshape(ctx_rows, groups, heads, 2, head_dim)
    ctx = ctx.transpose(1, 2, 3, 0, 4).reshape(groups, -1, head_dim)
    shared = jnp.concatenate([key_vals, ctx], axis=1)
    shared = jnp.broadcast_to(shared[:, None], (groups, copies) + shared.shape[1:])
    shared = shared.reshape((peers,) + shared.shape[2:])
    sent = jnp.concatenate([queries, shared], axis=1)
    got = lax.all_to_all(sent, AXES, split_axis=0, concat_axis=0, tiled=True)
    per_section = peers // sections
    cut = steps * heads * share
    end = cut + steps * heads * 2 * tok_rows
    q = got[:, :cut].reshape(sections, per_section, steps, heads, share, head_dim)
    q = q.transpose(2, 0, 3, 1, 4, 5).reshape(steps, sections, heads, -1, head_dim)
    kv = got[:, cut:end].reshape(sections, per_section, steps, heads, 2, tok_rows, head_dim)
    kv = kv.transpose(2, 0, 4, 3, 1, 5, 6).reshape(steps, sections, 2, heads, -1, head_dim)
    ctx = got[:, end:].reshape(peers, heads, 2, ctx_rows, head_dim)
    earlier = [ctx.transpose(2, 1, 0, 3, 4).reshape(2, heads, -1, head_dim)]
    results = []
    for step in range(steps):
        for s in range(sections):
            keys, vals = jnp.concatenate(earlier + [kv[step, s]], axis=2)
            results.append(
                jnp.stack([softmax_mix(q[step, s, h], keys[h], vals[h], scale) for h in range(heads)])
            )
        earlier = earlier + [kv[step, sections - 1]]
    mixed = jnp.stack(results).reshape(steps, sections, heads, per_section, share, head_dim)
    mixed = mixed.transpose(1, 3, 0, 2, 4, 5).reshape(peers, -1, head_dim)
    back = lax.all_to_all(mixed, AXES, split_axis=0, concat_axis=0, tiled=True)
    back = back.reshape(groups, copies, steps, heads, share, head_dim)
    back = back.transpose(2, 1, 4, 0, 3, 5)
    return back.reshape(steps, 1, tok_rows, HEADS * head_dim)


def solution(mesh):
    in_specs = (P(None, "section", ("rep", "seq"), None), P(("rep", "section", "seq"), None))
    out_specs = P(None, "section", ("rep", "seq"), None)
    return jax.shard_map(shards, mesh=mesh, in_specs=in_specs, out_specs=out_specs, check_vma=False)
```

```python
import functools

import jax
import jax.numpy as jnp
from jax import lax
from jax.experimental import pallas as pl
from jax.experimental.pallas import tpu as pltpu
from jax.sharding import PartitionSpec as P

HEADS = 32
AXES = ("section", "seq")


def softmax_mix(queries, keys, values, scale):
    scores = (
        lax.dot_general(
            queries, keys, (((1,), (1,)), ((), ())), preferred_element_type=jnp.float32
        )
        * scale
    )
    weights = jnp.exp(scores - jnp.max(scores, axis=1, keepdims=True))
    total = jnp.sum(weights, axis=1, keepdims=True)
    mixed = jnp.dot(weights.astype(jnp.bfloat16), values, preferred_element_type=jnp.float32)
    return (mixed / total).astype(jnp.bfloat16)


def attend_kernel(
    steps, sections, heads, tok_rows, ctx_rows, head_dim, scale, got_ref, *refs
):
    out_refs, out_ref = refs[:-1], refs[-1]
    sources = got_ref.shape[0]
    per_section = sources // sections
    ctx_base = steps * heads * 3 * tok_rows

    def part(step, section, head, role):
        base = ((step * heads + head) * 3 + role) * tok_rows
        block = got_ref[section * per_section : (section + 1) * per_section, base : base + tok_rows]
        return block.reshape(per_section * tok_rows, head_dim)

    ctx_all = got_ref[:, ctx_base:]

    def context(head, role):
        base = (head * 2 + role) * ctx_rows
        return ctx_all[:, base : base + ctx_rows].reshape(sources * ctx_rows, head_dim)

    for head in range(heads):
        earlier_keys = [context(head, 0)]
        earlier_vals = [context(head, 1)]
        for step in range(steps):
            own = [(part(step, s, head, 1), part(step, s, head, 2)) for s in range(sections)]
            for s in range(sections):
                keys = jnp.concatenate(earlier_keys + [own[s][0]], axis=0)
                vals = jnp.concatenate(earlier_vals + [own[s][1]], axis=0)
                mixed = softmax_mix(part(step, s, head, 0), keys, vals, scale)
                base = (step * heads + head) * tok_rows
                out_ref[s * per_section : (s + 1) * per_section, base : base + tok_rows] = (
                    mixed.reshape(per_section, tok_rows, head_dim)
                )
            earlier_keys.append(own[sections - 1][0])
            earlier_vals.append(own[sections - 1][1])
    me = lax.axis_index("section") * per_section + lax.axis_index("seq")
    for offset, piece_ref in enumerate(out_refs):
        piece_ref[...] = out_ref[lax.rem(me + offset, sources)]


def place_kernel(steps, sections, heads, tok_rows, head_dim, *refs):
    piece_refs, out_ref = refs[:-1], refs[-1]
    sources = len(piece_refs)
    me = lax.axis_index("section") * (sources // sections) + lax.axis_index("seq")
    for offset, piece_ref in enumerate(piece_refs):
        owner = lax.rem(me + sources - offset, sources)
        for step in range(steps):
            for head in range(heads):
                base = (step * heads + head) * tok_rows
                column = pl.multiple_of((owner * heads + head) * head_dim, head_dim)
                out_ref[step, 0, :, pl.ds(column, head_dim)] = piece_ref[base : base + tok_rows]


def shards(qkv_all, context_kv):
    sections = lax.axis_size("section")
    peers = sections * lax.axis_size("seq")
    groups = min(peers, HEADS)
    copies = peers // groups
    heads = HEADS // groups
    steps, _, tok_rows, width = qkv_all.shape
    head_dim = width // (3 * HEADS)
    ctx_rows = context_kv.shape[0]
    scale = head_dim ** (-0.5)
    if copies > 1:
        return shards_copied(qkv_all, context_kv, sections, groups, copies, heads, scale)

    blocks = qkv_all[:, 0].reshape(steps, tok_rows, groups, heads * 3, head_dim)
    blocks = blocks.transpose(2, 0, 3, 1, 4).reshape(groups, -1, head_dim)
    ctx = context_kv.reshape(ctx_rows, groups, heads * 2, head_dim)
    ctx = ctx.transpose(1, 2, 0, 3).reshape(groups, -1, head_dim)
    sent = jnp.concatenate([blocks, ctx], axis=1)
    got = lax.all_to_all(sent, AXES, split_axis=0, concat_axis=0, tiled=True)
    piece = jax.ShapeDtypeStruct((steps * heads * tok_rows, head_dim), jnp.bfloat16)
    in_vmem = pl.BlockSpec(memory_space=pltpu.VMEM)
    pieces = pl.pallas_call(
        functools.partial(
            attend_kernel, steps, sections, heads, tok_rows, ctx_rows, head_dim, scale
        ),
        out_shape=[piece] * peers,
        in_specs=[in_vmem],
        out_specs=[in_vmem] * peers,
        scratch_shapes=[pltpu.VMEM((peers,) + piece.shape, jnp.bfloat16)],
        compiler_params=pltpu.CompilerParams(vmem_limit_bytes=32 * 1024 * 1024),
    )(got)
    came = [pieces[0]]
    for offset in range(1, peers):
        came.append(
            lax.ppermute(pieces[offset], AXES, [(i, (i + offset) % peers) for i in range(peers)])
        )
    return pl.pallas_call(
        functools.partial(place_kernel, steps, sections, heads, tok_rows, head_dim),
        out_shape=jax.ShapeDtypeStruct((steps, 1, tok_rows, HEADS * head_dim), jnp.bfloat16),
        in_specs=[in_vmem] * peers,
        out_specs=in_vmem,
        compiler_params=pltpu.CompilerParams(vmem_limit_bytes=32 * 1024 * 1024),
    )(*came)


def shards_copied(qkv_all, context_kv, sections, groups, copies, heads, scale):
    steps, _, tok_rows, width = qkv_all.shape
    head_dim = width // (3 * HEADS)
    peers = groups * copies
    share = tok_rows // copies
    ctx_rows = context_kv.shape[0]
    frames = qkv_all[:, 0].reshape(steps, tok_rows, groups, heads, 3, head_dim)
    queries = frames[..., 0, :].reshape(steps, copies, share, groups, heads, head_dim)
    queries = queries.transpose(3, 1, 0, 4, 2, 5).reshape(peers, -1, head_dim)
    key_vals = frames[..., 1:, :].transpose(2, 0, 3, 4, 1, 5).reshape(groups, -1, head_dim)
    ctx = context_kv.reshape(ctx_rows, groups, heads, 2, head_dim)
    ctx = ctx.transpose(1, 2, 3, 0, 4).reshape(groups, -1, head_dim)
    shared = jnp.concatenate([key_vals, ctx], axis=1)
    shared = jnp.broadcast_to(shared[:, None], (groups, copies) + shared.shape[1:])
    shared = shared.reshape((peers,) + shared.shape[2:])
    sent = jnp.concatenate([queries, shared], axis=1)
    got = lax.all_to_all(sent, AXES, split_axis=0, concat_axis=0, tiled=True)
    per_section = peers // sections
    cut = steps * heads * share
    end = cut + steps * heads * 2 * tok_rows
    q = got[:, :cut].reshape(sections, per_section, steps, heads, share, head_dim)
    q = q.transpose(2, 0, 3, 1, 4, 5).reshape(steps, sections, heads, -1, head_dim)
    kv = got[:, cut:end].reshape(sections, per_section, steps, heads, 2, tok_rows, head_dim)
    kv = kv.transpose(2, 0, 4, 3, 1, 5, 6).reshape(steps, sections, 2, heads, -1, head_dim)
    ctx = got[:, end:].reshape(peers, heads, 2, ctx_rows, head_dim)
    earlier = [ctx.transpose(2, 1, 0, 3, 4).reshape(2, heads, -1, head_dim)]
    results = []
    for step in range(steps):
        for s in range(sections):
            keys, vals = jnp.concatenate(earlier + [kv[step, s]], axis=2)
            results.append(
                jnp.stack([softmax_mix(q[step, s, h], keys[h], vals[h], scale) for h in range(heads)])
            )
        earlier = earlier + [kv[step, sections - 1]]
    mixed = jnp.stack(results).reshape(steps, sections, heads, per_section, share, head_dim)
    mixed = mixed.transpose(1, 3, 0, 2, 4, 5).reshape(peers, -1, head_dim)
    back = lax.all_to_all(mixed, AXES, split_axis=0, concat_axis=0, tiled=True)
    back = back.reshape(groups, copies, steps, heads, share, head_dim)
    back = back.transpose(2, 1, 4, 0, 3, 5)
    return back.reshape(steps, 1, tok_rows, HEADS * head_dim)


def solution(mesh):
    in_specs = (P(None, "section", ("rep", "seq"), None), P(("rep", "section", "seq"), None))
    out_specs = P(None, "section", ("rep", "seq"), None)
    return jax.shard_map(shards, mesh=mesh, in_specs=in_specs, out_specs=out_specs, check_vma=False)
```

```python
import functools
import math

import jax
import jax.numpy as jnp
from jax import lax
from jax.experimental import pallas as pl
from jax.experimental.pallas import tpu as pltpu
from jax.sharding import PartitionSpec as P

HEADS = 32
AXES = ("section", "seq")


def softmax_mix(queries, keys, values, scale):
    scores = (
        lax.dot_general(
            queries, keys, (((1,), (1,)), ((), ())), preferred_element_type=jnp.float32
        )
        * scale
    )
    weights = jnp.exp(scores - jnp.max(scores, axis=1, keepdims=True))
    total = jnp.sum(weights, axis=1, keepdims=True)
    mixed = jnp.dot(weights.astype(jnp.bfloat16), values, preferred_element_type=jnp.float32)
    return (mixed / total).astype(jnp.bfloat16)


def attend_kernel(
    steps, sections, heads, tok_rows, ctx_rows, head_dim, scale, got_ref, out_ref
):
    sources = got_ref.shape[0]
    per_section = sources // sections
    tokens = per_section * tok_rows
    ctx_base = steps * heads * 3 * head_dim
    log2_scale = scale * math.log2(math.e)

    def part(step, section, head, role):
        base = ((step * heads + head) * 3 + role) * head_dim
        rows = slice(section * per_section, (section + 1) * per_section)
        return got_ref[rows, :, base : base + head_dim].reshape(tokens, head_dim)

    def context(head, role):
        base = ctx_base + role * head_dim
        rows = slice(head * ctx_rows, (head + 1) * ctx_rows)
        return got_ref[:, rows, base : base + head_dim].reshape(sources * ctx_rows, head_dim)

    tasks = []
    for head in range(heads):
        earlier = [(context(head, 0), context(head, 1))]
        for step in range(steps):
            own = [(part(step, s, head, 1), part(step, s, head, 2)) for s in range(sections)]
            for s in range(sections):
                pairs = earlier + [own[s]]
                keys = jnp.concatenate([k for k, _ in pairs], axis=0)
                vals = jnp.concatenate([v for _, v in pairs], axis=0)
                tasks.append((step, s, head, part(step, s, head, 0), keys, vals))
            earlier = earlier + [own[sections - 1]]
    all_scores = [
        lax.dot_general(q, k, (((1,), (1,)), ((), ())), preferred_element_type=jnp.float32)
        for _, _, _, q, k, _ in tasks
    ]
    all_tops = [jnp.max(scores, axis=1, keepdims=True) for scores in all_scores]
    all_weights = [
        jnp.exp2((scores - top) * log2_scale).astype(jnp.bfloat16)
        for scores, top in zip(all_scores, all_tops)
    ]
    all_mixed = [
        jnp.dot(
            weights,
            jnp.concatenate([vals, jnp.ones_like(vals)], axis=1),
            preferred_element_type=jnp.float32,
        )
        for weights, (_, _, _, _, _, vals) in zip(all_weights, tasks)
    ]
    for mixed, (step, s, head, _, _, _) in zip(all_mixed, tasks):
        done = (mixed[:, :head_dim] / mixed[:, head_dim:]).astype(jnp.bfloat16)
        base = (step * heads + head) * head_dim
        out_ref[s * per_section : (s + 1) * per_section, :, base : base + head_dim] = done.reshape(
            per_section, tok_rows, head_dim
        )


def pack_kernel(steps, groups, heads, ctx_rows, head_dim, qkv_ref, ctx_hbm, out_ref, ctx_ref, sems, ctx_sem):
    ctx_copy = pltpu.make_async_copy(ctx_hbm, ctx_ref, ctx_sem)
    ctx_copy.start()
    width = heads * 3 * head_dim
    copies = []
    for step in range(steps):
        for group in range(groups):
            copies.append(
                pltpu.make_async_copy(
                    qkv_ref.at[step, 0, :, pl.ds(group * width, width)],
                    out_ref.at[group, :, pl.ds(step * width, width)],
                    sems.at[step, group],
                )
            )
    for copy in copies:
        copy.start()
    base = steps * width
    ctx_copy.wait()
    for group in range(groups):
        for role in range(2):
            columns = [((group * heads + head) * 2 + role) * head_dim for head in range(heads)]
            block = [ctx_ref[:, c : c + head_dim] for c in columns]
            out_ref[group, :, base + role * head_dim : base + (role + 1) * head_dim] = (
                jnp.concatenate(block, axis=0)
            )
    for copy in copies:
        copy.wait()


def shards(qkv_all, context_kv):
    sections = lax.axis_size("section")
    peers = sections * lax.axis_size("seq")
    groups = min(peers, HEADS)
    copies = peers // groups
    heads = HEADS // groups
    steps, _, tok_rows, width = qkv_all.shape
    head_dim = width // (3 * HEADS)
    ctx_rows = context_kv.shape[0]
    scale = head_dim ** (-0.5)
    if copies > 1 or heads * ctx_rows != tok_rows:
        return shards_copied(qkv_all, context_kv, sections, groups, copies, heads, scale)

    in_vmem = pl.BlockSpec(memory_space=pltpu.VMEM)
    params = pltpu.CompilerParams(vmem_limit_bytes=32 * 1024 * 1024)
    sent = pl.pallas_call(
        functools.partial(pack_kernel, steps, groups, heads, ctx_rows, head_dim),
        out_shape=jax.ShapeDtypeStruct(
            (groups, tok_rows, (steps * heads * 3 + 2) * head_dim), jnp.bfloat16
        ),
        in_specs=[pl.BlockSpec(memory_space=pltpu.HBM)] * 2,
        out_specs=in_vmem,
        scratch_shapes=[
            pltpu.VMEM(context_kv.shape, jnp.bfloat16),
            pltpu.SemaphoreType.DMA((steps, groups)),
            pltpu.SemaphoreType.DMA,
        ],
        compiler_params=params,
    )(*(pltpu.with_memory_space_constraint(x, pltpu.HBM) for x in (qkv_all, context_kv)))
    got = lax.all_to_all(sent, AXES, split_axis=0, concat_axis=0, tiled=True)
    mixed = pl.pallas_call(
        functools.partial(
            attend_kernel, steps, sections, heads, tok_rows, ctx_rows, head_dim, scale
        ),
        out_shape=jax.ShapeDtypeStruct((peers, tok_rows, steps * heads * head_dim), jnp.bfloat16),
        in_specs=[in_vmem],
        out_specs=in_vmem,
        compiler_params=params,
    )(got)
    back = lax.all_to_all(mixed, AXES, split_axis=0, concat_axis=0, tiled=True)
    back = back.reshape(groups, tok_rows, steps, heads * head_dim).transpose(2, 1, 0, 3)
    return back.reshape(steps, 1, tok_rows, HEADS * head_dim)


def shards_copied(qkv_all, context_kv, sections, groups, copies, heads, scale):
    steps, _, tok_rows, width = qkv_all.shape
    head_dim = width // (3 * HEADS)
    peers = groups * copies
    share = tok_rows // copies
    ctx_rows = context_kv.shape[0]
    frames = qkv_all[:, 0].reshape(steps, tok_rows, groups, heads, 3, head_dim)
    queries = frames[..., 0, :].reshape(steps, copies, share, groups, heads, head_dim)
    queries = queries.transpose(3, 1, 0, 4, 2, 5).reshape(peers, -1, head_dim)
    key_vals = frames[..., 1:, :].transpose(2, 0, 3, 4, 1, 5).reshape(groups, -1, head_dim)
    ctx = context_kv.reshape(ctx_rows, groups, heads, 2, head_dim)
    ctx = ctx.transpose(1, 2, 3, 0, 4).reshape(groups, -1, head_dim)
    shared = jnp.concatenate([key_vals, ctx], axis=1)
    shared = jnp.broadcast_to(shared[:, None], (groups, copies) + shared.shape[1:])
    shared = shared.reshape((peers,) + shared.shape[2:])
    sent = jnp.concatenate([queries, shared], axis=1)
    got = lax.all_to_all(sent, AXES, split_axis=0, concat_axis=0, tiled=True)
    per_section = peers // sections
    cut = steps * heads * share
    end = cut + steps * heads * 2 * tok_rows
    q = got[:, :cut].reshape(sections, per_section, steps, heads, share, head_dim)
    q = q.transpose(2, 0, 3, 1, 4, 5).reshape(steps, sections, heads, -1, head_dim)
    kv = got[:, cut:end].reshape(sections, per_section, steps, heads, 2, tok_rows, head_dim)
    kv = kv.transpose(2, 0, 4, 3, 1, 5, 6).reshape(steps, sections, 2, heads, -1, head_dim)
    ctx = got[:, end:].reshape(peers, heads, 2, ctx_rows, head_dim)
    earlier = [ctx.transpose(2, 1, 0, 3, 4).reshape(2, heads, -1, head_dim)]
    results = []
    for step in range(steps):
        for s in range(sections):
            keys, vals = jnp.concatenate(earlier + [kv[step, s]], axis=2)
            results.append(
                jnp.stack([softmax_mix(q[step, s, h], keys[h], vals[h], scale) for h in range(heads)])
            )
        earlier = earlier + [kv[step, sections - 1]]
    mixed = jnp.stack(results).reshape(steps, sections, heads, per_section, share, head_dim)
    mixed = mixed.transpose(1, 3, 0, 2, 4, 5).reshape(peers, -1, head_dim)
    back = lax.all_to_all(mixed, AXES, split_axis=0, concat_axis=0, tiled=True)
    back = back.reshape(groups, copies, steps, heads, share, head_dim)
    back = back.transpose(2, 1, 4, 0, 3, 5)
    return back.reshape(steps, 1, tok_rows, HEADS * head_dim)


def solution(mesh):
    in_specs = (P(None, "section", ("rep", "seq"), None), P(("rep", "section", "seq"), None))
    out_specs = P(None, "section", ("rep", "seq"), None)
    return jax.shard_map(shards, mesh=mesh, in_specs=in_specs, out_specs=out_specs, check_vma=False)
```

```python
import functools
import math

import jax
import jax.numpy as jnp
from jax import lax
from jax.experimental import pallas as pl
from jax.experimental.pallas import tpu as pltpu
from jax.sharding import PartitionSpec as P

HEADS = 32
AXES = ("seq", "section")


def softmax_mix(queries, keys, values, scale):
    scores = (
        lax.dot_general(
            queries, keys, (((1,), (1,)), ((), ())), preferred_element_type=jnp.float32
        )
        * scale
    )
    weights = jnp.exp(scores - jnp.max(scores, axis=1, keepdims=True))
    total = jnp.sum(weights, axis=1, keepdims=True)
    mixed = jnp.dot(weights.astype(jnp.bfloat16), values, preferred_element_type=jnp.float32)
    return (mixed / total).astype(jnp.bfloat16)


def attend_kernel(
    steps, sections, heads, tok_rows, ctx_rows, head_dim, scale, got_ref, out_ref
):
    per_section = got_ref.shape[0]
    sources = per_section * sections
    tokens = per_section * tok_rows
    ctx_base = steps * heads * 3 * head_dim
    log2_scale = scale * math.log2(math.e)

    def part(step, section, head, role):
        base = ((step * heads + head) * 3 + role) * head_dim
        return got_ref[:, section, :, base : base + head_dim].reshape(tokens, head_dim)

    def context(head, role):
        base = ctx_base + role * head_dim
        rows = slice(head * ctx_rows, (head + 1) * ctx_rows)
        return got_ref[:, :, rows, base : base + head_dim].reshape(sources * ctx_rows, head_dim)

    tasks = []
    for head in range(heads):
        earlier = [(context(head, 0), context(head, 1))]
        for step in range(steps):
            own = [(part(step, s, head, 1), part(step, s, head, 2)) for s in range(sections)]
            for s in range(sections):
                pairs = earlier + [own[s]]
                keys = jnp.concatenate([k for k, _ in pairs], axis=0)
                vals = jnp.concatenate([v for _, v in pairs], axis=0)
                tasks.append((step, s, head, part(step, s, head, 0), keys, vals))
            earlier = earlier + [own[sections - 1]]
    all_scores = [
        lax.dot_general(q, k, (((1,), (1,)), ((), ())), preferred_element_type=jnp.float32)
        for _, _, _, q, k, _ in tasks
    ]
    all_tops = [jnp.max(scores, axis=1, keepdims=True) for scores in all_scores]
    all_weights = [
        jnp.exp2((scores - top) * log2_scale).astype(jnp.bfloat16)
        for scores, top in zip(all_scores, all_tops)
    ]
    all_mixed = [
        jnp.dot(
            weights,
            jnp.concatenate([vals, jnp.ones_like(vals)], axis=1),
            preferred_element_type=jnp.float32,
        )
        for weights, (_, _, _, _, _, vals) in zip(all_weights, tasks)
    ]
    for mixed, (step, s, head, _, _, _) in zip(all_mixed, tasks):
        done = (mixed[:, :head_dim] / mixed[:, head_dim:]).astype(jnp.bfloat16)
        base = (step * heads + head) * head_dim
        out_ref[:, s, :, base : base + head_dim] = done.reshape(
            per_section, tok_rows, head_dim
        )


def pack_kernel(
    steps, groups, heads, ctx_rows, head_dim, chunks, qkv_hbm, ctx_hbm, out_ref, qkv_ref, ctx_ref, sems, ctx_sem
):
    width = heads * 3 * head_dim
    span = groups // chunks
    ctx_copy = pltpu.make_async_copy(ctx_hbm, ctx_ref, ctx_sem)
    copies = []
    for step in range(steps):
        for chunk in range(chunks):
            columns = pl.ds(chunk * span * width, span * width)
            copies.append(
                pltpu.make_async_copy(
                    qkv_hbm.at[step, 0, :, columns],
                    qkv_ref.at[step, :, columns],
                    sems.at[step, chunk],
                )
            )
    ctx_copy.start()
    for copy in copies:
        copy.start()
    base = steps * width
    ctx_copy.wait()
    for group in range(groups):
        for role in range(2):
            columns = [((group * heads + head) * 2 + role) * head_dim for head in range(heads)]
            block = [ctx_ref[:, c : c + head_dim] for c in columns]
            out_ref[group, :, base + role * head_dim : base + (role + 1) * head_dim] = (
                jnp.concatenate(block, axis=0)
            )
    for step in range(steps):
        for chunk in range(chunks):
            copies[step * chunks + chunk].wait()
            for group in range(chunk * span, (chunk + 1) * span):
                out_ref[group, :, step * width : (step + 1) * width] = qkv_ref[
                    step, :, group * width : (group + 1) * width
                ]


def shards(qkv_all, context_kv):
    sections = lax.axis_size("section")
    peers = sections * lax.axis_size("seq")
    groups = min(peers, HEADS)
    copies = peers // groups
    heads = HEADS // groups
    steps, _, tok_rows, width = qkv_all.shape
    head_dim = width // (3 * HEADS)
    ctx_rows = context_kv.shape[0]
    scale = head_dim ** (-0.5)
    if copies > 1 or heads * ctx_rows != tok_rows:
        return shards_copied(qkv_all, context_kv, sections, groups, copies, heads, scale)

    chunks = math.gcd(groups, 2)
    in_vmem = pl.BlockSpec(memory_space=pltpu.VMEM)
    params = pltpu.CompilerParams(vmem_limit_bytes=32 * 1024 * 1024)
    sent = pl.pallas_call(
        functools.partial(pack_kernel, steps, groups, heads, ctx_rows, head_dim, chunks),
        out_shape=jax.ShapeDtypeStruct(
            (groups, tok_rows, (steps * heads * 3 + 2) * head_dim), jnp.bfloat16
        ),
        in_specs=[pl.BlockSpec(memory_space=pltpu.HBM)] * 2,
        out_specs=in_vmem,
        scratch_shapes=[
            pltpu.VMEM((steps, tok_rows, width), jnp.bfloat16),
            pltpu.VMEM(context_kv.shape, jnp.bfloat16),
            pltpu.SemaphoreType.DMA((steps, chunks)),
            pltpu.SemaphoreType.DMA,
        ],
        compiler_params=params,
    )(*(pltpu.with_memory_space_constraint(x, pltpu.HBM) for x in (qkv_all, context_kv)))
    got = lax.all_to_all(sent, AXES, split_axis=0, concat_axis=0, tiled=True)
    mixed = pl.pallas_call(
        functools.partial(
            attend_kernel, steps, sections, heads, tok_rows, ctx_rows, head_dim, scale
        ),
        out_shape=jax.ShapeDtypeStruct(
            (peers // sections, sections, tok_rows, steps * heads * head_dim), jnp.bfloat16
        ),
        in_specs=[in_vmem],
        out_specs=in_vmem,
        compiler_params=params,
    )(got.reshape((-1, sections) + got.shape[1:]))
    mixed = mixed.reshape((peers,) + mixed.shape[2:])
    back = lax.all_to_all(mixed, AXES, split_axis=0, concat_axis=0, tiled=True)
    back = back.reshape(groups, tok_rows, steps, heads * head_dim).transpose(2, 1, 0, 3)
    return back.reshape(steps, 1, tok_rows, HEADS * head_dim)


def shards_copied(qkv_all, context_kv, sections, groups, copies, heads, scale):
    steps, _, tok_rows, width = qkv_all.shape
    head_dim = width // (3 * HEADS)
    peers = groups * copies
    share = tok_rows // copies
    ctx_rows = context_kv.shape[0]
    frames = qkv_all[:, 0].reshape(steps, tok_rows, groups, heads, 3, head_dim)
    queries = frames[..., 0, :].reshape(steps, copies, share, groups, heads, head_dim)
    queries = queries.transpose(3, 1, 0, 4, 2, 5).reshape(peers, -1, head_dim)
    key_vals = frames[..., 1:, :].transpose(2, 0, 3, 4, 1, 5).reshape(groups, -1, head_dim)
    ctx = context_kv.reshape(ctx_rows, groups, heads, 2, head_dim)
    ctx = ctx.transpose(1, 2, 3, 0, 4).reshape(groups, -1, head_dim)
    shared = jnp.concatenate([key_vals, ctx], axis=1)
    shared = jnp.broadcast_to(shared[:, None], (groups, copies) + shared.shape[1:])
    shared = shared.reshape((peers,) + shared.shape[2:])
    sent = jnp.concatenate([queries, shared], axis=1)
    got = lax.all_to_all(sent, AXES, split_axis=0, concat_axis=0, tiled=True)
    per_section = peers // sections
    cut = steps * heads * share
    end = cut + steps * heads * 2 * tok_rows
    q = got[:, :cut].reshape(per_section, sections, steps, heads, share, head_dim)
    q = q.transpose(2, 1, 3, 0, 4, 5).reshape(steps, sections, heads, -1, head_dim)
    kv = got[:, cut:end].reshape(per_section, sections, steps, heads, 2, tok_rows, head_dim)
    kv = kv.transpose(2, 1, 4, 3, 0, 5, 6).reshape(steps, sections, 2, heads, -1, head_dim)
    ctx = got[:, end:].reshape(peers, heads, 2, ctx_rows, head_dim)
    earlier = [ctx.transpose(2, 1, 0, 3, 4).reshape(2, heads, -1, head_dim)]
    results = []
    for step in range(steps):
        for s in range(sections):
            keys, vals = jnp.concatenate(earlier + [kv[step, s]], axis=2)
            results.append(
                jnp.stack([softmax_mix(q[step, s, h], keys[h], vals[h], scale) for h in range(heads)])
            )
        earlier = earlier + [kv[step, sections - 1]]
    mixed = jnp.stack(results).reshape(steps, sections, heads, per_section, share, head_dim)
    mixed = mixed.transpose(3, 1, 0, 2, 4, 5).reshape(peers, -1, head_dim)
    back = lax.all_to_all(mixed, AXES, split_axis=0, concat_axis=0, tiled=True)
    back = back.reshape(groups, copies, steps, heads, share, head_dim)
    back = back.transpose(2, 1, 4, 0, 3, 5)
    return back.reshape(steps, 1, tok_rows, HEADS * head_dim)


def solution(mesh):
    in_specs = (P(None, "section", ("rep", "seq"), None), P(("rep", "section", "seq"), None))
    out_specs = P(None, "section", ("rep", "seq"), None)
    return jax.shard_map(shards, mesh=mesh, in_specs=in_specs, out_specs=out_specs, check_vma=False)
```

```python
import functools
import math

import jax
import jax.numpy as jnp
from jax import lax
from jax.experimental import pallas as pl
from jax.experimental.pallas import tpu as pltpu
from jax.sharding import PartitionSpec as P

HEADS = 32
AXES = ("seq", "section")


def softmax_mix(queries, keys, values, scale):
    scores = (
        lax.dot_general(
            queries, keys, (((1,), (1,)), ((), ())), preferred_element_type=jnp.float32
        )
        * scale
    )
    weights = jnp.exp(scores - jnp.max(scores, axis=1, keepdims=True))
    total = jnp.sum(weights, axis=1, keepdims=True)
    mixed = jnp.dot(weights.astype(jnp.bfloat16), values, preferred_element_type=jnp.float32)
    return (mixed / total).astype(jnp.bfloat16)


def attend_kernel(
    steps, sections, heads, tok_rows, ctx_rows, head_dim, scale, got_ref, out_ref
):
    per_section = got_ref.shape[0]
    sources = per_section * sections
    tokens = per_section * tok_rows
    ctx_base = steps * heads * 3 * head_dim
    log2_scale = scale * math.log2(math.e)

    def part(step, section, head, role):
        base = ((step * heads + head) * 3 + role) * head_dim
        return got_ref[:, sections - 1 - section, :, base : base + head_dim].reshape(tokens, head_dim)

    def context(head, role):
        base = ctx_base + role * head_dim
        rows = slice(head * ctx_rows, (head + 1) * ctx_rows)
        return got_ref[:, :, rows, base : base + head_dim].reshape(sources * ctx_rows, head_dim)

    tasks = []
    for head in range(heads):
        earlier = [(context(head, 0), context(head, 1))]
        for step in range(steps):
            own = [(part(step, s, head, 1), part(step, s, head, 2)) for s in range(sections)]
            for s in range(sections):
                pairs = earlier + [own[s]]
                keys = jnp.concatenate([k for k, _ in pairs], axis=0)
                vals = jnp.concatenate([v for _, v in pairs], axis=0)
                tasks.append((step, s, head, part(step, s, head, 0), keys, vals))
            earlier = earlier + [own[sections - 1]]
    all_scores = [
        lax.dot_general(q, k, (((1,), (1,)), ((), ())), preferred_element_type=jnp.float32)
        for _, _, _, q, k, _ in tasks
    ]
    all_tops = [jnp.max(scores, axis=1, keepdims=True) for scores in all_scores]
    all_weights = [
        jnp.exp2((scores - top) * log2_scale).astype(jnp.bfloat16)
        for scores, top in zip(all_scores, all_tops)
    ]
    all_mixed = [
        jnp.dot(
            weights,
            jnp.concatenate([vals, jnp.ones_like(vals)], axis=1),
            preferred_element_type=jnp.float32,
        )
        for weights, (_, _, _, _, _, vals) in zip(all_weights, tasks)
    ]
    for mixed, (step, s, head, _, _, _) in zip(all_mixed, tasks):
        done = (mixed[:, :head_dim] / mixed[:, head_dim:]).astype(jnp.bfloat16)
        base = (step * heads + head) * head_dim
        out_ref[:, sections - 1 - s, :, base : base + head_dim] = done.reshape(
            per_section, tok_rows, head_dim
        )


def pack_kernel(
    steps, groups, heads, ctx_rows, head_dim, chunks, qkv_hbm, ctx_hbm, out_ref, qkv_ref, ctx_ref, sems, ctx_sem
):
    width = heads * 3 * head_dim
    span = groups // chunks
    ctx_copy = pltpu.make_async_copy(ctx_hbm, ctx_ref, ctx_sem)
    copies = []
    for step in range(steps):
        for chunk in range(chunks):
            columns = pl.ds(chunk * span * width, span * width)
            copies.append(
                pltpu.make_async_copy(
                    qkv_hbm.at[step, 0, :, columns],
                    qkv_ref.at[step, :, columns],
                    sems.at[step, chunk],
                )
            )
    ctx_copy.start()
    for copy in copies:
        copy.start()
    base = steps * width
    ctx_copy.wait()
    for group in range(groups):
        for role in range(2):
            columns = [((group * heads + head) * 2 + role) * head_dim for head in range(heads)]
            block = [ctx_ref[:, c : c + head_dim] for c in columns]
            out_ref[group, :, base + role * head_dim : base + (role + 1) * head_dim] = (
                jnp.concatenate(block, axis=0)
            )
    for step in range(steps):
        for chunk in range(chunks):
            copies[step * chunks + chunk].wait()
            for group in range(chunk * span, (chunk + 1) * span):
                out_ref[group, :, step * width : (step + 1) * width] = qkv_ref[
                    step, :, group * width : (group + 1) * width
                ]


def shards(qkv_all, context_kv):
    sections = lax.axis_size("section")
    peers = sections * lax.axis_size("seq")
    groups = min(peers, HEADS)
    copies = peers // groups
    heads = HEADS // groups
    steps, _, tok_rows, width = qkv_all.shape
    head_dim = width // (3 * HEADS)
    ctx_rows = context_kv.shape[0]
    scale = head_dim ** (-0.5)
    if copies > 1 or heads * ctx_rows != tok_rows:
        return shards_copied(qkv_all, context_kv, sections, groups, copies, heads, scale)

    chunks = math.gcd(groups, 2)
    in_vmem = pl.BlockSpec(memory_space=pltpu.VMEM)
    params = pltpu.CompilerParams(vmem_limit_bytes=32 * 1024 * 1024)
    sent = pl.pallas_call(
        functools.partial(pack_kernel, steps, groups, heads, ctx_rows, head_dim, chunks),
        out_shape=jax.ShapeDtypeStruct(
            (groups, tok_rows, (steps * heads * 3 + 2) * head_dim), jnp.bfloat16
        ),
        in_specs=[pl.BlockSpec(memory_space=pltpu.HBM)] * 2,
        out_specs=in_vmem,
        scratch_shapes=[
            pltpu.VMEM((steps, tok_rows, width), jnp.bfloat16),
            pltpu.VMEM(context_kv.shape, jnp.bfloat16),
            pltpu.SemaphoreType.DMA((steps, chunks)),
            pltpu.SemaphoreType.DMA,
        ],
        compiler_params=params,
    )(*(pltpu.with_memory_space_constraint(x, pltpu.HBM) for x in (qkv_all, context_kv)))
    exchange = functools.partial(
        lax.all_to_all,
        axis_name=AXES,
        split_axis=0,
        concat_axis=0,
        axis_index_groups=[list(range(peers - 1, -1, -1))],
        tiled=True,
    )
    got = exchange(sent)
    mixed = pl.pallas_call(
        functools.partial(
            attend_kernel, steps, sections, heads, tok_rows, ctx_rows, head_dim, scale
        ),
        out_shape=jax.ShapeDtypeStruct(
            (peers // sections, sections, tok_rows, steps * heads * head_dim), jnp.bfloat16
        ),
        in_specs=[in_vmem],
        out_specs=in_vmem,
        compiler_params=params,
    )(got.reshape((-1, sections) + got.shape[1:]))
    mixed = mixed.reshape((peers,) + mixed.shape[2:])
    back = exchange(mixed)
    back = back.reshape(groups, tok_rows, steps, heads * head_dim).transpose(2, 1, 0, 3)
    return back.reshape(steps, 1, tok_rows, HEADS * head_dim)


def shards_copied(qkv_all, context_kv, sections, groups, copies, heads, scale):
    steps, _, tok_rows, width = qkv_all.shape
    head_dim = width // (3 * HEADS)
    peers = groups * copies
    share = tok_rows // copies
    ctx_rows = context_kv.shape[0]
    frames = qkv_all[:, 0].reshape(steps, tok_rows, groups, heads, 3, head_dim)
    queries = frames[..., 0, :].reshape(steps, copies, share, groups, heads, head_dim)
    queries = queries.transpose(3, 1, 0, 4, 2, 5).reshape(peers, -1, head_dim)
    key_vals = frames[..., 1:, :].transpose(2, 0, 3, 4, 1, 5).reshape(groups, -1, head_dim)
    ctx = context_kv.reshape(ctx_rows, groups, heads, 2, head_dim)
    ctx = ctx.transpose(1, 2, 3, 0, 4).reshape(groups, -1, head_dim)
    shared = jnp.concatenate([key_vals, ctx], axis=1)
    shared = jnp.broadcast_to(shared[:, None], (groups, copies) + shared.shape[1:])
    shared = shared.reshape((peers,) + shared.shape[2:])
    sent = jnp.concatenate([queries, shared], axis=1)
    got = lax.all_to_all(sent, AXES, split_axis=0, concat_axis=0, tiled=True)
    per_section = peers // sections
    cut = steps * heads * share
    end = cut + steps * heads * 2 * tok_rows
    q = got[:, :cut].reshape(per_section, sections, steps, heads, share, head_dim)
    q = q.transpose(2, 1, 3, 0, 4, 5).reshape(steps, sections, heads, -1, head_dim)
    kv = got[:, cut:end].reshape(per_section, sections, steps, heads, 2, tok_rows, head_dim)
    kv = kv.transpose(2, 1, 4, 3, 0, 5, 6).reshape(steps, sections, 2, heads, -1, head_dim)
    ctx = got[:, end:].reshape(peers, heads, 2, ctx_rows, head_dim)
    earlier = [ctx.transpose(2, 1, 0, 3, 4).reshape(2, heads, -1, head_dim)]
    results = []
    for step in range(steps):
        for s in range(sections):
            keys, vals = jnp.concatenate(earlier + [kv[step, s]], axis=2)
            results.append(
                jnp.stack([softmax_mix(q[step, s, h], keys[h], vals[h], scale) for h in range(heads)])
            )
        earlier = earlier + [kv[step, sections - 1]]
    mixed = jnp.stack(results).reshape(steps, sections, heads, per_section, share, head_dim)
    mixed = mixed.transpose(3, 1, 0, 2, 4, 5).reshape(peers, -1, head_dim)
    back = lax.all_to_all(mixed, AXES, split_axis=0, concat_axis=0, tiled=True)
    back = back.reshape(groups, copies, steps, heads, share, head_dim)
    back = back.transpose(2, 1, 4, 0, 3, 5)
    return back.reshape(steps, 1, tok_rows, HEADS * head_dim)


def solution(mesh):
    in_specs = (P(None, "section", ("rep", "seq"), None), P(("rep", "section", "seq"), None))
    out_specs = P(None, "section", ("rep", "seq"), None)
    return jax.shard_map(shards, mesh=mesh, in_specs=in_specs, out_specs=out_specs, check_vma=False)
```

```python
import functools
import math

import jax
import jax.numpy as jnp
from jax import lax
from jax.experimental import pallas as pl
from jax.experimental.pallas import tpu as pltpu
from jax.sharding import PartitionSpec as P

HEADS = 32
AXES = ("seq", "section")


def softmax_mix(queries, keys, values, scale):
    scores = (
        lax.dot_general(
            queries, keys, (((1,), (1,)), ((), ())), preferred_element_type=jnp.float32
        )
        * scale
    )
    weights = jnp.exp(scores - jnp.max(scores, axis=1, keepdims=True))
    total = jnp.sum(weights, axis=1, keepdims=True)
    mixed = jnp.dot(weights.astype(jnp.bfloat16), values, preferred_element_type=jnp.float32)
    return (mixed / total).astype(jnp.bfloat16)


def attend_kernel(
    steps, heads, tok_rows, ctx_rows, head_dim, scale, came_from, goes_to, got_ref, out_ref
):
    sections = len(came_from)
    sources = got_ref.shape[0]
    ctx_base = steps * heads * 3 * head_dim
    log2_scale = scale * math.log2(math.e)

    def part(step, section, head, role):
        base = ((step * heads + head) * 3 + role) * head_dim
        return jnp.concatenate(
            [got_ref[p, :, base : base + head_dim] for p in came_from[section]], axis=0
        )

    def context(head, role):
        base = ctx_base + role * head_dim
        rows = slice(head * ctx_rows, (head + 1) * ctx_rows)
        return got_ref[:, rows, base : base + head_dim].reshape(sources * ctx_rows, head_dim)

    tasks = []
    for head in range(heads):
        earlier = [(context(head, 0), context(head, 1))]
        for step in range(steps):
            own = [(part(step, s, head, 1), part(step, s, head, 2)) for s in range(sections)]
            for s in range(sections):
                pairs = earlier + [own[s]]
                keys = jnp.concatenate([k for k, _ in pairs], axis=0)
                vals = jnp.concatenate([v for _, v in pairs], axis=0)
                tasks.append((step, s, head, part(step, s, head, 0), keys, vals))
            earlier = earlier + [own[sections - 1]]
    all_scores = [
        lax.dot_general(q, k, (((1,), (1,)), ((), ())), preferred_element_type=jnp.float32)
        for _, _, _, q, k, _ in tasks
    ]
    all_tops = [jnp.max(scores, axis=1, keepdims=True) for scores in all_scores]
    all_weights = [
        jnp.exp2((scores - top) * log2_scale).astype(jnp.bfloat16)
        for scores, top in zip(all_scores, all_tops)
    ]
    all_mixed = [
        jnp.dot(
            weights,
            jnp.concatenate([vals, jnp.ones_like(vals)], axis=1),
            preferred_element_type=jnp.float32,
        )
        for weights, (_, _, _, _, _, vals) in zip(all_weights, tasks)
    ]
    for mixed, (step, s, head, _, _, _) in zip(all_mixed, tasks):
        done = (mixed[:, :head_dim] / mixed[:, head_dim:]).astype(jnp.bfloat16)
        base = (step * heads + head) * head_dim
        for slot, p in enumerate(goes_to[s]):
            out_ref[p, :, base : base + head_dim] = done[slot * tok_rows : (slot + 1) * tok_rows]


def pack_kernel(
    steps, block_of, heads, ctx_rows, head_dim, chunks, qkv_hbm, ctx_hbm, out_ref, qkv_ref, ctx_ref, sems, ctx_sem
):
    groups = len(block_of)
    width = heads * 3 * head_dim
    span = groups // chunks
    ctx_copy = pltpu.make_async_copy(ctx_hbm, ctx_ref, ctx_sem)
    copies = []
    for step in range(steps):
        for chunk in range(chunks):
            columns = pl.ds(chunk * span * width, span * width)
            copies.append(
                pltpu.make_async_copy(
                    qkv_hbm.at[step, 0, :, columns],
                    qkv_ref.at[step, :, columns],
                    sems.at[step, chunk],
                )
            )
    ctx_copy.start()
    for copy in copies:
        copy.start()
    base = steps * width
    ctx_copy.wait()
    for group in range(groups):
        for role in range(2):
            columns = [((group * heads + head) * 2 + role) * head_dim for head in range(heads)]
            block = [ctx_ref[:, c : c + head_dim] for c in columns]
            out_ref[block_of[group], :, base + role * head_dim : base + (role + 1) * head_dim] = (
                jnp.concatenate(block, axis=0)
            )
    for step in range(steps):
        for chunk in range(chunks):
            copies[step * chunks + chunk].wait()
            for group in range(chunk * span, (chunk + 1) * span):
                out_ref[block_of[group], :, step * width : (step + 1) * width] = qkv_ref[
                    step, :, group * width : (group + 1) * width
                ]


def exchange(blocks, order):
    return lax.all_to_all(
        blocks, AXES, split_axis=0, concat_axis=0, axis_index_groups=[order], tiled=True
    )


def send_orders(sections, per_section):
    peers = sections * per_section
    quarter = math.gcd(peers, 4)
    row = peers // quarter
    rows = ([3, 1, 0, 2] if quarter == 4 else list(range(quarter)))
    first = [z * row + i for z in rows for i in range(row - 1, -1, -1)]
    second = [
        seq * sections + s
        for s in range(sections - 1, -1, -1)
        for seq in range(per_section - 1, -1, -1)
    ]
    return first, second


def shards(qkv_all, context_kv):
    sections = lax.axis_size("section")
    peers = sections * lax.axis_size("seq")
    groups = min(peers, HEADS)
    copies = peers // groups
    heads = HEADS // groups
    steps, _, tok_rows, width = qkv_all.shape
    head_dim = width // (3 * HEADS)
    ctx_rows = context_kv.shape[0]
    scale = head_dim ** (-0.5)
    if copies > 1 or heads * ctx_rows != tok_rows:
        return shards_copied(qkv_all, context_kv, sections, groups, copies, heads, scale)

    chunks = math.gcd(groups, 2)
    per_section = peers // sections
    first, second = send_orders(sections, per_section)
    devices = range(sections * per_section)
    block_of = [first.index(second[group]) for group in range(groups)]
    came_from = [[first.index(d) for d in devices if d % sections == s] for s in range(sections)]
    goes_to = [[second.index(d) for d in devices if d % sections == s] for s in range(sections)]
    in_vmem = pl.BlockSpec(memory_space=pltpu.VMEM)
    params = pltpu.CompilerParams(vmem_limit_bytes=32 * 1024 * 1024)
    sent = pl.pallas_call(
        functools.partial(pack_kernel, steps, block_of, heads, ctx_rows, head_dim, chunks),
        out_shape=jax.ShapeDtypeStruct(
            (groups, tok_rows, (steps * heads * 3 + 2) * head_dim), jnp.bfloat16
        ),
        in_specs=[pl.BlockSpec(memory_space=pltpu.HBM)] * 2,
        out_specs=in_vmem,
        scratch_shapes=[
            pltpu.VMEM((steps, tok_rows, width), jnp.bfloat16),
            pltpu.VMEM(context_kv.shape, jnp.bfloat16),
            pltpu.SemaphoreType.DMA((steps, chunks)),
            pltpu.SemaphoreType.DMA,
        ],
        compiler_params=params,
    )(*(pltpu.with_memory_space_constraint(x, pltpu.HBM) for x in (qkv_all, context_kv)))
    got = exchange(sent, first)
    mixed = pl.pallas_call(
        functools.partial(
            attend_kernel, steps, heads, tok_rows, ctx_rows, head_dim, scale, came_from, goes_to
        ),
        out_shape=jax.ShapeDtypeStruct((peers, tok_rows, steps * heads * head_dim), jnp.bfloat16),
        in_specs=[in_vmem],
        out_specs=in_vmem,
        compiler_params=params,
    )(got)
    back = exchange(mixed, second)
    back = back.reshape(groups, tok_rows, steps, heads * head_dim).transpose(2, 1, 0, 3)
    return back.reshape(steps, 1, tok_rows, HEADS * head_dim)


def shards_copied(qkv_all, context_kv, sections, groups, copies, heads, scale):
    steps, _, tok_rows, width = qkv_all.shape
    head_dim = width // (3 * HEADS)
    peers = groups * copies
    share = tok_rows // copies
    ctx_rows = context_kv.shape[0]
    frames = qkv_all[:, 0].reshape(steps, tok_rows, groups, heads, 3, head_dim)
    queries = frames[..., 0, :].reshape(steps, copies, share, groups, heads, head_dim)
    queries = queries.transpose(3, 1, 0, 4, 2, 5).reshape(peers, -1, head_dim)
    key_vals = frames[..., 1:, :].transpose(2, 0, 3, 4, 1, 5).reshape(groups, -1, head_dim)
    ctx = context_kv.reshape(ctx_rows, groups, heads, 2, head_dim)
    ctx = ctx.transpose(1, 2, 3, 0, 4).reshape(groups, -1, head_dim)
    shared = jnp.concatenate([key_vals, ctx], axis=1)
    shared = jnp.broadcast_to(shared[:, None], (groups, copies) + shared.shape[1:])
    shared = shared.reshape((peers,) + shared.shape[2:])
    sent = jnp.concatenate([queries, shared], axis=1)
    got = lax.all_to_all(sent, AXES, split_axis=0, concat_axis=0, tiled=True)
    per_section = peers // sections
    cut = steps * heads * share
    end = cut + steps * heads * 2 * tok_rows
    q = got[:, :cut].reshape(per_section, sections, steps, heads, share, head_dim)
    q = q.transpose(2, 1, 3, 0, 4, 5).reshape(steps, sections, heads, -1, head_dim)
    kv = got[:, cut:end].reshape(per_section, sections, steps, heads, 2, tok_rows, head_dim)
    kv = kv.transpose(2, 1, 4, 3, 0, 5, 6).reshape(steps, sections, 2, heads, -1, head_dim)
    ctx = got[:, end:].reshape(peers, heads, 2, ctx_rows, head_dim)
    earlier = [ctx.transpose(2, 1, 0, 3, 4).reshape(2, heads, -1, head_dim)]
    results = []
    for step in range(steps):
        for s in range(sections):
            keys, vals = jnp.concatenate(earlier + [kv[step, s]], axis=2)
            results.append(
                jnp.stack([softmax_mix(q[step, s, h], keys[h], vals[h], scale) for h in range(heads)])
            )
        earlier = earlier + [kv[step, sections - 1]]
    mixed = jnp.stack(results).reshape(steps, sections, heads, per_section, share, head_dim)
    mixed = mixed.transpose(3, 1, 0, 2, 4, 5).reshape(peers, -1, head_dim)
    back = lax.all_to_all(mixed, AXES, split_axis=0, concat_axis=0, tiled=True)
    back = back.reshape(groups, copies, steps, heads, share, head_dim)
    back = back.transpose(2, 1, 4, 0, 3, 5)
    return back.reshape(steps, 1, tok_rows, HEADS * head_dim)


def solution(mesh):
    in_specs = (P(None, "section", ("rep", "seq"), None), P(("rep", "section", "seq"), None))
    out_specs = P(None, "section", ("rep", "seq"), None)
    return jax.shard_map(shards, mesh=mesh, in_specs=in_specs, out_specs=out_specs, check_vma=False)
```

```python
import functools
import math

import jax
import jax.numpy as jnp
from jax import lax
from jax.experimental import pallas as pl
from jax.experimental.pallas import tpu as pltpu
from jax.sharding import PartitionSpec as P

HEADS = 32
AXES = ("seq", "section")


def softmax_mix(queries, keys, values, scale):
    scores = (
        lax.dot_general(
            queries, keys, (((1,), (1,)), ((), ())), preferred_element_type=jnp.float32
        )
        * scale
    )
    weights = jnp.exp(scores - jnp.max(scores, axis=1, keepdims=True))
    total = jnp.sum(weights, axis=1, keepdims=True)
    mixed = jnp.dot(weights.astype(jnp.bfloat16), values, preferred_element_type=jnp.float32)
    return (mixed / total).astype(jnp.bfloat16)


def attend_kernel(
    steps, heads, tok_rows, ctx_rows, head_dim, scale, came_from, goes_to, got_ref, out_ref
):
    sections = len(came_from)
    sources = got_ref.shape[0]
    ctx_base = steps * heads * 3 * head_dim
    log2_scale = scale * math.log2(math.e)

    def part(step, section, head, role):
        base = ((step * heads + head) * 3 + role) * head_dim
        return jnp.concatenate(
            [got_ref[p, :, base : base + head_dim] for p in came_from[section]], axis=0
        )

    def context(head, role):
        base = ctx_base + role * head_dim
        rows = slice(head * ctx_rows, (head + 1) * ctx_rows)
        return got_ref[:, rows, base : base + head_dim].reshape(sources * ctx_rows, head_dim)

    tasks = []
    for head in range(heads):
        earlier = [(context(head, 0), context(head, 1))]
        for step in range(steps):
            own = [(part(step, s, head, 1), part(step, s, head, 2)) for s in range(sections)]
            for s in range(sections):
                pairs = earlier + [own[s]]
                keys = jnp.concatenate([k for k, _ in pairs], axis=0)
                vals = jnp.concatenate([v for _, v in pairs], axis=0)
                tasks.append((step, s, head, part(step, s, head, 0), keys, vals))
            earlier = earlier + [own[sections - 1]]
    all_scores = [
        lax.dot_general(q, k, (((1,), (1,)), ((), ())), preferred_element_type=jnp.float32)
        for _, _, _, q, k, _ in tasks
    ]
    all_tops = [jnp.max(scores, axis=1, keepdims=True) for scores in all_scores]
    all_weights = [
        jnp.exp2((scores - top) * log2_scale).astype(jnp.bfloat16)
        for scores, top in zip(all_scores, all_tops)
    ]
    all_mixed = [
        jnp.dot(
            weights,
            jnp.concatenate([vals, jnp.ones_like(vals)], axis=1),
            preferred_element_type=jnp.float32,
        )
        for weights, (_, _, _, _, _, vals) in zip(all_weights, tasks)
    ]
    for mixed, (step, s, head, _, _, _) in zip(all_mixed, tasks):
        done = (mixed[:, :head_dim] / mixed[:, head_dim:]).astype(jnp.bfloat16)
        base = (step * heads + head) * head_dim
        for slot, p in enumerate(goes_to[s]):
            out_ref[p, :, base : base + head_dim] = done[slot * tok_rows : (slot + 1) * tok_rows]


def pack_kernel(
    steps, block_of, heads, ctx_rows, head_dim, chunks, qkv_hbm, ctx_hbm, out_ref, qkv_ref, ctx_ref, sems, ctx_sem
):
    groups = len(block_of)
    width = heads * 3 * head_dim
    span = groups // chunks
    ctx_copy = pltpu.make_async_copy(ctx_hbm, ctx_ref, ctx_sem)
    copies = []
    for step in range(steps):
        for chunk in range(chunks):
            columns = pl.ds(chunk * span * width, span * width)
            copies.append(
                pltpu.make_async_copy(
                    qkv_hbm.at[step, 0, :, columns],
                    qkv_ref.at[step, :, columns],
                    sems.at[step, chunk],
                )
            )
    ctx_copy.start()
    for copy in copies:
        copy.start()
    base = steps * width
    ctx_copy.wait()
    for group in range(groups):
        for role in range(2):
            columns = [((group * heads + head) * 2 + role) * head_dim for head in range(heads)]
            block = [ctx_ref[:, c : c + head_dim] for c in columns]
            out_ref[block_of[group], :, base + role * head_dim : base + (role + 1) * head_dim] = (
                jnp.concatenate(block, axis=0)
            )
    for step in range(steps):
        for chunk in range(chunks):
            copies[step * chunks + chunk].wait()
            for group in range(chunk * span, (chunk + 1) * span):
                out_ref[block_of[group], :, step * width : (step + 1) * width] = qkv_ref[
                    step, :, group * width : (group + 1) * width
                ]


def exchange(blocks, order):
    return lax.all_to_all(
        blocks, AXES, split_axis=0, concat_axis=0, axis_index_groups=[order], tiled=True
    )


def send_orders(sections, per_section):
    peers = sections * per_section
    quarter = math.gcd(peers, 4)
    row = peers // quarter
    first = [z * row + i for i in range(row - 1, -1, -1) for z in range(quarter - 1, -1, -1)]
    second = first
    return first, second


def shards(qkv_all, context_kv):
    sections = lax.axis_size("section")
    peers = sections * lax.axis_size("seq")
    groups = min(peers, HEADS)
    copies = peers // groups
    heads = HEADS // groups
    steps, _, tok_rows, width = qkv_all.shape
    head_dim = width // (3 * HEADS)
    ctx_rows = context_kv.shape[0]
    scale = head_dim ** (-0.5)
    if copies > 1 or heads * ctx_rows != tok_rows:
        return shards_copied(qkv_all, context_kv, sections, groups, copies, heads, scale)

    chunks = math.gcd(groups, 2)
    per_section = peers // sections
    first, second = send_orders(sections, per_section)
    devices = range(sections * per_section)
    block_of = [first.index(second[group]) for group in range(groups)]
    came_from = [[first.index(d) for d in devices if d % sections == s] for s in range(sections)]
    goes_to = [[second.index(d) for d in devices if d % sections == s] for s in range(sections)]
    in_vmem = pl.BlockSpec(memory_space=pltpu.VMEM)
    params = pltpu.CompilerParams(vmem_limit_bytes=32 * 1024 * 1024)
    sent = pl.pallas_call(
        functools.partial(pack_kernel, steps, block_of, heads, ctx_rows, head_dim, chunks),
        out_shape=jax.ShapeDtypeStruct(
            (groups, tok_rows, (steps * heads * 3 + 2) * head_dim), jnp.bfloat16
        ),
        in_specs=[pl.BlockSpec(memory_space=pltpu.HBM)] * 2,
        out_specs=in_vmem,
        scratch_shapes=[
            pltpu.VMEM((steps, tok_rows, width), jnp.bfloat16),
            pltpu.VMEM(context_kv.shape, jnp.bfloat16),
            pltpu.SemaphoreType.DMA((steps, chunks)),
            pltpu.SemaphoreType.DMA,
        ],
        compiler_params=params,
    )(*(pltpu.with_memory_space_constraint(x, pltpu.HBM) for x in (qkv_all, context_kv)))
    got = exchange(sent, first)
    mixed = pl.pallas_call(
        functools.partial(
            attend_kernel, steps, heads, tok_rows, ctx_rows, head_dim, scale, came_from, goes_to
        ),
        out_shape=jax.ShapeDtypeStruct((peers, tok_rows, steps * heads * head_dim), jnp.bfloat16),
        in_specs=[in_vmem],
        out_specs=in_vmem,
        compiler_params=params,
    )(got)
    back = exchange(mixed, second)
    back = back.reshape(groups, tok_rows, steps, heads * head_dim).transpose(2, 1, 0, 3)
    return back.reshape(steps, 1, tok_rows, HEADS * head_dim)


def shards_copied(qkv_all, context_kv, sections, groups, copies, heads, scale):
    steps, _, tok_rows, width = qkv_all.shape
    head_dim = width // (3 * HEADS)
    peers = groups * copies
    share = tok_rows // copies
    ctx_rows = context_kv.shape[0]
    frames = qkv_all[:, 0].reshape(steps, tok_rows, groups, heads, 3, head_dim)
    queries = frames[..., 0, :].reshape(steps, copies, share, groups, heads, head_dim)
    queries = queries.transpose(3, 1, 0, 4, 2, 5).reshape(peers, -1, head_dim)
    key_vals = frames[..., 1:, :].transpose(2, 0, 3, 4, 1, 5).reshape(groups, -1, head_dim)
    ctx = context_kv.reshape(ctx_rows, groups, heads, 2, head_dim)
    ctx = ctx.transpose(1, 2, 3, 0, 4).reshape(groups, -1, head_dim)
    shared = jnp.concatenate([key_vals, ctx], axis=1)
    shared = jnp.broadcast_to(shared[:, None], (groups, copies) + shared.shape[1:])
    shared = shared.reshape((peers,) + shared.shape[2:])
    sent = jnp.concatenate([queries, shared], axis=1)
    got = lax.all_to_all(sent, AXES, split_axis=0, concat_axis=0, tiled=True)
    per_section = peers // sections
    cut = steps * heads * share
    end = cut + steps * heads * 2 * tok_rows
    q = got[:, :cut].reshape(per_section, sections, steps, heads, share, head_dim)
    q = q.transpose(2, 1, 3, 0, 4, 5).reshape(steps, sections, heads, -1, head_dim)
    kv = got[:, cut:end].reshape(per_section, sections, steps, heads, 2, tok_rows, head_dim)
    kv = kv.transpose(2, 1, 4, 3, 0, 5, 6).reshape(steps, sections, 2, heads, -1, head_dim)
    ctx = got[:, end:].reshape(peers, heads, 2, ctx_rows, head_dim)
    earlier = [ctx.transpose(2, 1, 0, 3, 4).reshape(2, heads, -1, head_dim)]
    results = []
    for step in range(steps):
        for s in range(sections):
            keys, vals = jnp.concatenate(earlier + [kv[step, s]], axis=2)
            results.append(
                jnp.stack([softmax_mix(q[step, s, h], keys[h], vals[h], scale) for h in range(heads)])
            )
        earlier = earlier + [kv[step, sections - 1]]
    mixed = jnp.stack(results).reshape(steps, sections, heads, per_section, share, head_dim)
    mixed = mixed.transpose(3, 1, 0, 2, 4, 5).reshape(peers, -1, head_dim)
    back = lax.all_to_all(mixed, AXES, split_axis=0, concat_axis=0, tiled=True)
    back = back.reshape(groups, copies, steps, heads, share, head_dim)
    back = back.transpose(2, 1, 4, 0, 3, 5)
    return back.reshape(steps, 1, tok_rows, HEADS * head_dim)


def solution(mesh):
    in_specs = (P(None, "section", ("rep", "seq"), None), P(("rep", "section", "seq"), None))
    out_specs = P(None, "section", ("rep", "seq"), None)
    return jax.shard_map(shards, mesh=mesh, in_specs=in_specs, out_specs=out_specs, check_vma=False)
```

```python
import functools
import math

import jax
import jax.numpy as jnp
from jax import lax
from jax.experimental import pallas as pl
from jax.experimental.pallas import tpu as pltpu
from jax.sharding import PartitionSpec as P

HEADS = 32
AXES = ("seq", "section")


def softmax_mix(queries, keys, values, scale):
    scores = (
        lax.dot_general(
            queries, keys, (((1,), (1,)), ((), ())), preferred_element_type=jnp.float32
        )
        * scale
    )
    weights = jnp.exp(scores - jnp.max(scores, axis=1, keepdims=True))
    total = jnp.sum(weights, axis=1, keepdims=True)
    mixed = jnp.dot(weights.astype(jnp.bfloat16), values, preferred_element_type=jnp.float32)
    return (mixed / total).astype(jnp.bfloat16)


def attend_kernel(
    steps, heads, tok_rows, ctx_rows, head_dim, scale, came_from, goes_to, got_ref, out_ref
):
    sections = len(came_from)
    sources = got_ref.shape[0]
    ctx_base = steps * heads * 3 * head_dim
    log2_scale = scale * math.log2(math.e)

    def part(step, section, head, role):
        base = ((step * heads + head) * 3 + role) * head_dim
        return jnp.concatenate(
            [got_ref[p, :, base : base + head_dim] for p in came_from[section]], axis=0
        )

    def context(head, role):
        base = ctx_base + role * head_dim
        rows = slice(head * ctx_rows, (head + 1) * ctx_rows)
        return got_ref[:, rows, base : base + head_dim].reshape(sources * ctx_rows, head_dim)

    tasks = []
    for head in range(heads):
        earlier = [(context(head, 0), context(head, 1))]
        for step in range(steps):
            own = [(part(step, s, head, 1), part(step, s, head, 2)) for s in range(sections)]
            for s in range(sections):
                pairs = earlier + [own[s]]
                keys = jnp.concatenate([k for k, _ in pairs], axis=0)
                vals = jnp.concatenate([v for _, v in pairs], axis=0)
                tasks.append((step, s, head, part(step, s, head, 0), keys, vals))
            earlier = earlier + [own[sections - 1]]
    all_scores = [
        lax.dot_general(q, k, (((1,), (1,)), ((), ())), preferred_element_type=jnp.float32)
        for _, _, _, q, k, _ in tasks
    ]
    all_tops = [jnp.max(scores, axis=1, keepdims=True) for scores in all_scores]
    all_weights = [
        jnp.exp2((scores - top) * log2_scale).astype(jnp.bfloat16)
        for scores, top in zip(all_scores, all_tops)
    ]
    all_mixed = [
        jnp.dot(
            weights,
            jnp.concatenate([vals, jnp.ones_like(vals)], axis=1),
            preferred_element_type=jnp.float32,
        )
        for weights, (_, _, _, _, _, vals) in zip(all_weights, tasks)
    ]
    for mixed, (step, s, head, _, _, _) in zip(all_mixed, tasks):
        done = (mixed[:, :head_dim] / mixed[:, head_dim:]).astype(jnp.bfloat16)
        base = (step * heads + head) * head_dim
        for slot, p in enumerate(goes_to[s]):
            out_ref[p, :, base : base + head_dim] = done[slot * tok_rows : (slot + 1) * tok_rows]


def pack_kernel(
    steps, block_of, heads, ctx_rows, head_dim, chunks, qkv_hbm, ctx_hbm, out_ref, qkv_ref, ctx_ref, sems, ctx_sem
):
    groups = len(block_of)
    width = heads * 3 * head_dim
    span = groups // chunks
    ctx_copy = pltpu.make_async_copy(ctx_hbm, ctx_ref, ctx_sem)
    copies = []
    for step in range(steps):
        for chunk in range(chunks):
            columns = pl.ds(chunk * span * width, span * width)
            copies.append(
                pltpu.make_async_copy(
                    qkv_hbm.at[step, 0, :, columns],
                    qkv_ref.at[step, :, columns],
                    sems.at[step, chunk],
                )
            )
    ctx_copy.start()
    for copy in copies:
        copy.start()
    base = steps * width
    ctx_copy.wait()
    for group in range(groups):
        for role in range(2):
            columns = [((group * heads + head) * 2 + role) * head_dim for head in range(heads)]
            block = [ctx_ref[:, c : c + head_dim] for c in columns]
            out_ref[block_of[group], :, base + role * head_dim : base + (role + 1) * head_dim] = (
                jnp.concatenate(block, axis=0)
            )
    for step in range(steps):
        for chunk in range(chunks):
            copies[step * chunks + chunk].wait()
            for group in range(chunk * span, (chunk + 1) * span):
                out_ref[block_of[group], :, step * width : (step + 1) * width] = qkv_ref[
                    step, :, group * width : (group + 1) * width
                ]


def exchange(blocks, order):
    return lax.all_to_all(
        blocks, AXES, split_axis=0, concat_axis=0, axis_index_groups=[order], tiled=True
    )


def send_orders(sections, per_section):
    peers = sections * per_section
    quarter = math.gcd(peers, 4)
    row = peers // quarter
    turned = [z * row + i for z in range(quarter - 1, -1, -1) for i in range(row - 1, -1, -1)]
    first = turned[row:] + turned[:row]
    second = turned[peers // 2 :] + turned[: peers // 2]
    return first, second


def shards(qkv_all, context_kv):
    sections = lax.axis_size("section")
    peers = sections * lax.axis_size("seq")
    groups = min(peers, HEADS)
    copies = peers // groups
    heads = HEADS // groups
    steps, _, tok_rows, width = qkv_all.shape
    head_dim = width // (3 * HEADS)
    ctx_rows = context_kv.shape[0]
    scale = head_dim ** (-0.5)
    if copies > 1 or heads * ctx_rows != tok_rows:
        return shards_copied(qkv_all, context_kv, sections, groups, copies, heads, scale)

    chunks = math.gcd(groups, 2)
    per_section = peers // sections
    first, second = send_orders(sections, per_section)
    devices = range(sections * per_section)
    block_of = [first.index(second[group]) for group in range(groups)]
    came_from = [[first.index(d) for d in devices if d % sections == s] for s in range(sections)]
    goes_to = [[second.index(d) for d in devices if d % sections == s] for s in range(sections)]
    in_vmem = pl.BlockSpec(memory_space=pltpu.VMEM)
    params = pltpu.CompilerParams(vmem_limit_bytes=32 * 1024 * 1024)
    sent = pl.pallas_call(
        functools.partial(pack_kernel, steps, block_of, heads, ctx_rows, head_dim, chunks),
        out_shape=jax.ShapeDtypeStruct(
            (groups, tok_rows, (steps * heads * 3 + 2) * head_dim), jnp.bfloat16
        ),
        in_specs=[pl.BlockSpec(memory_space=pltpu.HBM)] * 2,
        out_specs=in_vmem,
        scratch_shapes=[
            pltpu.VMEM((steps, tok_rows, width), jnp.bfloat16),
            pltpu.VMEM(context_kv.shape, jnp.bfloat16),
            pltpu.SemaphoreType.DMA((steps, chunks)),
            pltpu.SemaphoreType.DMA,
        ],
        compiler_params=params,
    )(*(pltpu.with_memory_space_constraint(x, pltpu.HBM) for x in (qkv_all, context_kv)))
    got = exchange(sent, first)
    mixed = pl.pallas_call(
        functools.partial(
            attend_kernel, steps, heads, tok_rows, ctx_rows, head_dim, scale, came_from, goes_to
        ),
        out_shape=jax.ShapeDtypeStruct((peers, tok_rows, steps * heads * head_dim), jnp.bfloat16),
        in_specs=[in_vmem],
        out_specs=in_vmem,
        compiler_params=params,
    )(got)
    back = exchange(mixed, second)
    back = back.reshape(groups, tok_rows, steps, heads * head_dim).transpose(2, 1, 0, 3)
    return back.reshape(steps, 1, tok_rows, HEADS * head_dim)


def shards_copied(qkv_all, context_kv, sections, groups, copies, heads, scale):
    steps, _, tok_rows, width = qkv_all.shape
    head_dim = width // (3 * HEADS)
    peers = groups * copies
    share = tok_rows // copies
    ctx_rows = context_kv.shape[0]
    frames = qkv_all[:, 0].reshape(steps, tok_rows, groups, heads, 3, head_dim)
    queries = frames[..., 0, :].reshape(steps, copies, share, groups, heads, head_dim)
    queries = queries.transpose(3, 1, 0, 4, 2, 5).reshape(peers, -1, head_dim)
    key_vals = frames[..., 1:, :].transpose(2, 0, 3, 4, 1, 5).reshape(groups, -1, head_dim)
    ctx = context_kv.reshape(ctx_rows, groups, heads, 2, head_dim)
    ctx = ctx.transpose(1, 2, 3, 0, 4).reshape(groups, -1, head_dim)
    shared = jnp.concatenate([key_vals, ctx], axis=1)
    shared = jnp.broadcast_to(shared[:, None], (groups, copies) + shared.shape[1:])
    shared = shared.reshape((peers,) + shared.shape[2:])
    sent = jnp.concatenate([queries, shared], axis=1)
    got = lax.all_to_all(sent, AXES, split_axis=0, concat_axis=0, tiled=True)
    per_section = peers // sections
    cut = steps * heads * share
    end = cut + steps * heads * 2 * tok_rows
    q = got[:, :cut].reshape(per_section, sections, steps, heads, share, head_dim)
    q = q.transpose(2, 1, 3, 0, 4, 5).reshape(steps, sections, heads, -1, head_dim)
    kv = got[:, cut:end].reshape(per_section, sections, steps, heads, 2, tok_rows, head_dim)
    kv = kv.transpose(2, 1, 4, 3, 0, 5, 6).reshape(steps, sections, 2, heads, -1, head_dim)
    ctx = got[:, end:].reshape(peers, heads, 2, ctx_rows, head_dim)
    earlier = [ctx.transpose(2, 1, 0, 3, 4).reshape(2, heads, -1, head_dim)]
    results = []
    for step in range(steps):
        for s in range(sections):
            keys, vals = jnp.concatenate(earlier + [kv[step, s]], axis=2)
            results.append(
                jnp.stack([softmax_mix(q[step, s, h], keys[h], vals[h], scale) for h in range(heads)])
            )
        earlier = earlier + [kv[step, sections - 1]]
    mixed = jnp.stack(results).reshape(steps, sections, heads, per_section, share, head_dim)
    mixed = mixed.transpose(3, 1, 0, 2, 4, 5).reshape(peers, -1, head_dim)
    back = lax.all_to_all(mixed, AXES, split_axis=0, concat_axis=0, tiled=True)
    back = back.reshape(groups, copies, steps, heads, share, head_dim)
    back = back.transpose(2, 1, 4, 0, 3, 5)
    return back.reshape(steps, 1, tok_rows, HEADS * head_dim)


def solution(mesh):
    in_specs = (P(None, "section", ("rep", "seq"), None), P(("rep", "section", "seq"), None))
    out_specs = P(None, "section", ("rep", "seq"), None)
    return jax.shard_map(shards, mesh=mesh, in_specs=in_specs, out_specs=out_specs, check_vma=False)
```

```python
import functools
import math

import jax
import jax.numpy as jnp
from jax import lax
from jax.experimental import pallas as pl
from jax.experimental.pallas import tpu as pltpu
from jax.sharding import PartitionSpec as P

HEADS = 32
AXES = ("seq", "section")


def softmax_mix(queries, keys, values, scale):
    scores = (
        lax.dot_general(
            queries, keys, (((1,), (1,)), ((), ())), preferred_element_type=jnp.float32
        )
        * scale
    )
    weights = jnp.exp(scores - jnp.max(scores, axis=1, keepdims=True))
    total = jnp.sum(weights, axis=1, keepdims=True)
    mixed = jnp.dot(weights.astype(jnp.bfloat16), values, preferred_element_type=jnp.float32)
    return (mixed / total).astype(jnp.bfloat16)


def attend_kernel(
    steps, heads, tok_rows, ctx_rows, head_dim, scale, came_from, goes_to, got_ref, out_ref
):
    sections = len(came_from)
    sources = got_ref.shape[0]
    ctx_base = steps * heads * 3 * head_dim
    log2_scale = scale * math.log2(math.e)

    def part(step, section, head, role):
        base = ((step * heads + head) * 3 + role) * head_dim
        return jnp.concatenate(
            [got_ref[p, :, base : base + head_dim] for p in came_from[section]], axis=0
        )

    def context(head, role):
        base = ctx_base + role * head_dim
        rows = slice(head * ctx_rows, (head + 1) * ctx_rows)
        return got_ref[:, rows, base : base + head_dim].reshape(sources * ctx_rows, head_dim)

    tasks = []
    for head in range(heads):
        earlier = [(context(head, 0), context(head, 1))]
        for step in range(steps):
            own = [(part(step, s, head, 1), part(step, s, head, 2)) for s in range(sections)]
            for s in range(sections):
                pairs = earlier + [own[s]]
                keys = jnp.concatenate([k for k, _ in pairs], axis=0)
                vals = jnp.concatenate([v for _, v in pairs], axis=0)
                tasks.append((step, s, head, part(step, s, head, 0), keys, vals))
            earlier = earlier + [own[sections - 1]]
    all_scores = [
        lax.dot_general(q, k, (((1,), (1,)), ((), ())), preferred_element_type=jnp.float32)
        for _, _, _, q, k, _ in tasks
    ]
    all_tops = [jnp.max(scores, axis=1, keepdims=True) for scores in all_scores]
    all_weights = [
        jnp.exp2((scores - top) * log2_scale).astype(jnp.bfloat16)
        for scores, top in zip(all_scores, all_tops)
    ]
    all_mixed = [
        jnp.dot(
            weights,
            jnp.concatenate([vals, jnp.ones_like(vals)], axis=1),
            preferred_element_type=jnp.float32,
        )
        for weights, (_, _, _, _, _, vals) in zip(all_weights, tasks)
    ]
    for mixed, (step, s, head, _, _, _) in zip(all_mixed, tasks):
        done = (mixed[:, :head_dim] / mixed[:, head_dim:]).astype(jnp.bfloat16)
        base = (step * heads + head) * head_dim
        for slot, p in enumerate(goes_to[s]):
            out_ref[p, :, base : base + head_dim] = done[slot * tok_rows : (slot + 1) * tok_rows]


def pack_kernel(
    steps, block_of, heads, ctx_rows, head_dim, chunks, qkv_hbm, ctx_hbm, out_ref, qkv_ref, ctx_ref, sems, ctx_sem
):
    groups = len(block_of)
    width = heads * 3 * head_dim
    span = groups // chunks
    ctx_copy = pltpu.make_async_copy(ctx_hbm, ctx_ref, ctx_sem)
    copies = []
    for step in range(steps):
        for chunk in range(chunks):
            columns = pl.ds(chunk * span * width, span * width)
            copies.append(
                pltpu.make_async_copy(
                    qkv_hbm.at[step, 0, :, columns],
                    qkv_ref.at[step, :, columns],
                    sems.at[step, chunk],
                )
            )
    ctx_copy.start()
    for copy in copies:
        copy.start()
    base = steps * width
    ctx_copy.wait()
    for group in range(groups):
        for role in range(2):
            columns = [((group * heads + head) * 2 + role) * head_dim for head in range(heads)]
            block = [ctx_ref[:, c : c + head_dim] for c in columns]
            out_ref[block_of[group], :, base + role * head_dim : base + (role + 1) * head_dim] = (
                jnp.concatenate(block, axis=0)
            )
    for step in range(steps):
        for chunk in range(chunks):
            copies[step * chunks + chunk].wait()
            for group in range(chunk * span, (chunk + 1) * span):
                out_ref[block_of[group], :, step * width : (step + 1) * width] = qkv_ref[
                    step, :, group * width : (group + 1) * width
                ]


def exchange(blocks, order):
    return lax.all_to_all(
        blocks, AXES, split_axis=0, concat_axis=0, axis_index_groups=[order], tiled=True
    )


def send_orders(sections, per_section):
    peers = sections * per_section
    quarter = math.gcd(peers, 4)
    row = peers // quarter
    turned = [z * row + i for z in range(quarter - 1, -1, -1) for i in range(row - 1, -1, -1)]
    first = turned[row + 1 :] + turned[: row + 1]
    second = turned[row:] + turned[:row]
    return first, second


def shards(qkv_all, context_kv):
    sections = lax.axis_size("section")
    peers = sections * lax.axis_size("seq")
    groups = min(peers, HEADS)
    copies = peers // groups
    heads = HEADS // groups
    steps, _, tok_rows, width = qkv_all.shape
    head_dim = width // (3 * HEADS)
    ctx_rows = context_kv.shape[0]
    scale = head_dim ** (-0.5)
    if copies > 1 or heads * ctx_rows != tok_rows:
        return shards_copied(qkv_all, context_kv, sections, groups, copies, heads, scale)

    chunks = math.gcd(groups, 2)
    per_section = peers // sections
    first, second = send_orders(sections, per_section)
    devices = range(sections * per_section)
    block_of = [first.index(second[group]) for group in range(groups)]
    came_from = [[first.index(d) for d in devices if d % sections == s] for s in range(sections)]
    goes_to = [[second.index(d) for d in devices if d % sections == s] for s in range(sections)]
    in_vmem = pl.BlockSpec(memory_space=pltpu.VMEM)
    params = pltpu.CompilerParams(vmem_limit_bytes=32 * 1024 * 1024)
    sent = pl.pallas_call(
        functools.partial(pack_kernel, steps, block_of, heads, ctx_rows, head_dim, chunks),
        out_shape=jax.ShapeDtypeStruct(
            (groups, tok_rows, (steps * heads * 3 + 2) * head_dim), jnp.bfloat16
        ),
        in_specs=[pl.BlockSpec(memory_space=pltpu.HBM)] * 2,
        out_specs=in_vmem,
        scratch_shapes=[
            pltpu.VMEM((steps, tok_rows, width), jnp.bfloat16),
            pltpu.VMEM(context_kv.shape, jnp.bfloat16),
            pltpu.SemaphoreType.DMA((steps, chunks)),
            pltpu.SemaphoreType.DMA,
        ],
        compiler_params=params,
    )(*(pltpu.with_memory_space_constraint(x, pltpu.HBM) for x in (qkv_all, context_kv)))
    got = exchange(sent, first)
    mixed = pl.pallas_call(
        functools.partial(
            attend_kernel, steps, heads, tok_rows, ctx_rows, head_dim, scale, came_from, goes_to
        ),
        out_shape=jax.ShapeDtypeStruct((peers, tok_rows, steps * heads * head_dim), jnp.bfloat16),
        in_specs=[in_vmem],
        out_specs=in_vmem,
        compiler_params=params,
    )(got)
    back = exchange(mixed, second)
    back = back.reshape(groups, tok_rows, steps, heads * head_dim).transpose(2, 1, 0, 3)
    return back.reshape(steps, 1, tok_rows, HEADS * head_dim)


def shards_copied(qkv_all, context_kv, sections, groups, copies, heads, scale):
    steps, _, tok_rows, width = qkv_all.shape
    head_dim = width // (3 * HEADS)
    peers = groups * copies
    share = tok_rows // copies
    ctx_rows = context_kv.shape[0]
    frames = qkv_all[:, 0].reshape(steps, tok_rows, groups, heads, 3, head_dim)
    queries = frames[..., 0, :].reshape(steps, copies, share, groups, heads, head_dim)
    queries = queries.transpose(3, 1, 0, 4, 2, 5).reshape(peers, -1, head_dim)
    key_vals = frames[..., 1:, :].transpose(2, 0, 3, 4, 1, 5).reshape(groups, -1, head_dim)
    ctx = context_kv.reshape(ctx_rows, groups, heads, 2, head_dim)
    ctx = ctx.transpose(1, 2, 3, 0, 4).reshape(groups, -1, head_dim)
    shared = jnp.concatenate([key_vals, ctx], axis=1)
    shared = jnp.broadcast_to(shared[:, None], (groups, copies) + shared.shape[1:])
    shared = shared.reshape((peers,) + shared.shape[2:])
    sent = jnp.concatenate([queries, shared], axis=1)
    got = lax.all_to_all(sent, AXES, split_axis=0, concat_axis=0, tiled=True)
    per_section = peers // sections
    cut = steps * heads * share
    end = cut + steps * heads * 2 * tok_rows
    q = got[:, :cut].reshape(per_section, sections, steps, heads, share, head_dim)
    q = q.transpose(2, 1, 3, 0, 4, 5).reshape(steps, sections, heads, -1, head_dim)
    kv = got[:, cut:end].reshape(per_section, sections, steps, heads, 2, tok_rows, head_dim)
    kv = kv.transpose(2, 1, 4, 3, 0, 5, 6).reshape(steps, sections, 2, heads, -1, head_dim)
    ctx = got[:, end:].reshape(peers, heads, 2, ctx_rows, head_dim)
    earlier = [ctx.transpose(2, 1, 0, 3, 4).reshape(2, heads, -1, head_dim)]
    results = []
    for step in range(steps):
        for s in range(sections):
            keys, vals = jnp.concatenate(earlier + [kv[step, s]], axis=2)
            results.append(
                jnp.stack([softmax_mix(q[step, s, h], keys[h], vals[h], scale) for h in range(heads)])
            )
        earlier = earlier + [kv[step, sections - 1]]
    mixed = jnp.stack(results).reshape(steps, sections, heads, per_section, share, head_dim)
    mixed = mixed.transpose(3, 1, 0, 2, 4, 5).reshape(peers, -1, head_dim)
    back = lax.all_to_all(mixed, AXES, split_axis=0, concat_axis=0, tiled=True)
    back = back.reshape(groups, copies, steps, heads, share, head_dim)
    back = back.transpose(2, 1, 4, 0, 3, 5)
    return back.reshape(steps, 1, tok_rows, HEADS * head_dim)


def solution(mesh):
    in_specs = (P(None, "section", ("rep", "seq"), None), P(("rep", "section", "seq"), None))
    out_specs = P(None, "section", ("rep", "seq"), None)
    return jax.shard_map(shards, mesh=mesh, in_specs=in_specs, out_specs=out_specs, check_vma=False)
```

```python
import functools
import math

import jax
import jax.numpy as jnp
from jax import lax
from jax.experimental import pallas as pl
from jax.experimental.pallas import tpu as pltpu
from jax.sharding import PartitionSpec as P

HEADS = 32
AXES = ("seq", "section")


def softmax_mix(queries, keys, values, scale):
    scores = (
        lax.dot_general(
            queries, keys, (((1,), (1,)), ((), ())), preferred_element_type=jnp.float32
        )
        * scale
    )
    weights = jnp.exp(scores - jnp.max(scores, axis=1, keepdims=True))
    total = jnp.sum(weights, axis=1, keepdims=True)
    mixed = jnp.dot(weights.astype(jnp.bfloat16), values, preferred_element_type=jnp.float32)
    return (mixed / total).astype(jnp.bfloat16)


def attend_kernel(
    steps, heads, tok_rows, ctx_rows, head_dim, scale, came_from, goes_to, got_ref, out_ref
):
    sections = len(came_from)
    sources = got_ref.shape[0]
    ctx_base = steps * heads * 3 * head_dim
    log2_scale = scale * math.log2(math.e)

    def part(step, section, head, role):
        base = ((step * heads + head) * 3 + role) * head_dim
        return jnp.concatenate(
            [got_ref[p, :, base : base + head_dim] for p in came_from[section]], axis=0
        )

    def context(head, role):
        base = ctx_base + role * head_dim
        rows = slice(head * ctx_rows, (head + 1) * ctx_rows)
        return got_ref[:, rows, base : base + head_dim].reshape(sources * ctx_rows, head_dim)

    tasks = []
    for head in range(heads):
        earlier = [(context(head, 0), context(head, 1))]
        for step in range(steps):
            own = [(part(step, s, head, 1), part(step, s, head, 2)) for s in range(sections)]
            for s in range(sections):
                pairs = earlier + [own[s]]
                keys = jnp.concatenate([k for k, _ in pairs], axis=0)
                vals = jnp.concatenate([v for _, v in pairs], axis=0)
                tasks.append((step, s, head, part(step, s, head, 0), keys, vals))
            earlier = earlier + [own[sections - 1]]
    all_scores = [
        lax.dot_general(q, k, (((1,), (1,)), ((), ())), preferred_element_type=jnp.float32)
        for _, _, _, q, k, _ in tasks
    ]
    all_tops = [jnp.max(scores, axis=1, keepdims=True) for scores in all_scores]
    all_weights = [
        jnp.exp2((scores - top) * log2_scale).astype(jnp.bfloat16)
        for scores, top in zip(all_scores, all_tops)
    ]
    all_mixed = [
        jnp.dot(
            weights,
            jnp.concatenate([vals, jnp.ones_like(vals)], axis=1),
            preferred_element_type=jnp.float32,
        )
        for weights, (_, _, _, _, _, vals) in zip(all_weights, tasks)
    ]
    for mixed, (step, s, head, _, _, _) in zip(all_mixed, tasks):
        done = (mixed[:, :head_dim] / mixed[:, head_dim:]).astype(jnp.bfloat16)
        base = (step * heads + head) * head_dim
        for slot, p in enumerate(goes_to[s]):
            out_ref[p, :, base : base + head_dim] = done[slot * tok_rows : (slot + 1) * tok_rows]


def pack_kernel(
    steps, block_of, heads, ctx_rows, head_dim, chunks, qkv_hbm, ctx_hbm, out_ref, qkv_ref, ctx_ref, sems, ctx_sem
):
    groups = len(block_of)
    width = heads * 3 * head_dim
    span = groups // chunks
    ctx_copy = pltpu.make_async_copy(ctx_hbm, ctx_ref, ctx_sem)
    copies = []
    for step in range(steps):
        for chunk in range(chunks):
            columns = pl.ds(chunk * span * width, span * width)
            copies.append(
                pltpu.make_async_copy(
                    qkv_hbm.at[step, 0, :, columns],
                    qkv_ref.at[step, :, columns],
                    sems.at[step, chunk],
                )
            )
    ctx_copy.start()
    for copy in copies:
        copy.start()
    base = steps * width
    ctx_copy.wait()
    for group in range(groups):
        for role in range(2):
            columns = [((group * heads + head) * 2 + role) * head_dim for head in range(heads)]
            block = [ctx_ref[:, c : c + head_dim] for c in columns]
            out_ref[block_of[group], :, base + role * head_dim : base + (role + 1) * head_dim] = (
                jnp.concatenate(block, axis=0)
            )
    for step in range(steps):
        for chunk in range(chunks):
            copies[step * chunks + chunk].wait()
            for group in range(chunk * span, (chunk + 1) * span):
                out_ref[block_of[group], :, step * width : (step + 1) * width] = qkv_ref[
                    step, :, group * width : (group + 1) * width
                ]


def exchange(blocks, order):
    return lax.all_to_all(
        blocks, AXES, split_axis=0, concat_axis=0, axis_index_groups=[order], tiled=True
    )


def send_orders(sections, per_section):
    peers = sections * per_section
    quarter = math.gcd(peers, 4)
    row = peers // quarter
    turned = [z * row + i for z in range(quarter - 1, -1, -1) for i in range(row - 1, -1, -1)]
    half = peers // 2
    first = turned[half:] + turned[:half]
    half += row // 2
    second = turned[half:] + turned[:half]
    return first, second


def shards(qkv_all, context_kv):
    sections = lax.axis_size("section")
    peers = sections * lax.axis_size("seq")
    groups = min(peers, HEADS)
    copies = peers // groups
    heads = HEADS // groups
    steps, _, tok_rows, width = qkv_all.shape
    head_dim = width // (3 * HEADS)
    ctx_rows = context_kv.shape[0]
    scale = head_dim ** (-0.5)
    if copies > 1 or heads * ctx_rows != tok_rows:
        return shards_copied(qkv_all, context_kv, sections, groups, copies, heads, scale)

    chunks = math.gcd(groups, 2)
    per_section = peers // sections
    first, second = send_orders(sections, per_section)
    devices = range(sections * per_section)
    block_of = [first.index(second[group]) for group in range(groups)]
    came_from = [[first.index(d) for d in devices if d % sections == s] for s in range(sections)]
    goes_to = [[second.index(d) for d in devices if d % sections == s] for s in range(sections)]
    in_vmem = pl.BlockSpec(memory_space=pltpu.VMEM)
    params = pltpu.CompilerParams(vmem_limit_bytes=32 * 1024 * 1024)
    sent = pl.pallas_call(
        functools.partial(pack_kernel, steps, block_of, heads, ctx_rows, head_dim, chunks),
        out_shape=jax.ShapeDtypeStruct(
            (groups, tok_rows, (steps * heads * 3 + 2) * head_dim), jnp.bfloat16
        ),
        in_specs=[pl.BlockSpec(memory_space=pltpu.HBM)] * 2,
        out_specs=in_vmem,
        scratch_shapes=[
            pltpu.VMEM((steps, tok_rows, width), jnp.bfloat16),
            pltpu.VMEM(context_kv.shape, jnp.bfloat16),
            pltpu.SemaphoreType.DMA((steps, chunks)),
            pltpu.SemaphoreType.DMA,
        ],
        compiler_params=params,
    )(*(pltpu.with_memory_space_constraint(x, pltpu.HBM) for x in (qkv_all, context_kv)))
    got = exchange(sent, first)
    mixed = pl.pallas_call(
        functools.partial(
            attend_kernel, steps, heads, tok_rows, ctx_rows, head_dim, scale, came_from, goes_to
        ),
        out_shape=jax.ShapeDtypeStruct((peers, tok_rows, steps * heads * head_dim), jnp.bfloat16),
        in_specs=[in_vmem],
        out_specs=in_vmem,
        compiler_params=params,
    )(got)
    back = exchange(mixed, second)
    back = back.reshape(groups, tok_rows, steps, heads * head_dim).transpose(2, 1, 0, 3)
    return back.reshape(steps, 1, tok_rows, HEADS * head_dim)


def shards_copied(qkv_all, context_kv, sections, groups, copies, heads, scale):
    steps, _, tok_rows, width = qkv_all.shape
    head_dim = width // (3 * HEADS)
    peers = groups * copies
    share = tok_rows // copies
    ctx_rows = context_kv.shape[0]
    frames = qkv_all[:, 0].reshape(steps, tok_rows, groups, heads, 3, head_dim)
    queries = frames[..., 0, :].reshape(steps, copies, share, groups, heads, head_dim)
    queries = queries.transpose(3, 1, 0, 4, 2, 5).reshape(peers, -1, head_dim)
    key_vals = frames[..., 1:, :].transpose(2, 0, 3, 4, 1, 5).reshape(groups, -1, head_dim)
    ctx = context_kv.reshape(ctx_rows, groups, heads, 2, head_dim)
    ctx = ctx.transpose(1, 2, 3, 0, 4).reshape(groups, -1, head_dim)
    shared = jnp.concatenate([key_vals, ctx], axis=1)
    shared = jnp.broadcast_to(shared[:, None], (groups, copies) + shared.shape[1:])
    shared = shared.reshape((peers,) + shared.shape[2:])
    sent = jnp.concatenate([queries, shared], axis=1)
    got = lax.all_to_all(sent, AXES, split_axis=0, concat_axis=0, tiled=True)
    per_section = peers // sections
    cut = steps * heads * share
    end = cut + steps * heads * 2 * tok_rows
    q = got[:, :cut].reshape(per_section, sections, steps, heads, share, head_dim)
    q = q.transpose(2, 1, 3, 0, 4, 5).reshape(steps, sections, heads, -1, head_dim)
    kv = got[:, cut:end].reshape(per_section, sections, steps, heads, 2, tok_rows, head_dim)
    kv = kv.transpose(2, 1, 4, 3, 0, 5, 6).reshape(steps, sections, 2, heads, -1, head_dim)
    ctx = got[:, end:].reshape(peers, heads, 2, ctx_rows, head_dim)
    earlier = [ctx.transpose(2, 1, 0, 3, 4).reshape(2, heads, -1, head_dim)]
    results = []
    for step in range(steps):
        for s in range(sections):
            keys, vals = jnp.concatenate(earlier + [kv[step, s]], axis=2)
            results.append(
                jnp.stack([softmax_mix(q[step, s, h], keys[h], vals[h], scale) for h in range(heads)])
            )
        earlier = earlier + [kv[step, sections - 1]]
    mixed = jnp.stack(results).reshape(steps, sections, heads, per_section, share, head_dim)
    mixed = mixed.transpose(3, 1, 0, 2, 4, 5).reshape(peers, -1, head_dim)
    back = lax.all_to_all(mixed, AXES, split_axis=0, concat_axis=0, tiled=True)
    back = back.reshape(groups, copies, steps, heads, share, head_dim)
    back = back.transpose(2, 1, 4, 0, 3, 5)
    return back.reshape(steps, 1, tok_rows, HEADS * head_dim)


def solution(mesh):
    in_specs = (P(None, "section", ("rep", "seq"), None), P(("rep", "section", "seq"), None))
    out_specs = P(None, "section", ("rep", "seq"), None)
    return jax.shard_map(shards, mesh=mesh, in_specs=in_specs, out_specs=out_specs, check_vma=False)
```

```python
import functools
import math

import jax
import jax.numpy as jnp
from jax import lax
from jax.experimental import pallas as pl
from jax.experimental.pallas import tpu as pltpu
from jax.sharding import PartitionSpec as P

HEADS = 32
AXES = ("seq", "section")


def softmax_mix(queries, keys, values, scale):
    scores = (
        lax.dot_general(
            queries, keys, (((1,), (1,)), ((), ())), preferred_element_type=jnp.float32
        )
        * scale
    )
    weights = jnp.exp(scores - jnp.max(scores, axis=1, keepdims=True))
    total = jnp.sum(weights, axis=1, keepdims=True)
    mixed = jnp.dot(weights.astype(jnp.bfloat16), values, preferred_element_type=jnp.float32)
    return (mixed / total).astype(jnp.bfloat16)


def attend_kernel(
    steps, heads, tok_rows, ctx_rows, head_dim, scale, came_from, goes_to, got_ref, out_ref
):
    sections = len(came_from)
    sources = got_ref.shape[0]
    ctx_base = steps * heads * 3 * head_dim
    log2_scale = scale * math.log2(math.e)

    def part(step, section, head, role):
        base = ((step * heads + head) * 3 + role) * head_dim
        return jnp.concatenate(
            [got_ref[p, :, base : base + head_dim] for p in came_from[section]], axis=0
        )

    def context(head, role):
        base = ctx_base + role * head_dim
        rows = slice(head * ctx_rows, (head + 1) * ctx_rows)
        return got_ref[:, rows, base : base + head_dim].reshape(sources * ctx_rows, head_dim)

    tasks = []
    for head in range(heads):
        earlier = [(context(head, 0), context(head, 1))]
        for step in range(steps):
            own = [(part(step, s, head, 1), part(step, s, head, 2)) for s in range(sections)]
            for s in range(sections):
                pairs = earlier + [own[s]]
                keys = jnp.concatenate([k for k, _ in pairs], axis=0)
                vals = jnp.concatenate([v for _, v in pairs], axis=0)
                tasks.append((step, s, head, part(step, s, head, 0), keys, vals))
            earlier = earlier + [own[sections - 1]]
    all_scores = [
        lax.dot_general(q, k, (((1,), (1,)), ((), ())), preferred_element_type=jnp.float32)
        for _, _, _, q, k, _ in tasks
    ]
    all_tops = [jnp.max(scores, axis=1, keepdims=True) for scores in all_scores]
    all_weights = [
        jnp.exp2((scores - top) * log2_scale).astype(jnp.bfloat16)
        for scores, top in zip(all_scores, all_tops)
    ]
    all_mixed = [
        jnp.dot(
            weights,
            jnp.concatenate([vals, jnp.ones_like(vals)], axis=1),
            preferred_element_type=jnp.float32,
        )
        for weights, (_, _, _, _, _, vals) in zip(all_weights, tasks)
    ]
    for mixed, (step, s, head, _, _, _) in zip(all_mixed, tasks):
        done = (mixed[:, :head_dim] / mixed[:, head_dim:]).astype(jnp.bfloat16)
        base = (step * heads + head) * head_dim
        for slot, p in enumerate(goes_to[s]):
            out_ref[p, :, base : base + head_dim] = done[slot * tok_rows : (slot + 1) * tok_rows]


def pack_kernel(
    steps, block_of, heads, ctx_rows, head_dim, chunks, qkv_hbm, ctx_hbm, out_ref, qkv_ref, ctx_ref, sems, ctx_sem
):
    groups = len(block_of)
    width = heads * 3 * head_dim
    span = groups // chunks
    ctx_copy = pltpu.make_async_copy(ctx_hbm, ctx_ref, ctx_sem)
    copies = []
    for step in range(steps):
        for chunk in range(chunks):
            columns = pl.ds(chunk * span * width, span * width)
            copies.append(
                pltpu.make_async_copy(
                    qkv_hbm.at[step, 0, :, columns],
                    qkv_ref.at[step, :, columns],
                    sems.at[step, chunk],
                )
            )
    ctx_copy.start()
    for copy in copies:
        copy.start()
    base = steps * width
    ctx_copy.wait()
    for group in range(groups):
        for role in range(2):
            columns = [((group * heads + head) * 2 + role) * head_dim for head in range(heads)]
            block = [ctx_ref[:, c : c + head_dim] for c in columns]
            out_ref[block_of[group], :, base + role * head_dim : base + (role + 1) * head_dim] = (
                jnp.concatenate(block, axis=0)
            )
    for step in range(steps):
        for chunk in range(chunks):
            copies[step * chunks + chunk].wait()
            for group in range(chunk * span, (chunk + 1) * span):
                out_ref[block_of[group], :, step * width : (step + 1) * width] = qkv_ref[
                    step, :, group * width : (group + 1) * width
                ]


def exchange(blocks, order):
    return lax.all_to_all(
        blocks, AXES, split_axis=0, concat_axis=0, axis_index_groups=[order], tiled=True
    )


def send_orders(sections, per_section):
    peers = sections * per_section
    quarter = math.gcd(peers, 4)
    row = peers // quarter
    turned = [z * row + i for z in range(quarter - 1, -1, -1) for i in range(row - 1, -1, -1)]
    first = turned[row:] + turned[:row]
    half = quarter // 2
    rows = list(range(half, quarter)) + list(range(half))
    second = [z * row + i for z in rows for i in range(row - 1, -1, -1)]
    return first, second


def shards(qkv_all, context_kv):
    sections = lax.axis_size("section")
    peers = sections * lax.axis_size("seq")
    groups = min(peers, HEADS)
    copies = peers // groups
    heads = HEADS // groups
    steps, _, tok_rows, width = qkv_all.shape
    head_dim = width // (3 * HEADS)
    ctx_rows = context_kv.shape[0]
    scale = head_dim ** (-0.5)
    if copies > 1 or heads * ctx_rows != tok_rows:
        return shards_copied(qkv_all, context_kv, sections, groups, copies, heads, scale)

    chunks = math.gcd(groups, 2)
    per_section = peers // sections
    first, second = send_orders(sections, per_section)
    devices = range(sections * per_section)
    block_of = [first.index(second[group]) for group in range(groups)]
    came_from = [[first.index(d) for d in devices if d % sections == s] for s in range(sections)]
    goes_to = [[second.index(d) for d in devices if d % sections == s] for s in range(sections)]
    in_vmem = pl.BlockSpec(memory_space=pltpu.VMEM)
    params = pltpu.CompilerParams(vmem_limit_bytes=32 * 1024 * 1024)
    sent = pl.pallas_call(
        functools.partial(pack_kernel, steps, block_of, heads, ctx_rows, head_dim, chunks),
        out_shape=jax.ShapeDtypeStruct(
            (groups, tok_rows, (steps * heads * 3 + 2) * head_dim), jnp.bfloat16
        ),
        in_specs=[pl.BlockSpec(memory_space=pltpu.HBM)] * 2,
        out_specs=in_vmem,
        scratch_shapes=[
            pltpu.VMEM((steps, tok_rows, width), jnp.bfloat16),
            pltpu.VMEM(context_kv.shape, jnp.bfloat16),
            pltpu.SemaphoreType.DMA((steps, chunks)),
            pltpu.SemaphoreType.DMA,
        ],
        compiler_params=params,
    )(*(pltpu.with_memory_space_constraint(x, pltpu.HBM) for x in (qkv_all, context_kv)))
    got = exchange(sent, first)
    mixed = pl.pallas_call(
        functools.partial(
            attend_kernel, steps, heads, tok_rows, ctx_rows, head_dim, scale, came_from, goes_to
        ),
        out_shape=jax.ShapeDtypeStruct((peers, tok_rows, steps * heads * head_dim), jnp.bfloat16),
        in_specs=[in_vmem],
        out_specs=in_vmem,
        compiler_params=params,
    )(got)
    back = exchange(mixed, second)
    back = back.reshape(groups, tok_rows, steps, heads * head_dim).transpose(2, 1, 0, 3)
    return back.reshape(steps, 1, tok_rows, HEADS * head_dim)


def shards_copied(qkv_all, context_kv, sections, groups, copies, heads, scale):
    steps, _, tok_rows, width = qkv_all.shape
    head_dim = width // (3 * HEADS)
    peers = groups * copies
    share = tok_rows // copies
    ctx_rows = context_kv.shape[0]
    frames = qkv_all[:, 0].reshape(steps, tok_rows, groups, heads, 3, head_dim)
    queries = frames[..., 0, :].reshape(steps, copies, share, groups, heads, head_dim)
    queries = queries.transpose(3, 1, 0, 4, 2, 5).reshape(peers, -1, head_dim)
    key_vals = frames[..., 1:, :].transpose(2, 0, 3, 4, 1, 5).reshape(groups, -1, head_dim)
    ctx = context_kv.reshape(ctx_rows, groups, heads, 2, head_dim)
    ctx = ctx.transpose(1, 2, 3, 0, 4).reshape(groups, -1, head_dim)
    shared = jnp.concatenate([key_vals, ctx], axis=1)
    shared = jnp.broadcast_to(shared[:, None], (groups, copies) + shared.shape[1:])
    shared = shared.reshape((peers,) + shared.shape[2:])
    sent = jnp.concatenate([queries, shared], axis=1)
    got = lax.all_to_all(sent, AXES, split_axis=0, concat_axis=0, tiled=True)
    per_section = peers // sections
    cut = steps * heads * share
    end = cut + steps * heads * 2 * tok_rows
    q = got[:, :cut].reshape(per_section, sections, steps, heads, share, head_dim)
    q = q.transpose(2, 1, 3, 0, 4, 5).reshape(steps, sections, heads, -1, head_dim)
    kv = got[:, cut:end].reshape(per_section, sections, steps, heads, 2, tok_rows, head_dim)
    kv = kv.transpose(2, 1, 4, 3, 0, 5, 6).reshape(steps, sections, 2, heads, -1, head_dim)
    ctx = got[:, end:].reshape(peers, heads, 2, ctx_rows, head_dim)
    earlier = [ctx.transpose(2, 1, 0, 3, 4).reshape(2, heads, -1, head_dim)]
    results = []
    for step in range(steps):
        for s in range(sections):
            keys, vals = jnp.concatenate(earlier + [kv[step, s]], axis=2)
            results.append(
                jnp.stack([softmax_mix(q[step, s, h], keys[h], vals[h], scale) for h in range(heads)])
            )
        earlier = earlier + [kv[step, sections - 1]]
    mixed = jnp.stack(results).reshape(steps, sections, heads, per_section, share, head_dim)
    mixed = mixed.transpose(3, 1, 0, 2, 4, 5).reshape(peers, -1, head_dim)
    back = lax.all_to_all(mixed, AXES, split_axis=0, concat_axis=0, tiled=True)
    back = back.reshape(groups, copies, steps, heads, share, head_dim)
    back = back.transpose(2, 1, 4, 0, 3, 5)
    return back.reshape(steps, 1, tok_rows, HEADS * head_dim)


def solution(mesh):
    in_specs = (P(None, "section", ("rep", "seq"), None), P(("rep", "section", "seq"), None))
    out_specs = P(None, "section", ("rep", "seq"), None)
    return jax.shard_map(shards, mesh=mesh, in_specs=in_specs, out_specs=out_specs, check_vma=False)
```

```python
import functools
import math

import jax
import jax.numpy as jnp
from jax import lax
from jax.experimental import pallas as pl
from jax.experimental.pallas import tpu as pltpu
from jax.sharding import PartitionSpec as P

HEADS = 32
AXES = ("seq", "section")


def softmax_mix(queries, keys, values, scale):
    scores = (
        lax.dot_general(
            queries, keys, (((1,), (1,)), ((), ())), preferred_element_type=jnp.float32
        )
        * scale
    )
    weights = jnp.exp(scores - jnp.max(scores, axis=1, keepdims=True))
    total = jnp.sum(weights, axis=1, keepdims=True)
    mixed = jnp.dot(weights.astype(jnp.bfloat16), values, preferred_element_type=jnp.float32)
    return (mixed / total).astype(jnp.bfloat16)


def attend_kernel(
    steps, heads, tok_rows, ctx_rows, head_dim, scale, came_from, goes_to, got_ref, out_ref
):
    sections = len(came_from)
    sources = got_ref.shape[0]
    ctx_base = steps * heads * 3 * head_dim
    log2_scale = scale * math.log2(math.e)

    def part(step, section, head, role):
        base = ((step * heads + head) * 3 + role) * head_dim
        return jnp.concatenate(
            [got_ref[p, :, base : base + head_dim] for p in came_from[section]], axis=0
        )

    def context(head, role):
        base = ctx_base + role * head_dim
        rows = slice(head * ctx_rows, (head + 1) * ctx_rows)
        return got_ref[:, rows, base : base + head_dim].reshape(sources * ctx_rows, head_dim)

    tasks = []
    for head in range(heads):
        earlier = [(context(head, 0), context(head, 1))]
        for step in range(steps):
            own = [(part(step, s, head, 1), part(step, s, head, 2)) for s in range(sections)]
            for s in range(sections):
                pairs = earlier + [own[s]]
                keys = jnp.concatenate([k for k, _ in pairs], axis=0)
                vals = jnp.concatenate([v for _, v in pairs], axis=0)
                tasks.append((step, s, head, part(step, s, head, 0), keys, vals))
            earlier = earlier + [own[sections - 1]]
    all_scores = [
        lax.dot_general(q, k, (((1,), (1,)), ((), ())), preferred_element_type=jnp.float32)
        for _, _, _, q, k, _ in tasks
    ]
    all_tops = [jnp.max(scores, axis=1, keepdims=True) for scores in all_scores]
    all_weights = [
        jnp.exp2((scores - top) * log2_scale).astype(jnp.bfloat16)
        for scores, top in zip(all_scores, all_tops)
    ]
    all_mixed = [
        jnp.dot(
            weights,
            jnp.concatenate([vals, jnp.ones_like(vals)], axis=1),
            preferred_element_type=jnp.float32,
        )
        for weights, (_, _, _, _, _, vals) in zip(all_weights, tasks)
    ]
    for mixed, (step, s, head, _, _, _) in zip(all_mixed, tasks):
        done = (mixed[:, :head_dim] / mixed[:, head_dim:]).astype(jnp.bfloat16)
        base = (step * heads + head) * head_dim
        for slot, p in enumerate(goes_to[s]):
            out_ref[p, :, base : base + head_dim] = done[slot * tok_rows : (slot + 1) * tok_rows]


def pack_kernel(
    steps, block_of, heads, ctx_rows, head_dim, chunks, qkv_hbm, ctx_hbm, out_ref, qkv_ref, ctx_ref, sems, ctx_sem
):
    groups = len(block_of)
    width = heads * 3 * head_dim
    span = groups // chunks
    ctx_copy = pltpu.make_async_copy(ctx_hbm, ctx_ref, ctx_sem)
    copies = []
    for step in range(steps):
        for chunk in range(chunks):
            columns = pl.ds(chunk * span * width, span * width)
            copies.append(
                pltpu.make_async_copy(
                    qkv_hbm.at[step, 0, :, columns],
                    qkv_ref.at[step, :, columns],
                    sems.at[step, chunk],
                )
            )
    ctx_copy.start()
    for copy in copies:
        copy.start()
    base = steps * width
    ctx_copy.wait()
    for group in range(groups):
        for role in range(2):
            columns = [((group * heads + head) * 2 + role) * head_dim for head in range(heads)]
            block = [ctx_ref[:, c : c + head_dim] for c in columns]
            out_ref[block_of[group], :, base + role * head_dim : base + (role + 1) * head_dim] = (
                jnp.concatenate(block, axis=0)
            )
    for step in range(steps):
        for chunk in range(chunks):
            copies[step * chunks + chunk].wait()
            for group in range(chunk * span, (chunk + 1) * span):
                out_ref[block_of[group], :, step * width : (step + 1) * width] = qkv_ref[
                    step, :, group * width : (group + 1) * width
                ]


def unpack_kernel(back_ref, out_hbm, rows_ref, sems):
    groups = back_ref.shape[0]
    steps = rows_ref.shape[0]
    width = rows_ref.shape[2] // groups
    copies = []
    for step in range(steps):
        for group in range(groups):
            rows_ref[step, :, group * width : (group + 1) * width] = back_ref[
                group, :, step * width : (step + 1) * width
            ]
        copies.append(
            pltpu.make_async_copy(rows_ref.at[step], out_hbm.at[step, 0], sems.at[step])
        )
        copies[-1].start()
    for copy in copies:
        copy.wait()


def exchange(blocks, order):
    return lax.all_to_all(
        blocks, AXES, split_axis=0, concat_axis=0, axis_index_groups=[order], tiled=True
    )


def send_orders(sections, per_section):
    peers = sections * per_section
    quarter = math.gcd(peers, 4)
    row = peers // quarter
    half = quarter // 2
    rows = list(range(half, quarter)) + list(range(half))
    first = [z * row + i for z in rows for i in range(row - 1, -1, -1)]
    second = first
    return first, second


def shards(qkv_all, context_kv):
    sections = lax.axis_size("section")
    peers = sections * lax.axis_size("seq")
    groups = min(peers, HEADS)
    copies = peers // groups
    heads = HEADS // groups
    steps, _, tok_rows, width = qkv_all.shape
    head_dim = width // (3 * HEADS)
    ctx_rows = context_kv.shape[0]
    scale = head_dim ** (-0.5)
    if copies > 1 or heads * ctx_rows != tok_rows:
        return shards_copied(qkv_all, context_kv, sections, groups, copies, heads, scale)

    chunks = math.gcd(groups, 4)
    per_section = peers // sections
    first, second = send_orders(sections, per_section)
    devices = range(sections * per_section)
    block_of = [first.index(second[group]) for group in range(groups)]
    came_from = [[first.index(d) for d in devices if d % sections == s] for s in range(sections)]
    goes_to = [[second.index(d) for d in devices if d % sections == s] for s in range(sections)]
    in_vmem = pl.BlockSpec(memory_space=pltpu.VMEM)
    params = pltpu.CompilerParams(vmem_limit_bytes=32 * 1024 * 1024)
    sent = pl.pallas_call(
        functools.partial(pack_kernel, steps, block_of, heads, ctx_rows, head_dim, chunks),
        out_shape=jax.ShapeDtypeStruct(
            (groups, tok_rows, (steps * heads * 3 + 2) * head_dim), jnp.bfloat16
        ),
        in_specs=[pl.BlockSpec(memory_space=pltpu.HBM)] * 2,
        out_specs=in_vmem,
        scratch_shapes=[
            pltpu.VMEM((steps, tok_rows, width), jnp.bfloat16),
            pltpu.VMEM(context_kv.shape, jnp.bfloat16),
            pltpu.SemaphoreType.DMA((steps, chunks)),
            pltpu.SemaphoreType.DMA,
        ],
        compiler_params=params,
    )(*(pltpu.with_memory_space_constraint(x, pltpu.HBM) for x in (qkv_all, context_kv)))
    got = exchange(sent, first)
    mixed = pl.pallas_call(
        functools.partial(
            attend_kernel, steps, heads, tok_rows, ctx_rows, head_dim, scale, came_from, goes_to
        ),
        out_shape=jax.ShapeDtypeStruct((peers, tok_rows, steps * heads * head_dim), jnp.bfloat16),
        in_specs=[in_vmem],
        out_specs=in_vmem,
        compiler_params=params,
    )(got)
    back = exchange(mixed, second)
    return pl.pallas_call(
        unpack_kernel,
        out_shape=jax.ShapeDtypeStruct((steps, 1, tok_rows, HEADS * head_dim), jnp.bfloat16),
        in_specs=[in_vmem],
        out_specs=pl.BlockSpec(memory_space=pltpu.HBM),
        scratch_shapes=[
            pltpu.VMEM((steps, tok_rows, HEADS * head_dim), jnp.bfloat16),
            pltpu.SemaphoreType.DMA((steps,)),
        ],
        compiler_params=params,
    )(back)


def shards_copied(qkv_all, context_kv, sections, groups, copies, heads, scale):
    steps, _, tok_rows, width = qkv_all.shape
    head_dim = width // (3 * HEADS)
    peers = groups * copies
    share = tok_rows // copies
    ctx_rows = context_kv.shape[0]
    frames = qkv_all[:, 0].reshape(steps, tok_rows, groups, heads, 3, head_dim)
    queries = frames[..., 0, :].reshape(steps, copies, share, groups, heads, head_dim)
    queries = queries.transpose(3, 1, 0, 4, 2, 5).reshape(peers, -1, head_dim)
    key_vals = frames[..., 1:, :].transpose(2, 0, 3, 4, 1, 5).reshape(groups, -1, head_dim)
    ctx = context_kv.reshape(ctx_rows, groups, heads, 2, head_dim)
    ctx = ctx.transpose(1, 2, 3, 0, 4).reshape(groups, -1, head_dim)
    shared = jnp.concatenate([key_vals, ctx], axis=1)
    shared = jnp.broadcast_to(shared[:, None], (groups, copies) + shared.shape[1:])
    shared = shared.reshape((peers,) + shared.shape[2:])
    sent = jnp.concatenate([queries, shared], axis=1)
    got = lax.all_to_all(sent, AXES, split_axis=0, concat_axis=0, tiled=True)
    per_section = peers // sections
    cut = steps * heads * share
    end = cut + steps * heads * 2 * tok_rows
    q = got[:, :cut].reshape(per_section, sections, steps, heads, share, head_dim)
    q = q.transpose(2, 1, 3, 0, 4, 5).reshape(steps, sections, heads, -1, head_dim)
    kv = got[:, cut:end].reshape(per_section, sections, steps, heads, 2, tok_rows, head_dim)
    kv = kv.transpose(2, 1, 4, 3, 0, 5, 6).reshape(steps, sections, 2, heads, -1, head_dim)
    ctx = got[:, end:].reshape(peers, heads, 2, ctx_rows, head_dim)
    earlier = [ctx.transpose(2, 1, 0, 3, 4).reshape(2, heads, -1, head_dim)]
    results = []
    for step in range(steps):
        for s in range(sections):
            keys, vals = jnp.concatenate(earlier + [kv[step, s]], axis=2)
            results.append(
                jnp.stack([softmax_mix(q[step, s, h], keys[h], vals[h], scale) for h in range(heads)])
            )
        earlier = earlier + [kv[step, sections - 1]]
    mixed = jnp.stack(results).reshape(steps, sections, heads, per_section, share, head_dim)
    mixed = mixed.transpose(3, 1, 0, 2, 4, 5).reshape(peers, -1, head_dim)
    back = lax.all_to_all(mixed, AXES, split_axis=0, concat_axis=0, tiled=True)
    back = back.reshape(groups, copies, steps, heads, share, head_dim)
    back = back.transpose(2, 1, 4, 0, 3, 5)
    return back.reshape(steps, 1, tok_rows, HEADS * head_dim)


def solution(mesh):
    in_specs = (P(None, "section", ("rep", "seq"), None), P(("rep", "section", "seq"), None))
    out_specs = P(None, "section", ("rep", "seq"), None)
    return jax.shard_map(shards, mesh=mesh, in_specs=in_specs, out_specs=out_specs, check_vma=False)
```

```python
import functools
import math

import jax
import jax.numpy as jnp
from jax import lax
from jax.experimental import pallas as pl
from jax.experimental.pallas import tpu as pltpu
from jax.sharding import PartitionSpec as P

HEADS = 32
AXES = ("seq", "section")


def softmax_mix(queries, keys, values, scale):
    scores = (
        lax.dot_general(
            queries, keys, (((1,), (1,)), ((), ())), preferred_element_type=jnp.float32
        )
        * scale
    )
    weights = jnp.exp(scores - jnp.max(scores, axis=1, keepdims=True))
    total = jnp.sum(weights, axis=1, keepdims=True)
    mixed = jnp.dot(weights.astype(jnp.bfloat16), values, preferred_element_type=jnp.float32)
    return (mixed / total).astype(jnp.bfloat16)


def attend_kernel(
    steps, heads, tok_rows, ctx_rows, head_dim, scale, came_from, goes_to, got_ref, out_ref
):
    sections = len(came_from)
    sources = got_ref.shape[0]
    ctx_base = steps * heads * 3 * head_dim
    log2_scale = scale * math.log2(math.e)

    def part(step, section, head, role):
        base = ((step * heads + head) * 3 + role) * head_dim
        return jnp.concatenate(
            [got_ref[p, :, base : base + head_dim] for p in came_from[section]], axis=0
        )

    def context(head, role):
        base = ctx_base + role * head_dim
        rows = slice(head * ctx_rows, (head + 1) * ctx_rows)
        return got_ref[:, rows, base : base + head_dim].reshape(sources * ctx_rows, head_dim)

    tasks = []
    for head in range(heads):
        earlier = [(context(head, 0), context(head, 1))]
        for step in range(steps):
            own = [(part(step, s, head, 1), part(step, s, head, 2)) for s in range(sections)]
            for s in range(sections):
                pairs = earlier + [own[s]]
                keys = jnp.concatenate([k for k, _ in pairs], axis=0)
                vals = jnp.concatenate([v for _, v in pairs], axis=0)
                tasks.append((step, s, head, part(step, s, head, 0), keys, vals))
            earlier = earlier + [own[sections - 1]]
    all_scores = [
        lax.dot_general(q, k, (((1,), (1,)), ((), ())), preferred_element_type=jnp.float32)
        for _, _, _, q, k, _ in tasks
    ]
    all_tops = [jnp.max(scores, axis=1, keepdims=True) for scores in all_scores]
    all_weights = [
        jnp.exp2((scores - top) * log2_scale).astype(jnp.bfloat16)
        for scores, top in zip(all_scores, all_tops)
    ]
    all_mixed = [
        jnp.dot(
            weights,
            jnp.concatenate([vals, jnp.ones_like(vals)], axis=1),
            preferred_element_type=jnp.float32,
        )
        for weights, (_, _, _, _, _, vals) in zip(all_weights, tasks)
    ]
    for mixed, (step, s, head, _, _, _) in zip(all_mixed, tasks):
        done = (mixed[:, :head_dim] / mixed[:, head_dim:]).astype(jnp.bfloat16)
        base = (step * heads + head) * head_dim
        for slot, p in enumerate(goes_to[s]):
            out_ref[p, :, base : base + head_dim] = done[slot * tok_rows : (slot + 1) * tok_rows]


def pack_kernel(
    steps, block_of, heads, ctx_rows, head_dim, chunks, qkv_hbm, ctx_hbm, out_ref, qkv_ref, ctx_ref, sems, ctx_sem
):
    groups = len(block_of)
    width = heads * 3 * head_dim
    span = groups // chunks
    ctx_copy = pltpu.make_async_copy(ctx_hbm, ctx_ref, ctx_sem)
    copies = []
    for step in range(steps):
        for chunk in range(chunks):
            columns = pl.ds(chunk * span * width, span * width)
            copies.append(
                pltpu.make_async_copy(
                    qkv_hbm.at[step, 0, :, columns],
                    qkv_ref.at[step, :, columns],
                    sems.at[step, chunk],
                )
            )
    ctx_copy.start()
    for copy in copies:
        copy.start()
    base = steps * width
    ctx_copy.wait()
    for group in range(groups):
        for role in range(2):
            columns = [((group * heads + head) * 2 + role) * head_dim for head in range(heads)]
            block = [ctx_ref[:, c : c + head_dim] for c in columns]
            out_ref[block_of[group], :, base + role * head_dim : base + (role + 1) * head_dim] = (
                jnp.concatenate(block, axis=0)
            )
    for step in range(steps):
        for chunk in range(chunks):
            copies[step * chunks + chunk].wait()
            for group in range(chunk * span, (chunk + 1) * span):
                out_ref[block_of[group], :, step * width : (step + 1) * width] = qkv_ref[
                    step, :, group * width : (group + 1) * width
                ]


def exchange(blocks, order):
    return lax.all_to_all(
        blocks, AXES, split_axis=0, concat_axis=0, axis_index_groups=[order], tiled=True
    )


def send_orders(sections, per_section):
    peers = sections * per_section
    quarter = math.gcd(peers, 4)
    row = peers // quarter
    inner = [i for s in range(sections - 1, -1, -1) for i in range(row - sections + s, -1, -sections)]
    turned = [z * row + i for z in range(quarter - 1, -1, -1) for i in inner]
    first = turned[row:] + turned[:row]
    half = quarter // 2
    rows = list(range(half, quarter)) + list(range(half))
    second = [z * row + i for z in rows for i in inner]
    return first, second


def shards(qkv_all, context_kv):
    sections = lax.axis_size("section")
    peers = sections * lax.axis_size("seq")
    groups = min(peers, HEADS)
    copies = peers // groups
    heads = HEADS // groups
    steps, _, tok_rows, width = qkv_all.shape
    head_dim = width // (3 * HEADS)
    ctx_rows = context_kv.shape[0]
    scale = head_dim ** (-0.5)
    if copies > 1 or heads * ctx_rows != tok_rows:
        return shards_copied(qkv_all, context_kv, sections, groups, copies, heads, scale)

    chunks = math.gcd(groups, 2)
    per_section = peers // sections
    first, second = send_orders(sections, per_section)
    devices = range(sections * per_section)
    block_of = [first.index(second[group]) for group in range(groups)]
    came_from = [[first.index(d) for d in devices if d % sections == s] for s in range(sections)]
    goes_to = [[second.index(d) for d in devices if d % sections == s] for s in range(sections)]
    in_vmem = pl.BlockSpec(memory_space=pltpu.VMEM)
    params = pltpu.CompilerParams(vmem_limit_bytes=32 * 1024 * 1024)
    sent = pl.pallas_call(
        functools.partial(pack_kernel, steps, block_of, heads, ctx_rows, head_dim, chunks),
        out_shape=jax.ShapeDtypeStruct(
            (groups, tok_rows, (steps * heads * 3 + 2) * head_dim), jnp.bfloat16
        ),
        in_specs=[pl.BlockSpec(memory_space=pltpu.HBM)] * 2,
        out_specs=in_vmem,
        scratch_shapes=[
            pltpu.VMEM((steps, tok_rows, width), jnp.bfloat16),
            pltpu.VMEM(context_kv.shape, jnp.bfloat16),
            pltpu.SemaphoreType.DMA((steps, chunks)),
            pltpu.SemaphoreType.DMA,
        ],
        compiler_params=params,
    )(*(pltpu.with_memory_space_constraint(x, pltpu.HBM) for x in (qkv_all, context_kv)))
    got = exchange(sent, first)
    mixed = pl.pallas_call(
        functools.partial(
            attend_kernel, steps, heads, tok_rows, ctx_rows, head_dim, scale, came_from, goes_to
        ),
        out_shape=jax.ShapeDtypeStruct((peers, tok_rows, steps * heads * head_dim), jnp.bfloat16),
        in_specs=[in_vmem],
        out_specs=in_vmem,
        compiler_params=params,
    )(got)
    back = exchange(mixed, second)
    back = back.reshape(groups, tok_rows, steps, heads * head_dim).transpose(2, 1, 0, 3)
    return back.reshape(steps, 1, tok_rows, HEADS * head_dim)


def shards_copied(qkv_all, context_kv, sections, groups, copies, heads, scale):
    steps, _, tok_rows, width = qkv_all.shape
    head_dim = width // (3 * HEADS)
    peers = groups * copies
    share = tok_rows // copies
    ctx_rows = context_kv.shape[0]
    frames = qkv_all[:, 0].reshape(steps, tok_rows, groups, heads, 3, head_dim)
    queries = frames[..., 0, :].reshape(steps, copies, share, groups, heads, head_dim)
    queries = queries.transpose(3, 1, 0, 4, 2, 5).reshape(peers, -1, head_dim)
    key_vals = frames[..., 1:, :].transpose(2, 0, 3, 4, 1, 5).reshape(groups, -1, head_dim)
    ctx = context_kv.reshape(ctx_rows, groups, heads, 2, head_dim)
    ctx = ctx.transpose(1, 2, 3, 0, 4).reshape(groups, -1, head_dim)
    shared = jnp.concatenate([key_vals, ctx], axis=1)
    shared = jnp.broadcast_to(shared[:, None], (groups, copies) + shared.shape[1:])
    shared = shared.reshape((peers,) + shared.shape[2:])
    sent = jnp.concatenate([queries, shared], axis=1)
    got = lax.all_to_all(sent, AXES, split_axis=0, concat_axis=0, tiled=True)
    per_section = peers // sections
    cut = steps * heads * share
    end = cut + steps * heads * 2 * tok_rows
    q = got[:, :cut].reshape(per_section, sections, steps, heads, share, head_dim)
    q = q.transpose(2, 1, 3, 0, 4, 5).reshape(steps, sections, heads, -1, head_dim)
    kv = got[:, cut:end].reshape(per_section, sections, steps, heads, 2, tok_rows, head_dim)
    kv = kv.transpose(2, 1, 4, 3, 0, 5, 6).reshape(steps, sections, 2, heads, -1, head_dim)
    ctx = got[:, end:].reshape(peers, heads, 2, ctx_rows, head_dim)
    earlier = [ctx.transpose(2, 1, 0, 3, 4).reshape(2, heads, -1, head_dim)]
    results = []
    for step in range(steps):
        for s in range(sections):
            keys, vals = jnp.concatenate(earlier + [kv[step, s]], axis=2)
            results.append(
                jnp.stack([softmax_mix(q[step, s, h], keys[h], vals[h], scale) for h in range(heads)])
            )
        earlier = earlier + [kv[step, sections - 1]]
    mixed = jnp.stack(results).reshape(steps, sections, heads, per_section, share, head_dim)
    mixed = mixed.transpose(3, 1, 0, 2, 4, 5).reshape(peers, -1, head_dim)
    back = lax.all_to_all(mixed, AXES, split_axis=0, concat_axis=0, tiled=True)
    back = back.reshape(groups, copies, steps, heads, share, head_dim)
    back = back.transpose(2, 1, 4, 0, 3, 5)
    return back.reshape(steps, 1, tok_rows, HEADS * head_dim)


def solution(mesh):
    in_specs = (P(None, "section", ("rep", "seq"), None), P(("rep", "section", "seq"), None))
    out_specs = P(None, "section", ("rep", "seq"), None)
    return jax.shard_map(shards, mesh=mesh, in_specs=in_specs, out_specs=out_specs, check_vma=False)
```

```python
import functools
import math

import jax
import jax.numpy as jnp
from jax import lax
from jax.experimental import pallas as pl
from jax.experimental.pallas import tpu as pltpu
from jax.sharding import PartitionSpec as P

HEADS = 32
AXES = ("seq", "section")


def softmax_mix(queries, keys, values, scale):
    scores = (
        lax.dot_general(
            queries, keys, (((1,), (1,)), ((), ())), preferred_element_type=jnp.float32
        )
        * scale
    )
    weights = jnp.exp(scores - jnp.max(scores, axis=1, keepdims=True))
    total = jnp.sum(weights, axis=1, keepdims=True)
    mixed = jnp.dot(weights.astype(jnp.bfloat16), values, preferred_element_type=jnp.float32)
    return (mixed / total).astype(jnp.bfloat16)


def attend_kernel(
    steps, heads, tok_rows, ctx_rows, head_dim, scale, came_from, goes_to, got_ref, out_ref
):
    sections = len(came_from)
    sources = got_ref.shape[0]
    ctx_base = steps * heads * 3 * head_dim
    log2_scale = scale * math.log2(math.e)

    def part(step, section, head, role):
        base = ((step * heads + head) * 3 + role) * head_dim
        return jnp.concatenate(
            [got_ref[p, :, base : base + head_dim] for p in came_from[section]], axis=0
        )

    def context(head, role):
        base = ctx_base + role * head_dim
        rows = slice(head * ctx_rows, (head + 1) * ctx_rows)
        return got_ref[:, rows, base : base + head_dim].reshape(sources * ctx_rows, head_dim)

    tasks = []
    for head in range(heads):
        earlier = [(context(head, 0), context(head, 1))]
        for step in range(steps):
            own = [(part(step, s, head, 1), part(step, s, head, 2)) for s in range(sections)]
            for s in range(sections):
                pairs = earlier + [own[s]]
                keys = jnp.concatenate([k for k, _ in pairs], axis=0)
                vals = jnp.concatenate([v for _, v in pairs], axis=0)
                tasks.append((step, s, head, part(step, s, head, 0), keys, vals))
            earlier = earlier + [own[sections - 1]]
    all_scores = [
        lax.dot_general(q, k, (((1,), (1,)), ((), ())), preferred_element_type=jnp.float32)
        for _, _, _, q, k, _ in tasks
    ]
    all_tops = [jnp.max(scores, axis=1, keepdims=True) for scores in all_scores]
    all_weights = [
        jnp.exp2((scores - top) * log2_scale).astype(jnp.bfloat16)
        for scores, top in zip(all_scores, all_tops)
    ]
    all_mixed = [
        jnp.dot(
            weights,
            jnp.concatenate([vals, jnp.ones_like(vals)], axis=1),
            preferred_element_type=jnp.float32,
        )
        for weights, (_, _, _, _, _, vals) in zip(all_weights, tasks)
    ]
    for mixed, (step, s, head, _, _, _) in zip(all_mixed, tasks):
        done = (mixed[:, :head_dim] / mixed[:, head_dim:]).astype(jnp.bfloat16)
        base = (step * heads + head) * head_dim
        for slot, p in enumerate(goes_to[s]):
            out_ref[p, :, base : base + head_dim] = done[slot * tok_rows : (slot + 1) * tok_rows]


def pack_kernel(
    steps, block_of, heads, ctx_rows, head_dim, chunks, qkv_hbm, ctx_hbm, out_ref, qkv_ref, ctx_ref, sems, ctx_sem
):
    groups = len(block_of)
    width = heads * 3 * head_dim
    span = groups // chunks
    ctx_copy = pltpu.make_async_copy(ctx_hbm, ctx_ref, ctx_sem)
    copies = []
    for step in range(steps):
        for chunk in range(chunks):
            columns = pl.ds(chunk * span * width, span * width)
            copies.append(
                pltpu.make_async_copy(
                    qkv_hbm.at[step, 0, :, columns],
                    qkv_ref.at[step, :, columns],
                    sems.at[step, chunk],
                )
            )
    ctx_copy.start()
    for copy in copies:
        copy.start()
    base = steps * width
    ctx_copy.wait()
    for group in range(groups):
        for role in range(2):
            columns = [((group * heads + head) * 2 + role) * head_dim for head in range(heads)]
            block = [ctx_ref[:, c : c + head_dim] for c in columns]
            out_ref[block_of[group], :, base + role * head_dim : base + (role + 1) * head_dim] = (
                jnp.concatenate(block, axis=0)
            )
    for step in range(steps):
        for chunk in range(chunks):
            copies[step * chunks + chunk].wait()
            for group in range(chunk * span, (chunk + 1) * span):
                out_ref[block_of[group], :, step * width : (step + 1) * width] = qkv_ref[
                    step, :, group * width : (group + 1) * width
                ]


def exchange(blocks, order):
    return lax.all_to_all(
        blocks, AXES, split_axis=0, concat_axis=0, axis_index_groups=[order], tiled=True
    )


def send_orders(sections, per_section):
    peers = sections * per_section
    quarter = math.gcd(peers, 4)
    row = peers // quarter
    half = quarter // 2
    rows = list(range(half, quarter)) + list(range(half))
    across = rows[::half] + rows[1::half] if quarter == 4 else rows
    first = [z * row + i for z in across for i in range(row - 1, -1, -1)]
    rows = rows[:half] + rows[: half - 1 : -1]
    second = [z * row + i for z in rows for i in range(row - 1, -1, -1)]
    return first, second


def shards(qkv_all, context_kv):
    sections = lax.axis_size("section")
    peers = sections * lax.axis_size("seq")
    groups = min(peers, HEADS)
    copies = peers // groups
    heads = HEADS // groups
    steps, _, tok_rows, width = qkv_all.shape
    head_dim = width // (3 * HEADS)
    ctx_rows = context_kv.shape[0]
    scale = head_dim ** (-0.5)
    if copies > 1 or heads * ctx_rows != tok_rows:
        return shards_copied(qkv_all, context_kv, sections, groups, copies, heads, scale)

    chunks = math.gcd(groups, 2)
    per_section = peers // sections
    first, second = send_orders(sections, per_section)
    devices = range(sections * per_section)
    block_of = [first.index(second[group]) for group in range(groups)]
    came_from = [[first.index(d) for d in devices if d % sections == s] for s in range(sections)]
    goes_to = [[second.index(d) for d in devices if d % sections == s] for s in range(sections)]
    in_vmem = pl.BlockSpec(memory_space=pltpu.VMEM)
    params = pltpu.CompilerParams(vmem_limit_bytes=32 * 1024 * 1024)
    sent = pl.pallas_call(
        functools.partial(pack_kernel, steps, block_of, heads, ctx_rows, head_dim, chunks),
        out_shape=jax.ShapeDtypeStruct(
            (groups, tok_rows, (steps * heads * 3 + 2) * head_dim), jnp.bfloat16
        ),
        in_specs=[pl.BlockSpec(memory_space=pltpu.HBM)] * 2,
        out_specs=in_vmem,
        scratch_shapes=[
            pltpu.VMEM((steps, tok_rows, width), jnp.bfloat16),
            pltpu.VMEM(context_kv.shape, jnp.bfloat16),
            pltpu.SemaphoreType.DMA((steps, chunks)),
            pltpu.SemaphoreType.DMA,
        ],
        compiler_params=params,
    )(*(pltpu.with_memory_space_constraint(x, pltpu.HBM) for x in (qkv_all, context_kv)))
    got = exchange(sent, first)
    mixed = pl.pallas_call(
        functools.partial(
            attend_kernel, steps, heads, tok_rows, ctx_rows, head_dim, scale, came_from, goes_to
        ),
        out_shape=jax.ShapeDtypeStruct((peers, tok_rows, steps * heads * head_dim), jnp.bfloat16),
        in_specs=[in_vmem],
        out_specs=in_vmem,
        compiler_params=params,
    )(got)
    back = exchange(mixed, second)
    back = back.reshape(groups, tok_rows, steps, heads * head_dim).transpose(2, 1, 0, 3)
    return back.reshape(steps, 1, tok_rows, HEADS * head_dim)


def shards_copied(qkv_all, context_kv, sections, groups, copies, heads, scale):
    steps, _, tok_rows, width = qkv_all.shape
    head_dim = width // (3 * HEADS)
    peers = groups * copies
    share = tok_rows // copies
    ctx_rows = context_kv.shape[0]
    frames = qkv_all[:, 0].reshape(steps, tok_rows, groups, heads, 3, head_dim)
    queries = frames[..., 0, :].reshape(steps, copies, share, groups, heads, head_dim)
    queries = queries.transpose(3, 1, 0, 4, 2, 5).reshape(peers, -1, head_dim)
    key_vals = frames[..., 1:, :].transpose(2, 0, 3, 4, 1, 5).reshape(groups, -1, head_dim)
    ctx = context_kv.reshape(ctx_rows, groups, heads, 2, head_dim)
    ctx = ctx.transpose(1, 2, 3, 0, 4).reshape(groups, -1, head_dim)
    shared = jnp.concatenate([key_vals, ctx], axis=1)
    shared = jnp.broadcast_to(shared[:, None], (groups, copies) + shared.shape[1:])
    shared = shared.reshape((peers,) + shared.shape[2:])
    sent = jnp.concatenate([queries, shared], axis=1)
    got = lax.all_to_all(sent, AXES, split_axis=0, concat_axis=0, tiled=True)
    per_section = peers // sections
    cut = steps * heads * share
    end = cut + steps * heads * 2 * tok_rows
    q = got[:, :cut].reshape(per_section, sections, steps, heads, share, head_dim)
    q = q.transpose(2, 1, 3, 0, 4, 5).reshape(steps, sections, heads, -1, head_dim)
    kv = got[:, cut:end].reshape(per_section, sections, steps, heads, 2, tok_rows, head_dim)
    kv = kv.transpose(2, 1, 4, 3, 0, 5, 6).reshape(steps, sections, 2, heads, -1, head_dim)
    ctx = got[:, end:].reshape(peers, heads, 2, ctx_rows, head_dim)
    earlier = [ctx.transpose(2, 1, 0, 3, 4).reshape(2, heads, -1, head_dim)]
    results = []
    for step in range(steps):
        for s in range(sections):
            keys, vals = jnp.concatenate(earlier + [kv[step, s]], axis=2)
            results.append(
                jnp.stack([softmax_mix(q[step, s, h], keys[h], vals[h], scale) for h in range(heads)])
            )
        earlier = earlier + [kv[step, sections - 1]]
    mixed = jnp.stack(results).reshape(steps, sections, heads, per_section, share, head_dim)
    mixed = mixed.transpose(3, 1, 0, 2, 4, 5).reshape(peers, -1, head_dim)
    back = lax.all_to_all(mixed, AXES, split_axis=0, concat_axis=0, tiled=True)
    back = back.reshape(groups, copies, steps, heads, share, head_dim)
    back = back.transpose(2, 1, 4, 0, 3, 5)
    return back.reshape(steps, 1, tok_rows, HEADS * head_dim)


def solution(mesh):
    in_specs = (P(None, "section", ("rep", "seq"), None), P(("rep", "section", "seq"), None))
    out_specs = P(None, "section", ("rep", "seq"), None)
    return jax.shard_map(shards, mesh=mesh, in_specs=in_specs, out_specs=out_specs, check_vma=False)
```

```python
import functools
import math

import jax
import jax.numpy as jnp
from jax import lax
from jax.experimental import pallas as pl
from jax.experimental.pallas import tpu as pltpu
from jax.sharding import PartitionSpec as P

HEADS = 32
AXES = ("seq", "section")


def softmax_mix(queries, keys, values, scale):
    scores = (
        lax.dot_general(
            queries, keys, (((1,), (1,)), ((), ())), preferred_element_type=jnp.float32
        )
        * scale
    )
    weights = jnp.exp(scores - jnp.max(scores, axis=1, keepdims=True))
    total = jnp.sum(weights, axis=1, keepdims=True)
    mixed = jnp.dot(weights.astype(jnp.bfloat16), values, preferred_element_type=jnp.float32)
    return (mixed / total).astype(jnp.bfloat16)


def attend_kernel(
    steps, heads, tok_rows, ctx_rows, head_dim, scale, came_from, goes_to, got_ref, out_ref
):
    sections = len(came_from)
    sources = got_ref.shape[0]
    ctx_base = steps * heads * 3 * head_dim
    log2_scale = scale * math.log2(math.e)

    def part(step, section, head, role):
        base = ((step * heads + head) * 3 + role) * head_dim
        return jnp.concatenate(
            [got_ref[p, :, base : base + head_dim] for p in came_from[section]], axis=0
        )

    def context(head, role):
        base = ctx_base + role * head_dim
        rows = slice(head * ctx_rows, (head + 1) * ctx_rows)
        return got_ref[:, rows, base : base + head_dim].reshape(sources * ctx_rows, head_dim)

    tasks = []
    for head in range(heads):
        earlier = [(context(head, 0), context(head, 1))]
        for step in range(steps):
            own = [(part(step, s, head, 1), part(step, s, head, 2)) for s in range(sections)]
            for s in range(sections):
                pairs = earlier + [own[s]]
                keys = jnp.concatenate([k for k, _ in pairs], axis=0)
                vals = jnp.concatenate([v for _, v in pairs], axis=0)
                tasks.append((step, s, head, part(step, s, head, 0), keys, vals))
            earlier = earlier + [own[sections - 1]]
    all_scores = [
        lax.dot_general(q, k, (((1,), (1,)), ((), ())), preferred_element_type=jnp.float32)
        for _, _, _, q, k, _ in tasks
    ]
    all_tops = [jnp.max(scores, axis=1, keepdims=True) for scores in all_scores]
    all_weights = [
        jnp.exp2((scores - top) * log2_scale).astype(jnp.bfloat16)
        for scores, top in zip(all_scores, all_tops)
    ]
    all_mixed = [
        jnp.dot(
            weights,
            jnp.concatenate([vals, jnp.ones_like(vals)], axis=1),
            preferred_element_type=jnp.float32,
        )
        for weights, (_, _, _, _, _, vals) in zip(all_weights, tasks)
    ]
    for mixed, (step, s, head, _, _, _) in zip(all_mixed, tasks):
        done = (mixed[:, :head_dim] / mixed[:, head_dim:]).astype(jnp.bfloat16)
        base = (step * heads + head) * head_dim
        for slot, p in enumerate(goes_to[s]):
            out_ref[p, :, base : base + head_dim] = done[slot * tok_rows : (slot + 1) * tok_rows]


def pack_kernel(
    steps, block_of, heads, ctx_rows, head_dim, chunks, qkv_hbm, ctx_hbm, out_ref, qkv_ref, ctx_ref, sems, ctx_sem
):
    groups = len(block_of)
    width = heads * 3 * head_dim
    span = groups // chunks
    ctx_copy = pltpu.make_async_copy(ctx_hbm, ctx_ref, ctx_sem)
    copies = []
    for step in range(steps):
        for chunk in range(chunks):
            columns = pl.ds(chunk * span * width, span * width)
            copies.append(
                pltpu.make_async_copy(
                    qkv_hbm.at[step, 0, :, columns],
                    qkv_ref.at[step, :, columns],
                    sems.at[step, chunk],
                )
            )
    ctx_copy.start()
    for copy in copies:
        copy.start()
    base = steps * width
    ctx_copy.wait()
    for group in range(groups):
        for role in range(2):
            columns = [((group * heads + head) * 2 + role) * head_dim for head in range(heads)]
            block = [ctx_ref[:, c : c + head_dim] for c in columns]
            out_ref[block_of[group], :, base + role * head_dim : base + (role + 1) * head_dim] = (
                jnp.concatenate(block, axis=0)
            )
    for step in range(steps):
        for chunk in range(chunks):
            copies[step * chunks + chunk].wait()
            for group in range(chunk * span, (chunk + 1) * span):
                out_ref[block_of[group], :, step * width : (step + 1) * width] = qkv_ref[
                    step, :, group * width : (group + 1) * width
                ]


def exchange(blocks, order):
    return lax.all_to_all(
        blocks, AXES, split_axis=0, concat_axis=0, axis_index_groups=[order], tiled=True
    )


def send_orders(sections, per_section):
    peers = sections * per_section
    quarter = math.gcd(peers, 4)
    row = peers // quarter
    half = quarter // 2
    rows = list(range(half, quarter)) + list(range(half))
    across = rows[::half] + rows[1::half] if quarter == 4 else rows
    inner = [i for i in range(row) if i % 2][::-1] + [i for i in range(row) if i % 2 == 0]
    first = [z * row + i for z in across for i in inner]
    second = [z * row + i for z in rows for i in inner]
    return first, second


def shards(qkv_all, context_kv):
    sections = lax.axis_size("section")
    peers = sections * lax.axis_size("seq")
    groups = min(peers, HEADS)
    copies = peers // groups
    heads = HEADS // groups
    steps, _, tok_rows, width = qkv_all.shape
    head_dim = width // (3 * HEADS)
    ctx_rows = context_kv.shape[0]
    scale = head_dim ** (-0.5)
    if copies > 1 or heads * ctx_rows != tok_rows:
        return shards_copied(qkv_all, context_kv, sections, groups, copies, heads, scale)

    chunks = math.gcd(groups, 2)
    per_section = peers // sections
    first, second = send_orders(sections, per_section)
    devices = range(sections * per_section)
    block_of = [first.index(second[group]) for group in range(groups)]
    came_from = [[first.index(d) for d in devices if d % sections == s] for s in range(sections)]
    goes_to = [[second.index(d) for d in devices if d % sections == s] for s in range(sections)]
    in_vmem = pl.BlockSpec(memory_space=pltpu.VMEM)
    params = pltpu.CompilerParams(vmem_limit_bytes=32 * 1024 * 1024)
    sent = pl.pallas_call(
        functools.partial(pack_kernel, steps, block_of, heads, ctx_rows, head_dim, chunks),
        out_shape=jax.ShapeDtypeStruct(
            (groups, tok_rows, (steps * heads * 3 + 2) * head_dim), jnp.bfloat16
        ),
        in_specs=[pl.BlockSpec(memory_space=pltpu.HBM)] * 2,
        out_specs=in_vmem,
        scratch_shapes=[
            pltpu.VMEM((steps, tok_rows, width), jnp.bfloat16),
            pltpu.VMEM(context_kv.shape, jnp.bfloat16),
            pltpu.SemaphoreType.DMA((steps, chunks)),
            pltpu.SemaphoreType.DMA,
        ],
        compiler_params=params,
    )(*(pltpu.with_memory_space_constraint(x, pltpu.HBM) for x in (qkv_all, context_kv)))
    got = exchange(sent, first)
    mixed = pl.pallas_call(
        functools.partial(
            attend_kernel, steps, heads, tok_rows, ctx_rows, head_dim, scale, came_from, goes_to
        ),
        out_shape=jax.ShapeDtypeStruct((peers, tok_rows, steps * heads * head_dim), jnp.bfloat16),
        in_specs=[in_vmem],
        out_specs=in_vmem,
        compiler_params=params,
    )(got)
    back = exchange(mixed, second)
    back = back.reshape(groups, tok_rows, steps, heads * head_dim).transpose(2, 1, 0, 3)
    return back.reshape(steps, 1, tok_rows, HEADS * head_dim)


def shards_copied(qkv_all, context_kv, sections, groups, copies, heads, scale):
    steps, _, tok_rows, width = qkv_all.shape
    head_dim = width // (3 * HEADS)
    peers = groups * copies
    share = tok_rows // copies
    ctx_rows = context_kv.shape[0]
    frames = qkv_all[:, 0].reshape(steps, tok_rows, groups, heads, 3, head_dim)
    queries = frames[..., 0, :].reshape(steps, copies, share, groups, heads, head_dim)
    queries = queries.transpose(3, 1, 0, 4, 2, 5).reshape(peers, -1, head_dim)
    key_vals = frames[..., 1:, :].transpose(2, 0, 3, 4, 1, 5).reshape(groups, -1, head_dim)
    ctx = context_kv.reshape(ctx_rows, groups, heads, 2, head_dim)
    ctx = ctx.transpose(1, 2, 3, 0, 4).reshape(groups, -1, head_dim)
    shared = jnp.concatenate([key_vals, ctx], axis=1)
    shared = jnp.broadcast_to(shared[:, None], (groups, copies) + shared.shape[1:])
    shared = shared.reshape((peers,) + shared.shape[2:])
    sent = jnp.concatenate([queries, shared], axis=1)
    got = lax.all_to_all(sent, AXES, split_axis=0, concat_axis=0, tiled=True)
    per_section = peers // sections
    cut = steps * heads * share
    end = cut + steps * heads * 2 * tok_rows
    q = got[:, :cut].reshape(per_section, sections, steps, heads, share, head_dim)
    q = q.transpose(2, 1, 3, 0, 4, 5).reshape(steps, sections, heads, -1, head_dim)
    kv = got[:, cut:end].reshape(per_section, sections, steps, heads, 2, tok_rows, head_dim)
    kv = kv.transpose(2, 1, 4, 3, 0, 5, 6).reshape(steps, sections, 2, heads, -1, head_dim)
    ctx = got[:, end:].reshape(peers, heads, 2, ctx_rows, head_dim)
    earlier = [ctx.transpose(2, 1, 0, 3, 4).reshape(2, heads, -1, head_dim)]
    results = []
    for step in range(steps):
        for s in range(sections):
            keys, vals = jnp.concatenate(earlier + [kv[step, s]], axis=2)
            results.append(
                jnp.stack([softmax_mix(q[step, s, h], keys[h], vals[h], scale) for h in range(heads)])
            )
        earlier = earlier + [kv[step, sections - 1]]
    mixed = jnp.stack(results).reshape(steps, sections, heads, per_section, share, head_dim)
    mixed = mixed.transpose(3, 1, 0, 2, 4, 5).reshape(peers, -1, head_dim)
    back = lax.all_to_all(mixed, AXES, split_axis=0, concat_axis=0, tiled=True)
    back = back.reshape(groups, copies, steps, heads, share, head_dim)
    back = back.transpose(2, 1, 4, 0, 3, 5)
    return back.reshape(steps, 1, tok_rows, HEADS * head_dim)


def solution(mesh):
    in_specs = (P(None, "section", ("rep", "seq"), None), P(("rep", "section", "seq"), None))
    out_specs = P(None, "section", ("rep", "seq"), None)
    return jax.shard_map(shards, mesh=mesh, in_specs=in_specs, out_specs=out_specs, check_vma=False)
```

```python
import functools
import math

import jax
import jax.numpy as jnp
from jax import lax
from jax.experimental import pallas as pl
from jax.experimental.pallas import tpu as pltpu
from jax.sharding import PartitionSpec as P

HEADS = 32
AXES = ("seq", "section")


def softmax_mix(queries, keys, values, scale):
    scores = (
        lax.dot_general(
            queries, keys, (((1,), (1,)), ((), ())), preferred_element_type=jnp.float32
        )
        * scale
    )
    weights = jnp.exp(scores - jnp.max(scores, axis=1, keepdims=True))
    total = jnp.sum(weights, axis=1, keepdims=True)
    mixed = jnp.dot(weights.astype(jnp.bfloat16), values, preferred_element_type=jnp.float32)
    return (mixed / total).astype(jnp.bfloat16)


def attend_kernel(
    steps, heads, tok_rows, ctx_rows, head_dim, scale, came_from, goes_to, got_ref, out_ref
):
    sections = len(came_from)
    sources = got_ref.shape[0]
    ctx_base = steps * heads * 3 * head_dim
    log2_scale = scale * math.log2(math.e)

    def part(step, section, head, role):
        base = ((step * heads + head) * 3 + role) * head_dim
        return jnp.concatenate(
            [got_ref[p, :, base : base + head_dim] for p in came_from[section]], axis=0
        )

    def context(head, role):
        base = ctx_base + role * head_dim
        rows = slice(head * ctx_rows, (head + 1) * ctx_rows)
        return got_ref[:, rows, base : base + head_dim].reshape(sources * ctx_rows, head_dim)

    tasks = []
    for head in range(heads):
        earlier = [(context(head, 0), context(head, 1))]
        for step in range(steps):
            own = [(part(step, s, head, 1), part(step, s, head, 2)) for s in range(sections)]
            for s in range(sections):
                pairs = earlier + [own[s]]
                keys = jnp.concatenate([k for k, _ in pairs], axis=0)
                vals = jnp.concatenate([v for _, v in pairs], axis=0)
                tasks.append((step, s, head, part(step, s, head, 0), keys, vals))
            earlier = earlier + [own[sections - 1]]
    all_scores = [
        lax.dot_general(q, k, (((1,), (1,)), ((), ())), preferred_element_type=jnp.float32)
        for _, _, _, q, k, _ in tasks
    ]
    all_tops = [jnp.max(scores, axis=1, keepdims=True) for scores in all_scores]
    all_weights = [
        jnp.exp2((scores - top) * log2_scale).astype(jnp.bfloat16)
        for scores, top in zip(all_scores, all_tops)
    ]
    all_mixed = [
        jnp.dot(
            weights,
            jnp.concatenate([vals, jnp.ones_like(vals)], axis=1),
            preferred_element_type=jnp.float32,
        )
        for weights, (_, _, _, _, _, vals) in zip(all_weights, tasks)
    ]
    for mixed, (step, s, head, _, _, _) in zip(all_mixed, tasks):
        done = (mixed[:, :head_dim] / mixed[:, head_dim:]).astype(jnp.bfloat16)
        base = (step * heads + head) * head_dim
        for slot, p in enumerate(goes_to[s]):
            out_ref[p, :, base : base + head_dim] = done[slot * tok_rows : (slot + 1) * tok_rows]


def pack_kernel(
    steps, block_of, heads, ctx_rows, head_dim, chunks, qkv_hbm, ctx_hbm, out_ref, qkv_ref, ctx_ref, sems, ctx_sem
):
    groups = len(block_of)
    width = heads * 3 * head_dim
    span = groups // chunks
    ctx_copy = pltpu.make_async_copy(ctx_hbm, ctx_ref, ctx_sem)
    copies = []
    for step in range(steps):
        for chunk in range(chunks):
            columns = pl.ds(chunk * span * width, span * width)
            copies.append(
                pltpu.make_async_copy(
                    qkv_hbm.at[step, 0, :, columns],
                    qkv_ref.at[step, :, columns],
                    sems.at[step, chunk],
                )
            )
    ctx_copy.start()
    for copy in copies:
        copy.start()
    base = steps * width
    ctx_copy.wait()
    for group in range(groups):
        for role in range(2):
            columns = [((group * heads + head) * 2 + role) * head_dim for head in range(heads)]
            block = [ctx_ref[:, c : c + head_dim] for c in columns]
            out_ref[block_of[group], :, base + role * head_dim : base + (role + 1) * head_dim] = (
                jnp.concatenate(block, axis=0)
            )
    for step in range(steps):
        for chunk in range(chunks):
            copies[step * chunks + chunk].wait()
            for group in range(chunk * span, (chunk + 1) * span):
                out_ref[block_of[group], :, step * width : (step + 1) * width] = qkv_ref[
                    step, :, group * width : (group + 1) * width
                ]


def exchange(blocks, order):
    return lax.all_to_all(
        blocks, AXES, split_axis=0, concat_axis=0, axis_index_groups=[order], tiled=True
    )


def send_orders(sections, per_section):
    peers = sections * per_section
    quarter = math.gcd(peers, 4)
    row = peers // quarter
    half = quarter // 2
    rows = list(range(half, quarter)) + list(range(half))
    across = rows[::half] + rows[1::half] if quarter == 4 else rows
    first = [z * row + i for z in across for i in range(row - 1, -1, -1)]
    second = [z * row + i for z in rows for i in range(row - 1, -1, -1)]
    return first, second


def shards(qkv_all, context_kv):
    sections = lax.axis_size("section")
    peers = sections * lax.axis_size("seq")
    groups = min(peers, HEADS)
    copies = peers // groups
    heads = HEADS // groups
    steps, _, tok_rows, width = qkv_all.shape
    head_dim = width // (3 * HEADS)
    ctx_rows = context_kv.shape[0]
    scale = head_dim ** (-0.5)
    if copies > 1 or heads * ctx_rows != tok_rows:
        return shards_copied(qkv_all, context_kv, sections, groups, copies, heads, scale)

    chunks = math.gcd(groups, 2)
    per_section = peers // sections
    first, second = send_orders(sections, per_section)
    devices = range(sections * per_section)
    block_of = [first.index(second[group]) for group in range(groups)]
    came_from = [[first.index(d) for d in devices if d % sections == s] for s in range(sections)]
    goes_to = [[second.index(d) for d in devices if d % sections == s] for s in range(sections)]
    in_vmem = pl.BlockSpec(memory_space=pltpu.VMEM)
    params = pltpu.CompilerParams(vmem_limit_bytes=32 * 1024 * 1024)
    sent = pl.pallas_call(
        functools.partial(pack_kernel, steps, block_of, heads, ctx_rows, head_dim, chunks),
        out_shape=jax.ShapeDtypeStruct(
            (groups, tok_rows, (steps * heads * 3 + 2) * head_dim), jnp.bfloat16
        ),
        in_specs=[pl.BlockSpec(memory_space=pltpu.HBM)] * 2,
        out_specs=in_vmem,
        scratch_shapes=[
            pltpu.VMEM((steps, tok_rows, width), jnp.bfloat16),
            pltpu.VMEM(context_kv.shape, jnp.bfloat16),
            pltpu.SemaphoreType.DMA((steps, chunks)),
            pltpu.SemaphoreType.DMA,
        ],
        compiler_params=params,
    )(*(pltpu.with_memory_space_constraint(x, pltpu.HBM) for x in (qkv_all, context_kv)))
    got = exchange(sent, first)
    mixed = pl.pallas_call(
        functools.partial(
            attend_kernel, steps, heads, tok_rows, ctx_rows, head_dim, scale, came_from, goes_to
        ),
        out_shape=jax.ShapeDtypeStruct((peers, tok_rows, steps * heads * head_dim), jnp.bfloat16),
        in_specs=[in_vmem],
        out_specs=in_vmem,
        compiler_params=params,
    )(got)
    back = exchange(mixed, second)
    back = back.reshape(groups, tok_rows, steps, heads * head_dim).transpose(2, 1, 0, 3)
    return back.reshape(steps, 1, tok_rows, HEADS * head_dim)


def shards_copied(qkv_all, context_kv, sections, groups, copies, heads, scale):
    steps, _, tok_rows, width = qkv_all.shape
    head_dim = width // (3 * HEADS)
    peers = groups * copies
    share = tok_rows // copies
    ctx_rows = context_kv.shape[0]
    frames = qkv_all[:, 0].reshape(steps, tok_rows, groups, heads, 3, head_dim)
    queries = frames[..., 0, :].reshape(steps, copies, share, groups, heads, head_dim)
    queries = queries.transpose(3, 1, 0, 4, 2, 5).reshape(peers, -1, head_dim)
    key_vals = frames[..., 1:, :].transpose(2, 0, 3, 4, 1, 5).reshape(groups, -1, head_dim)
    ctx = context_kv.reshape(ctx_rows, groups, heads, 2, head_dim)
    ctx = ctx.transpose(1, 2, 3, 0, 4).reshape(groups, -1, head_dim)
    shared = jnp.concatenate([key_vals, ctx], axis=1)
    shared = jnp.broadcast_to(shared[:, None], (groups, copies) + shared.shape[1:])
    shared = shared.reshape((peers,) + shared.shape[2:])
    sent = jnp.concatenate([queries, shared], axis=1)
    got = lax.all_to_all(sent, AXES, split_axis=0, concat_axis=0, tiled=True)
    per_section = peers // sections
    cut = steps * heads * share
    end = cut + steps * heads * 2 * tok_rows
    q = got[:, :cut].reshape(per_section, sections, steps, heads, share, head_dim)
    q = q.transpose(2, 1, 3, 0, 4, 5).reshape(steps, sections, heads, -1, head_dim)
    kv = got[:, cut:end].reshape(per_section, sections, steps, heads, 2, tok_rows, head_dim)
    kv = kv.transpose(2, 1, 4, 3, 0, 5, 6).reshape(steps, sections, 2, heads, -1, head_dim)
    ctx = got[:, end:].reshape(peers, heads, 2, ctx_rows, head_dim)
    earlier = [ctx.transpose(2, 1, 0, 3, 4).reshape(2, heads, -1, head_dim)]
    results = []
    for step in range(steps):
        for s in range(sections):
            keys, vals = jnp.concatenate(earlier + [kv[step, s]], axis=2)
            results.append(
                jnp.stack([softmax_mix(q[step, s, h], keys[h], vals[h], scale) for h in range(heads)])
            )
        earlier = earlier + [kv[step, sections - 1]]
    mixed = jnp.stack(results).reshape(steps, sections, heads, per_section, share, head_dim)
    mixed = mixed.transpose(3, 1, 0, 2, 4, 5).reshape(peers, -1, head_dim)
    back = lax.all_to_all(mixed, AXES, split_axis=0, concat_axis=0, tiled=True)
    back = back.reshape(groups, copies, steps, heads, share, head_dim)
    back = back.transpose(2, 1, 4, 0, 3, 5)
    return back.reshape(steps, 1, tok_rows, HEADS * head_dim)


def solution(mesh):
    in_specs = (P(None, "section", ("rep", "seq"), None), P(("rep", "section", "seq"), None))
    out_specs = P(None, "section", ("rep", "seq"), None)
    return jax.shard_map(shards, mesh=mesh, in_specs=in_specs, out_specs=out_specs, check_vma=False)
```

```python
import functools
import math

import jax
import jax.numpy as jnp
from jax import lax
from jax.experimental import pallas as pl
from jax.experimental.pallas import tpu as pltpu
from jax.sharding import PartitionSpec as P

HEADS = 32
AXES = ("seq", "section")


def softmax_mix(queries, keys, values, scale):
    scores = (
        lax.dot_general(
            queries, keys, (((1,), (1,)), ((), ())), preferred_element_type=jnp.float32
        )
        * scale
    )
    weights = jnp.exp(scores - jnp.max(scores, axis=1, keepdims=True))
    total = jnp.sum(weights, axis=1, keepdims=True)
    mixed = jnp.dot(weights.astype(jnp.bfloat16), values, preferred_element_type=jnp.float32)
    return (mixed / total).astype(jnp.bfloat16)


def attend_kernel(
    steps, heads, tok_rows, ctx_rows, head_dim, scale, came_from, goes_to, got_ref, out_ref
):
    sections = len(came_from)
    sources = got_ref.shape[0]
    ctx_base = steps * heads * 3 * head_dim
    log2_scale = scale * math.log2(math.e)

    def part(step, section, head, role):
        base = ((step * heads + head) * 3 + role) * head_dim
        return jnp.concatenate(
            [got_ref[p, :, base : base + head_dim] for p in came_from[section]], axis=0
        )

    def context(head, role):
        base = ctx_base + role * head_dim
        rows = slice(head * ctx_rows, (head + 1) * ctx_rows)
        return got_ref[:, rows, base : base + head_dim].reshape(sources * ctx_rows, head_dim)

    tasks = []
    for head in range(heads):
        earlier = [(context(head, 0), context(head, 1))]
        for step in range(steps):
            own = [(part(step, s, head, 1), part(step, s, head, 2)) for s in range(sections)]
            for s in range(sections):
                pairs = earlier + [own[s]]
                keys = jnp.concatenate([k for k, _ in pairs], axis=0)
                vals = jnp.concatenate([v for _, v in pairs], axis=0)
                tasks.append((step, s, head, part(step, s, head, 0), keys, vals))
            earlier = earlier + [own[sections - 1]]
    all_scores = [
        lax.dot_general(q, k, (((1,), (1,)), ((), ())), preferred_element_type=jnp.float32)
        for _, _, _, q, k, _ in tasks
    ]
    all_tops = [jnp.max(scores, axis=1, keepdims=True) for scores in all_scores]
    all_weights = [
        jnp.exp2((scores - top) * log2_scale).astype(jnp.bfloat16)
        for scores, top in zip(all_scores, all_tops)
    ]
    all_mixed = [
        jnp.dot(
            weights,
            jnp.concatenate([vals, jnp.ones_like(vals)], axis=1),
            preferred_element_type=jnp.float32,
        )
        for weights, (_, _, _, _, _, vals) in zip(all_weights, tasks)
    ]
    for mixed, (step, s, head, _, _, _) in zip(all_mixed, tasks):
        done = (mixed[:, :head_dim] / mixed[:, head_dim:]).astype(jnp.bfloat16)
        base = (step * heads + head) * head_dim
        for slot, p in enumerate(goes_to[s]):
            out_ref[p, :, base : base + head_dim] = done[slot * tok_rows : (slot + 1) * tok_rows]


def pack_kernel(
    steps, block_of, heads, ctx_rows, head_dim, chunks, qkv_hbm, ctx_hbm, out_ref, qkv_ref, ctx_ref, sems, ctx_sem
):
    groups = len(block_of)
    width = heads * 3 * head_dim
    span = groups // chunks
    ctx_copy = pltpu.make_async_copy(ctx_hbm, ctx_ref, ctx_sem)
    copies = []
    for step in range(steps):
        for chunk in range(chunks):
            columns = pl.ds(chunk * span * width, span * width)
            copies.append(
                pltpu.make_async_copy(
                    qkv_hbm.at[step, 0, :, columns],
                    qkv_ref.at[step, :, columns],
                    sems.at[step, chunk],
                )
            )
    ctx_copy.start()
    for copy in copies:
        copy.start()
    base = steps * width
    ctx_copy.wait()
    for group in range(groups):
        for role in range(2):
            columns = [((group * heads + head) * 2 + role) * head_dim for head in range(heads)]
            block = [ctx_ref[:, c : c + head_dim] for c in columns]
            out_ref[block_of[group], :, base + role * head_dim : base + (role + 1) * head_dim] = (
                jnp.concatenate(block, axis=0)
            )
    for step in range(steps):
        for chunk in range(chunks):
            copies[step * chunks + chunk].wait()
            for group in range(chunk * span, (chunk + 1) * span):
                out_ref[block_of[group], :, step * width : (step + 1) * width] = qkv_ref[
                    step, :, group * width : (group + 1) * width
                ]


def exchange(blocks, order):
    return lax.all_to_all(
        blocks, AXES, split_axis=0, concat_axis=0, axis_index_groups=[order], tiled=True
    )


def send_orders(sections, per_section):
    peers = sections * per_section
    quarter = math.gcd(peers, 4)
    row = peers // quarter
    half = quarter // 2
    rows = list(range(half, quarter)) + list(range(half))
    across = [half, half - 1, quarter - 1, 0] if quarter == 4 else rows
    first = [z * row + i for z in across for i in range(row - 1, -1, -1)]
    second = [z * row + i for z in rows for i in range(row - 1, -1, -1)]
    return first, second


def shards(qkv_all, context_kv):
    sections = lax.axis_size("section")
    peers = sections * lax.axis_size("seq")
    groups = min(peers, HEADS)
    copies = peers // groups
    heads = HEADS // groups
    steps, _, tok_rows, width = qkv_all.shape
    head_dim = width // (3 * HEADS)
    ctx_rows = context_kv.shape[0]
    scale = head_dim ** (-0.5)
    if copies > 1 or heads * ctx_rows != tok_rows:
        return shards_copied(qkv_all, context_kv, sections, groups, copies, heads, scale)

    chunks = math.gcd(groups, 2)
    per_section = peers // sections
    first, second = send_orders(sections, per_section)
    devices = range(sections * per_section)
    block_of = [first.index(second[group]) for group in range(groups)]
    came_from = [[first.index(d) for d in devices if d % sections == s] for s in range(sections)]
    goes_to = [[second.index(d) for d in devices if d % sections == s] for s in range(sections)]
    in_vmem = pl.BlockSpec(memory_space=pltpu.VMEM)
    params = pltpu.CompilerParams(vmem_limit_bytes=32 * 1024 * 1024)
    sent = pl.pallas_call(
        functools.partial(pack_kernel, steps, block_of, heads, ctx_rows, head_dim, chunks),
        out_shape=jax.ShapeDtypeStruct(
            (groups, tok_rows, (steps * heads * 3 + 2) * head_dim), jnp.bfloat16
        ),
        in_specs=[pl.BlockSpec(memory_space=pltpu.HBM)] * 2,
        out_specs=in_vmem,
        scratch_shapes=[
            pltpu.VMEM((steps, tok_rows, width), jnp.bfloat16),
            pltpu.VMEM(context_kv.shape, jnp.bfloat16),
            pltpu.SemaphoreType.DMA((steps, chunks)),
            pltpu.SemaphoreType.DMA,
        ],
        compiler_params=params,
    )(*(pltpu.with_memory_space_constraint(x, pltpu.HBM) for x in (qkv_all, context_kv)))
    got = exchange(sent, first)
    mixed = pl.pallas_call(
        functools.partial(
            attend_kernel, steps, heads, tok_rows, ctx_rows, head_dim, scale, came_from, goes_to
        ),
        out_shape=jax.ShapeDtypeStruct((peers, tok_rows, steps * heads * head_dim), jnp.bfloat16),
        in_specs=[in_vmem],
        out_specs=in_vmem,
        compiler_params=params,
    )(got)
    back = exchange(mixed, second)
    back = back.reshape(groups, tok_rows, steps, heads * head_dim).transpose(2, 1, 0, 3)
    return back.reshape(steps, 1, tok_rows, HEADS * head_dim)


def shards_copied(qkv_all, context_kv, sections, groups, copies, heads, scale):
    steps, _, tok_rows, width = qkv_all.shape
    head_dim = width // (3 * HEADS)
    peers = groups * copies
    share = tok_rows // copies
    ctx_rows = context_kv.shape[0]
    frames = qkv_all[:, 0].reshape(steps, tok_rows, groups, heads, 3, head_dim)
    queries = frames[..., 0, :].reshape(steps, copies, share, groups, heads, head_dim)
    queries = queries.transpose(3, 1, 0, 4, 2, 5).reshape(peers, -1, head_dim)
    key_vals = frames[..., 1:, :].transpose(2, 0, 3, 4, 1, 5).reshape(groups, -1, head_dim)
    ctx = context_kv.reshape(ctx_rows, groups, heads, 2, head_dim)
    ctx = ctx.transpose(1, 2, 3, 0, 4).reshape(groups, -1, head_dim)
    shared = jnp.concatenate([key_vals, ctx], axis=1)
    shared = jnp.broadcast_to(shared[:, None], (groups, copies) + shared.shape[1:])
    shared = shared.reshape((peers,) + shared.shape[2:])
    sent = jnp.concatenate([queries, shared], axis=1)
    got = lax.all_to_all(sent, AXES, split_axis=0, concat_axis=0, tiled=True)
    per_section = peers // sections
    cut = steps * heads * share
    end = cut + steps * heads * 2 * tok_rows
    q = got[:, :cut].reshape(per_section, sections, steps, heads, share, head_dim)
    q = q.transpose(2, 1, 3, 0, 4, 5).reshape(steps, sections, heads, -1, head_dim)
    kv = got[:, cut:end].reshape(per_section, sections, steps, heads, 2, tok_rows, head_dim)
    kv = kv.transpose(2, 1, 4, 3, 0, 5, 6).reshape(steps, sections, 2, heads, -1, head_dim)
    ctx = got[:, end:].reshape(peers, heads, 2, ctx_rows, head_dim)
    earlier = [ctx.transpose(2, 1, 0, 3, 4).reshape(2, heads, -1, head_dim)]
    results = []
    for step in range(steps):
        for s in range(sections):
            keys, vals = jnp.concatenate(earlier + [kv[step, s]], axis=2)
            results.append(
                jnp.stack([softmax_mix(q[step, s, h], keys[h], vals[h], scale) for h in range(heads)])
            )
        earlier = earlier + [kv[step, sections - 1]]
    mixed = jnp.stack(results).reshape(steps, sections, heads, per_section, share, head_dim)
    mixed = mixed.transpose(3, 1, 0, 2, 4, 5).reshape(peers, -1, head_dim)
    back = lax.all_to_all(mixed, AXES, split_axis=0, concat_axis=0, tiled=True)
    back = back.reshape(groups, copies, steps, heads, share, head_dim)
    back = back.transpose(2, 1, 4, 0, 3, 5)
    return back.reshape(steps, 1, tok_rows, HEADS * head_dim)


def solution(mesh):
    in_specs = (P(None, "section", ("rep", "seq"), None), P(("rep", "section", "seq"), None))
    out_specs = P(None, "section", ("rep", "seq"), None)
    return jax.shard_map(shards, mesh=mesh, in_specs=in_specs, out_specs=out_specs, check_vma=False)
```

```python
import functools
import math

import jax
import jax.numpy as jnp
from jax import lax
from jax.experimental import pallas as pl
from jax.experimental.pallas import tpu as pltpu
from jax.sharding import PartitionSpec as P

HEADS = 32
AXES = ("seq", "section")


def softmax_mix(queries, keys, values, scale):
    scores = (
        lax.dot_general(
            queries, keys, (((1,), (1,)), ((), ())), preferred_element_type=jnp.float32
        )
        * scale
    )
    weights = jnp.exp(scores - jnp.max(scores, axis=1, keepdims=True))
    total = jnp.sum(weights, axis=1, keepdims=True)
    mixed = jnp.dot(weights.astype(jnp.bfloat16), values, preferred_element_type=jnp.float32)
    return (mixed / total).astype(jnp.bfloat16)


def attend_kernel(
    steps, heads, tok_rows, ctx_rows, head_dim, scale, came_from, goes_to, got_ref, out_ref
):
    sections = len(came_from)
    sources = got_ref.shape[0]
    ctx_base = steps * heads * 3 * head_dim
    log2_scale = scale * math.log2(math.e)

    def part(step, section, head, role):
        base = ((step * heads + head) * 3 + role) * head_dim
        return jnp.concatenate(
            [got_ref[p, :, base : base + head_dim] for p in came_from[section]], axis=0
        )

    def context(head, role):
        base = ctx_base + role * head_dim
        rows = slice(head * ctx_rows, (head + 1) * ctx_rows)
        return got_ref[:, rows, base : base + head_dim].reshape(sources * ctx_rows, head_dim)

    def with_ones(vals):
        return jnp.concatenate([vals, jnp.ones_like(vals)], axis=1)

    def product(left, right):
        return lax.dot_general(
            left, right, (((1,), (1,)), ((), ())), preferred_element_type=jnp.float32
        )

    last = sections - 1
    ctx_tokens = sources * ctx_rows
    tokens = len(came_from[0]) * tok_rows
    blocks = [(step, s) for step in range(steps) for s in range(sections)]
    shared = [s == last and step + 1 < steps for step, s in blocks]
    allowed = [
        ctx_tokens + (step + is_shared) * tokens
        for (step, _), is_shared in zip(blocks, shared)
    ]
    every_task = []
    for head in range(heads):
        earlier = [(step, last, head) for step in range(steps - 1)]
        keys = jnp.concatenate([context(head, 0)] + [part(*e, 1) for e in earlier], axis=0)
        vals = jnp.concatenate([context(head, 1)] + [part(*e, 2) for e in earlier], axis=0)
        queries = [part(step, s, head, 0) for step, s in blocks]
        scores = product(jnp.concatenate(queries, axis=0), keys)
        lane = lax.broadcasted_iota(jnp.int32, (tokens, keys.shape[0]), 1)
        tasks = []
        for i, (step, s) in enumerate(blocks):
            common = scores[i * tokens : (i + 1) * tokens]
            if allowed[i] < keys.shape[0]:
                common = jnp.where(lane < allowed[i], common, -jnp.inf)
            own = None if shared[i] else product(queries[i], part(step, s, head, 1))
            tasks.append((common, own))
        every_task.append((tasks, vals))
    every_weight = []
    for tasks, _ in every_task:
        weights = []
        for common, own in tasks:
            top = jnp.max(common, axis=1, keepdims=True)
            if own is not None:
                top = jnp.maximum(top, jnp.max(own, axis=1, keepdims=True))
            weights.append(
                [
                    None if x is None else jnp.exp2((x - top) * log2_scale).astype(jnp.bfloat16)
                    for x in (common, own)
                ]
            )
        every_weight.append(weights)
    for head, (weights, (_, vals)) in enumerate(zip(every_weight, every_task)):
        mixed_all = jnp.dot(
            jnp.concatenate([common for common, _ in weights], axis=0),
            with_ones(vals),
            preferred_element_type=jnp.float32,
        )
        for i, (step, s) in enumerate(blocks):
            mixed = mixed_all[i * tokens : (i + 1) * tokens]
            if not shared[i]:
                mixed = mixed + jnp.dot(
                    weights[i][1],
                    with_ones(part(step, s, head, 2)),
                    preferred_element_type=jnp.float32,
                )
            done = (mixed[:, :head_dim] / mixed[:, head_dim:]).astype(jnp.bfloat16)
            base = (step * heads + head) * head_dim
            for slot, p in enumerate(goes_to[s]):
                out_ref[p, :, base : base + head_dim] = done[slot * tok_rows : (slot + 1) * tok_rows]


def pack_kernel(
    steps, block_of, heads, ctx_rows, head_dim, chunks, qkv_hbm, ctx_hbm, out_ref, qkv_ref, ctx_ref, sems, ctx_sem
):
    groups = len(block_of)
    width = heads * 3 * head_dim
    span = groups // chunks
    ctx_copy = pltpu.make_async_copy(ctx_hbm, ctx_ref, ctx_sem)
    copies = []
    for step in range(steps):
        for chunk in range(chunks):
            columns = pl.ds(chunk * span * width, span * width)
            copies.append(
                pltpu.make_async_copy(
                    qkv_hbm.at[step, 0, :, columns],
                    qkv_ref.at[step, :, columns],
                    sems.at[step, chunk],
                )
            )
    ctx_copy.start()
    for copy in copies:
        copy.start()
    base = steps * width
    ctx_copy.wait()
    for group in range(groups):
        for role in range(2):
            columns = [((group * heads + head) * 2 + role) * head_dim for head in range(heads)]
            block = [ctx_ref[:, c : c + head_dim] for c in columns]
            out_ref[block_of[group], :, base + role * head_dim : base + (role + 1) * head_dim] = (
                jnp.concatenate(block, axis=0)
            )
    for step in range(steps):
        for chunk in range(chunks):
            copies[step * chunks + chunk].wait()
            for group in range(chunk * span, (chunk + 1) * span):
                out_ref[block_of[group], :, step * width : (step + 1) * width] = qkv_ref[
                    step, :, group * width : (group + 1) * width
                ]


def exchange(blocks, order):
    return lax.all_to_all(
        blocks, AXES, split_axis=0, concat_axis=0, axis_index_groups=[order], tiled=True
    )


def send_orders(sections, per_section):
    peers = sections * per_section
    quarter = math.gcd(peers, 4)
    row = peers // quarter
    turned = [z * row + i for z in range(quarter - 1, -1, -1) for i in range(row - 1, -1, -1)]
    first = turned[row:] + turned[:row]
    half = quarter // 2
    rows = list(range(half, quarter)) + list(range(half))
    second = [z * row + i for z in rows for i in range(row - 1, -1, -1)]
    return first, second


def shards(qkv_all, context_kv):
    sections = lax.axis_size("section")
    peers = sections * lax.axis_size("seq")
    groups = min(peers, HEADS)
    copies = peers // groups
    heads = HEADS // groups
    steps, _, tok_rows, width = qkv_all.shape
    head_dim = width // (3 * HEADS)
    ctx_rows = context_kv.shape[0]
    scale = head_dim ** (-0.5)
    if copies > 1 or heads * ctx_rows != tok_rows:
        return shards_copied(qkv_all, context_kv, sections, groups, copies, heads, scale)

    chunks = 1
    per_section = peers // sections
    first, second = send_orders(sections, per_section)
    devices = range(sections * per_section)
    block_of = [first.index(second[group]) for group in range(groups)]
    came_from = [[first.index(d) for d in devices if d % sections == s] for s in range(sections)]
    goes_to = [[second.index(d) for d in devices if d % sections == s] for s in range(sections)]
    in_vmem = pl.BlockSpec(memory_space=pltpu.VMEM)
    params = pltpu.CompilerParams(vmem_limit_bytes=32 * 1024 * 1024)
    sent = pl.pallas_call(
        functools.partial(pack_kernel, steps, block_of, heads, ctx_rows, head_dim, chunks),
        out_shape=jax.ShapeDtypeStruct(
            (groups, tok_rows, (steps * heads * 3 + 2) * head_dim), jnp.bfloat16
        ),
        in_specs=[pl.BlockSpec(memory_space=pltpu.HBM)] * 2,
        out_specs=in_vmem,
        scratch_shapes=[
            pltpu.VMEM((steps, tok_rows, width), jnp.bfloat16),
            pltpu.VMEM(context_kv.shape, jnp.bfloat16),
            pltpu.SemaphoreType.DMA((steps, chunks)),
            pltpu.SemaphoreType.DMA,
        ],
        compiler_params=params,
    )(*(pltpu.with_memory_space_constraint(x, pltpu.HBM) for x in (qkv_all, context_kv)))
    got = exchange(sent, first)
    mixed = pl.pallas_call(
        functools.partial(
            attend_kernel, steps, heads, tok_rows, ctx_rows, head_dim, scale, came_from, goes_to
        ),
        out_shape=jax.ShapeDtypeStruct((peers, tok_rows, steps * heads * head_dim), jnp.bfloat16),
        in_specs=[in_vmem],
        out_specs=in_vmem,
        compiler_params=params,
    )(got)
    back = exchange(mixed, second)
    back = back.reshape(groups, tok_rows, steps, heads * head_dim).transpose(2, 1, 0, 3)
    return back.reshape(steps, 1, tok_rows, HEADS * head_dim)


def shards_copied(qkv_all, context_kv, sections, groups, copies, heads, scale):
    steps, _, tok_rows, width = qkv_all.shape
    head_dim = width // (3 * HEADS)
    peers = groups * copies
    share = tok_rows // copies
    ctx_rows = context_kv.shape[0]
    frames = qkv_all[:, 0].reshape(steps, tok_rows, groups, heads, 3, head_dim)
    queries = frames[..., 0, :].reshape(steps, copies, share, groups, heads, head_dim)
    queries = queries.transpose(3, 1, 0, 4, 2, 5).reshape(peers, -1, head_dim)
    key_vals = frames[..., 1:, :].transpose(2, 0, 3, 4, 1, 5).reshape(groups, -1, head_dim)
    ctx = context_kv.reshape(ctx_rows, groups, heads, 2, head_dim)
    ctx = ctx.transpose(1, 2, 3, 0, 4).reshape(groups, -1, head_dim)
    shared = jnp.concatenate([key_vals, ctx], axis=1)
    shared = jnp.broadcast_to(shared[:, None], (groups, copies) + shared.shape[1:])
    shared = shared.reshape((peers,) + shared.shape[2:])
    sent = jnp.concatenate([queries, shared], axis=1)
    got = lax.all_to_all(sent, AXES, split_axis=0, concat_axis=0, tiled=True)
    per_section = peers // sections
    cut = steps * heads * share
    end = cut + steps * heads * 2 * tok_rows
    q = got[:, :cut].reshape(per_section, sections, steps, heads, share, head_dim)
    q = q.transpose(2, 1, 3, 0, 4, 5).reshape(steps, sections, heads, -1, head_dim)
    kv = got[:, cut:end].reshape(per_section, sections, steps, heads, 2, tok_rows, head_dim)
    kv = kv.transpose(2, 1, 4, 3, 0, 5, 6).reshape(steps, sections, 2, heads, -1, head_dim)
    ctx = got[:, end:].reshape(peers, heads, 2, ctx_rows, head_dim)
    earlier = [ctx.transpose(2, 1, 0, 3, 4).reshape(2, heads, -1, head_dim)]
    results = []
    for step in range(steps):
        for s in range(sections):
            keys, vals = jnp.concatenate(earlier + [kv[step, s]], axis=2)
            results.append(
                jnp.stack([softmax_mix(q[step, s, h], keys[h], vals[h], scale) for h in range(heads)])
            )
        earlier = earlier + [kv[step, sections - 1]]
    mixed = jnp.stack(results).reshape(steps, sections, heads, per_section, share, head_dim)
    mixed = mixed.transpose(3, 1, 0, 2, 4, 5).reshape(peers, -1, head_dim)
    back = lax.all_to_all(mixed, AXES, split_axis=0, concat_axis=0, tiled=True)
    back = back.reshape(groups, copies, steps, heads, share, head_dim)
    back = back.transpose(2, 1, 4, 0, 3, 5)
    return back.reshape(steps, 1, tok_rows, HEADS * head_dim)


def solution(mesh):
    in_specs = (P(None, "section", ("rep", "seq"), None), P(("rep", "section", "seq"), None))
    out_specs = P(None, "section", ("rep", "seq"), None)
    return jax.shard_map(shards, mesh=mesh, in_specs=in_specs, out_specs=out_specs, check_vma=False)
```

```python
import functools
import math

import jax
import jax.numpy as jnp
from jax import lax
from jax.experimental import pallas as pl
from jax.experimental.pallas import tpu as pltpu
from jax.sharding import PartitionSpec as P

HEADS = 32
AXES = ("seq", "section")


def softmax_mix(queries, keys, values, scale):
    scores = (
        lax.dot_general(
            queries, keys, (((1,), (1,)), ((), ())), preferred_element_type=jnp.float32
        )
        * scale
    )
    weights = jnp.exp(scores - jnp.max(scores, axis=1, keepdims=True))
    total = jnp.sum(weights, axis=1, keepdims=True)
    mixed = jnp.dot(weights.astype(jnp.bfloat16), values, preferred_element_type=jnp.float32)
    return (mixed / total).astype(jnp.bfloat16)


def attend_kernel(
    steps, heads, tok_rows, ctx_rows, head_dim, scale, came_from, goes_to, got_ref, out_ref
):
    sections = len(came_from)
    sources = got_ref.shape[0]
    ctx_base = steps * heads * 3 * head_dim
    log2_scale = scale * math.log2(math.e)

    def part(step, section, head, role):
        base = ((step * heads + head) * 3 + role) * head_dim
        return jnp.concatenate(
            [got_ref[p, :, base : base + head_dim] for p in came_from[section]], axis=0
        )

    def context(head, role):
        base = ctx_base + role * head_dim
        rows = slice(head * ctx_rows, (head + 1) * ctx_rows)
        return got_ref[:, rows, base : base + head_dim].reshape(sources * ctx_rows, head_dim)

    def with_ones(vals):
        return jnp.concatenate([vals, jnp.ones_like(vals)], axis=1)

    def product(left, right):
        return lax.dot_general(
            left, right, (((1,), (1,)), ((), ())), preferred_element_type=jnp.float32
        )

    last = sections - 1
    ctx_tokens = sources * ctx_rows
    tokens = len(came_from[0]) * tok_rows
    blocks = [(step, s) for step in range(steps) for s in range(sections)]
    shared = [s == last and step + 1 < steps for step, s in blocks]
    allowed = [
        ctx_tokens + (step + is_shared) * tokens
        for (step, _), is_shared in zip(blocks, shared)
    ]
    every_task = []
    for head in range(heads):
        earlier = [(step, last, head) for step in range(steps - 1)]
        keys = jnp.concatenate([context(head, 0)] + [part(*e, 1) for e in earlier], axis=0)
        vals = jnp.concatenate([context(head, 1)] + [part(*e, 2) for e in earlier], axis=0)
        queries = [part(step, s, head, 0) for step, s in blocks]
        scores = product(jnp.concatenate(queries, axis=0), keys)
        lane = lax.broadcasted_iota(jnp.int32, (tokens, keys.shape[0]), 1)
        tasks = []
        for i, (step, s) in enumerate(blocks):
            common = scores[i * tokens : (i + 1) * tokens]
            if allowed[i] < keys.shape[0]:
                common = jnp.where(lane < allowed[i], common, -jnp.inf)
            own = None if shared[i] else product(queries[i], part(step, s, head, 1))
            tasks.append((common, own))
        every_task.append((tasks, vals))
    every_weight = []
    for tasks, _ in every_task:
        weights = []
        for common, own in tasks:
            top = jnp.max(common, axis=1, keepdims=True)
            if own is not None:
                top = jnp.maximum(top, jnp.max(own, axis=1, keepdims=True))
            weights.append(
                [
                    None if x is None else jnp.exp2((x - top) * log2_scale).astype(jnp.bfloat16)
                    for x in (common, own)
                ]
            )
        every_weight.append(weights)
    for head, (weights, (_, vals)) in enumerate(zip(every_weight, every_task)):
        mixed_all = jnp.dot(
            jnp.concatenate([common for common, _ in weights], axis=0),
            with_ones(vals),
            preferred_element_type=jnp.float32,
        )
        for i, (step, s) in enumerate(blocks):
            mixed = mixed_all[i * tokens : (i + 1) * tokens]
            if not shared[i]:
                mixed = mixed + jnp.dot(
                    weights[i][1],
                    with_ones(part(step, s, head, 2)),
                    preferred_element_type=jnp.float32,
                )
            done = (mixed[:, :head_dim] / mixed[:, head_dim:]).astype(jnp.bfloat16)
            base = (step * heads + head) * head_dim
            for slot, p in enumerate(goes_to[s]):
                out_ref[p, :, base : base + head_dim] = done[slot * tok_rows : (slot + 1) * tok_rows]


def pack_kernel(
    steps, block_of, heads, ctx_rows, head_dim, chunks, qkv_hbm, ctx_hbm, out_ref, qkv_ref, ctx_ref, sems, ctx_sem
):
    groups = len(block_of)
    width = heads * 3 * head_dim
    span = groups // chunks
    ctx_copy = pltpu.make_async_copy(ctx_hbm, ctx_ref, ctx_sem)
    copies = []
    for step in range(steps):
        for chunk in range(chunks):
            columns = pl.ds(chunk * span * width, span * width)
            copies.append(
                pltpu.make_async_copy(
                    qkv_hbm.at[step, 0, :, columns],
                    qkv_ref.at[step, :, columns],
                    sems.at[step, chunk],
                )
            )
    ctx_copy.start()
    for copy in copies:
        copy.start()
    base = steps * width
    ctx_copy.wait()
    for group in range(groups):
        for role in range(2):
            columns = [((group * heads + head) * 2 + role) * head_dim for head in range(heads)]
            block = [ctx_ref[:, c : c + head_dim] for c in columns]
            out_ref[block_of[group], :, base + role * head_dim : base + (role + 1) * head_dim] = (
                jnp.concatenate(block, axis=0)
            )
    for step in range(steps):
        for chunk in range(chunks):
            copies[step * chunks + chunk].wait()
            for group in range(chunk * span, (chunk + 1) * span):
                out_ref[block_of[group], :, step * width : (step + 1) * width] = qkv_ref[
                    step, :, group * width : (group + 1) * width
                ]


def exchange(blocks, order):
    return lax.all_to_all(
        blocks, AXES, split_axis=0, concat_axis=0, axis_index_groups=[order], tiled=True
    )


def send_orders(sections, per_section):
    peers = sections * per_section
    quarter = math.gcd(peers, 4)
    row = peers // quarter
    inner = [i + s for i in range(row - sections, -1, -sections) for s in range(sections)]
    turned = [z * row + i for z in range(quarter - 1, -1, -1) for i in inner]
    first = turned[row:] + turned[:row]
    half = quarter // 2
    rows = list(range(half, quarter)) + list(range(half))
    second = [z * row + i for z in rows for i in inner]
    return first, second


def shards(qkv_all, context_kv):
    sections = lax.axis_size("section")
    peers = sections * lax.axis_size("seq")
    groups = min(peers, HEADS)
    copies = peers // groups
    heads = HEADS // groups
    steps, _, tok_rows, width = qkv_all.shape
    head_dim = width // (3 * HEADS)
    ctx_rows = context_kv.shape[0]
    scale = head_dim ** (-0.5)
    if copies > 1 or heads * ctx_rows != tok_rows:
        return shards_copied(qkv_all, context_kv, sections, groups, copies, heads, scale)

    chunks = 1
    per_section = peers // sections
    first, second = send_orders(sections, per_section)
    devices = range(sections * per_section)
    block_of = [first.index(second[group]) for group in range(groups)]
    came_from = [[first.index(d) for d in devices if d % sections == s] for s in range(sections)]
    goes_to = [[second.index(d) for d in devices if d % sections == s] for s in range(sections)]
    in_vmem = pl.BlockSpec(memory_space=pltpu.VMEM)
    params = pltpu.CompilerParams(vmem_limit_bytes=32 * 1024 * 1024)
    sent = pl.pallas_call(
        functools.partial(pack_kernel, steps, block_of, heads, ctx_rows, head_dim, chunks),
        out_shape=jax.ShapeDtypeStruct(
            (groups, tok_rows, (steps * heads * 3 + 2) * head_dim), jnp.bfloat16
        ),
        in_specs=[pl.BlockSpec(memory_space=pltpu.HBM)] * 2,
        out_specs=in_vmem,
        scratch_shapes=[
            pltpu.VMEM((steps, tok_rows, width), jnp.bfloat16),
            pltpu.VMEM(context_kv.shape, jnp.bfloat16),
            pltpu.SemaphoreType.DMA((steps, chunks)),
            pltpu.SemaphoreType.DMA,
        ],
        compiler_params=params,
    )(*(pltpu.with_memory_space_constraint(x, pltpu.HBM) for x in (qkv_all, context_kv)))
    got = exchange(sent, first)
    mixed = pl.pallas_call(
        functools.partial(
            attend_kernel, steps, heads, tok_rows, ctx_rows, head_dim, scale, came_from, goes_to
        ),
        out_shape=jax.ShapeDtypeStruct((peers, tok_rows, steps * heads * head_dim), jnp.bfloat16),
        in_specs=[in_vmem],
        out_specs=in_vmem,
        compiler_params=params,
    )(got)
    back = exchange(mixed, second)
    back = back.reshape(groups, tok_rows, steps, heads * head_dim).transpose(2, 1, 0, 3)
    return back.reshape(steps, 1, tok_rows, HEADS * head_dim)


def shards_copied(qkv_all, context_kv, sections, groups, copies, heads, scale):
    steps, _, tok_rows, width = qkv_all.shape
    head_dim = width // (3 * HEADS)
    peers = groups * copies
    share = tok_rows // copies
    ctx_rows = context_kv.shape[0]
    frames = qkv_all[:, 0].reshape(steps, tok_rows, groups, heads, 3, head_dim)
    queries = frames[..., 0, :].reshape(steps, copies, share, groups, heads, head_dim)
    queries = queries.transpose(3, 1, 0, 4, 2, 5).reshape(peers, -1, head_dim)
    key_vals = frames[..., 1:, :].transpose(2, 0, 3, 4, 1, 5).reshape(groups, -1, head_dim)
    ctx = context_kv.reshape(ctx_rows, groups, heads, 2, head_dim)
    ctx = ctx.transpose(1, 2, 3, 0, 4).reshape(groups, -1, head_dim)
    shared = jnp.concatenate([key_vals, ctx], axis=1)
    shared = jnp.broadcast_to(shared[:, None], (groups, copies) + shared.shape[1:])
    shared = shared.reshape((peers,) + shared.shape[2:])
    sent = jnp.concatenate([queries, shared], axis=1)
    got = lax.all_to_all(sent, AXES, split_axis=0, concat_axis=0, tiled=True)
    per_section = peers // sections
    cut = steps * heads * share
    end = cut + steps * heads * 2 * tok_rows
    q = got[:, :cut].reshape(per_section, sections, steps, heads, share, head_dim)
    q = q.transpose(2, 1, 3, 0, 4, 5).reshape(steps, sections, heads, -1, head_dim)
    kv = got[:, cut:end].reshape(per_section, sections, steps, heads, 2, tok_rows, head_dim)
    kv = kv.transpose(2, 1, 4, 3, 0, 5, 6).reshape(steps, sections, 2, heads, -1, head_dim)
    ctx = got[:, end:].reshape(peers, heads, 2, ctx_rows, head_dim)
    earlier = [ctx.transpose(2, 1, 0, 3, 4).reshape(2, heads, -1, head_dim)]
    results = []
    for step in range(steps):
        for s in range(sections):
            keys, vals = jnp.concatenate(earlier + [kv[step, s]], axis=2)
            results.append(
                jnp.stack([softmax_mix(q[step, s, h], keys[h], vals[h], scale) for h in range(heads)])
            )
        earlier = earlier + [kv[step, sections - 1]]
    mixed = jnp.stack(results).reshape(steps, sections, heads, per_section, share, head_dim)
    mixed = mixed.transpose(3, 1, 0, 2, 4, 5).reshape(peers, -1, head_dim)
    back = lax.all_to_all(mixed, AXES, split_axis=0, concat_axis=0, tiled=True)
    back = back.reshape(groups, copies, steps, heads, share, head_dim)
    back = back.transpose(2, 1, 4, 0, 3, 5)
    return back.reshape(steps, 1, tok_rows, HEADS * head_dim)


def solution(mesh):
    in_specs = (P(None, "section", ("rep", "seq"), None), P(("rep", "section", "seq"), None))
    out_specs = P(None, "section", ("rep", "seq"), None)
    return jax.shard_map(shards, mesh=mesh, in_specs=in_specs, out_specs=out_specs, check_vma=False)
```

```python
import functools
import math

import jax
import jax.numpy as jnp
from jax import lax
from jax.experimental import pallas as pl
from jax.experimental.pallas import tpu as pltpu
from jax.sharding import PartitionSpec as P

HEADS = 32
AXES = ("seq", "section")


def softmax_mix(queries, keys, values, scale):
    scores = (
        lax.dot_general(
            queries, keys, (((1,), (1,)), ((), ())), preferred_element_type=jnp.float32
        )
        * scale
    )
    weights = jnp.exp(scores - jnp.max(scores, axis=1, keepdims=True))
    total = jnp.sum(weights, axis=1, keepdims=True)
    mixed = jnp.dot(weights.astype(jnp.bfloat16), values, preferred_element_type=jnp.float32)
    return (mixed / total).astype(jnp.bfloat16)


def attend_kernel(
    steps, heads, tok_rows, ctx_rows, head_dim, scale, came_from, goes_to, got_ref, out_ref
):
    sections = len(came_from)
    sources = got_ref.shape[0]
    ctx_base = steps * heads * 3 * head_dim
    log2_scale = scale * math.log2(math.e)

    def part(step, section, head, role):
        base = ((step * heads + head) * 3 + role) * head_dim
        return jnp.concatenate(
            [got_ref[p, :, base : base + head_dim] for p in came_from[section]], axis=0
        )

    def context(head, role):
        base = ctx_base + role * head_dim
        rows = slice(head * ctx_rows, (head + 1) * ctx_rows)
        return got_ref[:, rows, base : base + head_dim].reshape(sources * ctx_rows, head_dim)

    def with_ones(vals):
        return jnp.concatenate([vals, jnp.ones_like(vals)], axis=1)

    def product(left, right):
        return lax.dot_general(
            left, right, (((1,), (1,)), ((), ())), preferred_element_type=jnp.float32
        )

    last = sections - 1
    ctx_tokens = sources * ctx_rows
    tokens = len(came_from[0]) * tok_rows
    blocks = [(step, s) for step in range(steps) for s in range(sections)]
    shared = [s == last and step + 1 < steps for step, s in blocks]
    allowed = [
        ctx_tokens + (step + is_shared) * tokens
        for (step, _), is_shared in zip(blocks, shared)
    ]
    every_task = []
    for head in range(heads):
        earlier = [(step, last, head) for step in range(steps - 1)]
        keys = jnp.concatenate([context(head, 0)] + [part(*e, 1) for e in earlier], axis=0)
        vals = jnp.concatenate([context(head, 1)] + [part(*e, 2) for e in earlier], axis=0)
        queries = [part(step, s, head, 0) for step, s in blocks]
        scores = product(jnp.concatenate(queries, axis=0), keys)
        lane = lax.broadcasted_iota(jnp.int32, (tokens, keys.shape[0]), 1)
        tasks = []
        for i, (step, s) in enumerate(blocks):
            common = scores[i * tokens : (i + 1) * tokens]
            if allowed[i] < keys.shape[0]:
                common = jnp.where(lane < allowed[i], common, -jnp.inf)
            own = None if shared[i] else product(queries[i], part(step, s, head, 1))
            tasks.append((common, own))
        every_task.append((tasks, vals))
    every_weight = []
    for tasks, _ in every_task:
        weights = []
        for common, own in tasks:
            top = jnp.max(common, axis=1, keepdims=True)
            if own is not None:
                top = jnp.maximum(top, jnp.max(own, axis=1, keepdims=True))
            weights.append(
                [
                    None if x is None else jnp.exp2((x - top) * log2_scale).astype(jnp.bfloat16)
                    for x in (common, own)
                ]
            )
        every_weight.append(weights)
    for head, (weights, (_, vals)) in enumerate(zip(every_weight, every_task)):
        mixed_all = jnp.dot(
            jnp.concatenate([common for common, _ in weights], axis=0),
            with_ones(vals),
            preferred_element_type=jnp.float32,
        )
        for i, (step, s) in enumerate(blocks):
            mixed = mixed_all[i * tokens : (i + 1) * tokens]
            if not shared[i]:
                mixed = mixed + jnp.dot(
                    weights[i][1],
                    with_ones(part(step, s, head, 2)),
                    preferred_element_type=jnp.float32,
                )
            done = (mixed[:, :head_dim] / mixed[:, head_dim:]).astype(jnp.bfloat16)
            base = (step * heads + head) * head_dim
            for slot, p in enumerate(goes_to[s]):
                out_ref[p, :, base : base + head_dim] = done[slot * tok_rows : (slot + 1) * tok_rows]


def pack_kernel(
    steps, block_of, heads, ctx_rows, head_dim, chunks, qkv_hbm, ctx_hbm, out_ref, qkv_ref, ctx_ref, sems, ctx_sem
):
    groups = len(block_of)
    width = heads * 3 * head_dim
    span = groups // chunks
    ctx_copy = pltpu.make_async_copy(ctx_hbm, ctx_ref, ctx_sem)
    copies = []
    for step in range(steps):
        for chunk in range(chunks):
            columns = pl.ds(chunk * span * width, span * width)
            copies.append(
                pltpu.make_async_copy(
                    qkv_hbm.at[step, 0, :, columns],
                    qkv_ref.at[step, :, columns],
                    sems.at[step, chunk],
                )
            )
    ctx_copy.start()
    for copy in copies:
        copy.start()
    base = steps * width
    ctx_copy.wait()
    for group in range(groups):
        for role in range(2):
            columns = [((group * heads + head) * 2 + role) * head_dim for head in range(heads)]
            block = [ctx_ref[:, c : c + head_dim] for c in columns]
            out_ref[block_of[group], :, base + role * head_dim : base + (role + 1) * head_dim] = (
                jnp.concatenate(block, axis=0)
            )
    for step in range(steps):
        for chunk in range(chunks):
            copies[step * chunks + chunk].wait()
            for group in range(chunk * span, (chunk + 1) * span):
                out_ref[block_of[group], :, step * width : (step + 1) * width] = qkv_ref[
                    step, :, group * width : (group + 1) * width
                ]


def exchange(blocks, order):
    return lax.all_to_all(
        blocks, AXES, split_axis=0, concat_axis=0, axis_index_groups=[order], tiled=True
    )


def send_orders(sections, per_section):
    peers = sections * per_section
    quarter = math.gcd(peers, 4)
    row = peers // quarter
    inner = [i + s for i in range(0, row, sections) for s in range(sections - 1, -1, -1)]
    turned = [z * row + i for z in range(quarter - 1, -1, -1) for i in inner]
    first = turned[row:] + turned[:row]
    half = quarter // 2
    rows = list(range(half, quarter)) + list(range(half))
    second = [z * row + i for z in rows for i in inner]
    return first, second


def shards(qkv_all, context_kv):
    sections = lax.axis_size("section")
    peers = sections * lax.axis_size("seq")
    groups = min(peers, HEADS)
    copies = peers // groups
    heads = HEADS // groups
    steps, _, tok_rows, width = qkv_all.shape
    head_dim = width // (3 * HEADS)
    ctx_rows = context_kv.shape[0]
    scale = head_dim ** (-0.5)
    if copies > 1 or heads * ctx_rows != tok_rows:
        return shards_copied(qkv_all, context_kv, sections, groups, copies, heads, scale)

    chunks = 1
    per_section = peers // sections
    first, second = send_orders(sections, per_section)
    devices = range(sections * per_section)
    block_of = [first.index(second[group]) for group in range(groups)]
    came_from = [[first.index(d) for d in devices if d % sections == s] for s in range(sections)]
    goes_to = [[second.index(d) for d in devices if d % sections == s] for s in range(sections)]
    in_vmem = pl.BlockSpec(memory_space=pltpu.VMEM)
    params = pltpu.CompilerParams(vmem_limit_bytes=32 * 1024 * 1024)
    sent = pl.pallas_call(
        functools.partial(pack_kernel, steps, block_of, heads, ctx_rows, head_dim, chunks),
        out_shape=jax.ShapeDtypeStruct(
            (groups, tok_rows, (steps * heads * 3 + 2) * head_dim), jnp.bfloat16
        ),
        in_specs=[pl.BlockSpec(memory_space=pltpu.HBM)] * 2,
        out_specs=in_vmem,
        scratch_shapes=[
            pltpu.VMEM((steps, tok_rows, width), jnp.bfloat16),
            pltpu.VMEM(context_kv.shape, jnp.bfloat16),
            pltpu.SemaphoreType.DMA((steps, chunks)),
            pltpu.SemaphoreType.DMA,
        ],
        compiler_params=params,
    )(*(pltpu.with_memory_space_constraint(x, pltpu.HBM) for x in (qkv_all, context_kv)))
    got = exchange(sent, first)
    mixed = pl.pallas_call(
        functools.partial(
            attend_kernel, steps, heads, tok_rows, ctx_rows, head_dim, scale, came_from, goes_to
        ),
        out_shape=jax.ShapeDtypeStruct((peers, tok_rows, steps * heads * head_dim), jnp.bfloat16),
        in_specs=[in_vmem],
        out_specs=in_vmem,
        compiler_params=params,
    )(got)
    back = exchange(mixed, second)
    back = back.reshape(groups, tok_rows, steps, heads * head_dim).transpose(2, 1, 0, 3)
    return back.reshape(steps, 1, tok_rows, HEADS * head_dim)


def shards_copied(qkv_all, context_kv, sections, groups, copies, heads, scale):
    steps, _, tok_rows, width = qkv_all.shape
    head_dim = width // (3 * HEADS)
    peers = groups * copies
    share = tok_rows // copies
    ctx_rows = context_kv.shape[0]
    frames = qkv_all[:, 0].reshape(steps, tok_rows, groups, heads, 3, head_dim)
    queries = frames[..., 0, :].reshape(steps, copies, share, groups, heads, head_dim)
    queries = queries.transpose(3, 1, 0, 4, 2, 5).reshape(peers, -1, head_dim)
    key_vals = frames[..., 1:, :].transpose(2, 0, 3, 4, 1, 5).reshape(groups, -1, head_dim)
    ctx = context_kv.reshape(ctx_rows, groups, heads, 2, head_dim)
    ctx = ctx.transpose(1, 2, 3, 0, 4).reshape(groups, -1, head_dim)
    shared = jnp.concatenate([key_vals, ctx], axis=1)
    shared = jnp.broadcast_to(shared[:, None], (groups, copies) + shared.shape[1:])
    shared = shared.reshape((peers,) + shared.shape[2:])
    sent = jnp.concatenate([queries, shared], axis=1)
    got = lax.all_to_all(sent, AXES, split_axis=0, concat_axis=0, tiled=True)
    per_section = peers // sections
    cut = steps * heads * share
    end = cut + steps * heads * 2 * tok_rows
    q = got[:, :cut].reshape(per_section, sections, steps, heads, share, head_dim)
    q = q.transpose(2, 1, 3, 0, 4, 5).reshape(steps, sections, heads, -1, head_dim)
    kv = got[:, cut:end].reshape(per_section, sections, steps, heads, 2, tok_rows, head_dim)
    kv = kv.transpose(2, 1, 4, 3, 0, 5, 6).reshape(steps, sections, 2, heads, -1, head_dim)
    ctx = got[:, end:].reshape(peers, heads, 2, ctx_rows, head_dim)
    earlier = [ctx.transpose(2, 1, 0, 3, 4).reshape(2, heads, -1, head_dim)]
    results = []
    for step in range(steps):
        for s in range(sections):
            keys, vals = jnp.concatenate(earlier + [kv[step, s]], axis=2)
            results.append(
                jnp.stack([softmax_mix(q[step, s, h], keys[h], vals[h], scale) for h in range(heads)])
            )
        earlier = earlier + [kv[step, sections - 1]]
    mixed = jnp.stack(results).reshape(steps, sections, heads, per_section, share, head_dim)
    mixed = mixed.transpose(3, 1, 0, 2, 4, 5).reshape(peers, -1, head_dim)
    back = lax.all_to_all(mixed, AXES, split_axis=0, concat_axis=0, tiled=True)
    back = back.reshape(groups, copies, steps, heads, share, head_dim)
    back = back.transpose(2, 1, 4, 0, 3, 5)
    return back.reshape(steps, 1, tok_rows, HEADS * head_dim)


def solution(mesh):
    in_specs = (P(None, "section", ("rep", "seq"), None), P(("rep", "section", "seq"), None))
    out_specs = P(None, "section", ("rep", "seq"), None)
    return jax.shard_map(shards, mesh=mesh, in_specs=in_specs, out_specs=out_specs, check_vma=False)
```

```python
import functools
import math

import jax
import jax.numpy as jnp
from jax import lax
from jax.experimental import pallas as pl
from jax.experimental.pallas import tpu as pltpu
from jax.sharding import PartitionSpec as P

HEADS = 32
AXES = ("seq", "section")


def softmax_mix(queries, keys, values, scale):
    scores = (
        lax.dot_general(
            queries, keys, (((1,), (1,)), ((), ())), preferred_element_type=jnp.float32
        )
        * scale
    )
    weights = jnp.exp(scores - jnp.max(scores, axis=1, keepdims=True))
    total = jnp.sum(weights, axis=1, keepdims=True)
    mixed = jnp.dot(weights.astype(jnp.bfloat16), values, preferred_element_type=jnp.float32)
    return (mixed / total).astype(jnp.bfloat16)


def attend_kernel(
    steps, heads, tok_rows, ctx_rows, head_dim, scale, came_from, goes_to, got_ref, out_ref
):
    sections = len(came_from)
    sources = got_ref.shape[0]
    ctx_base = steps * heads * 3 * head_dim
    log2_scale = scale * math.log2(math.e)

    def part(step, section, head, role):
        base = ((step * heads + head) * 3 + role) * head_dim
        return jnp.concatenate(
            [got_ref[p, :, base : base + head_dim] for p in came_from[section]], axis=0
        )

    def context(head, role):
        base = ctx_base + role * head_dim
        rows = slice(head * ctx_rows, (head + 1) * ctx_rows)
        return got_ref[:, rows, base : base + head_dim].reshape(sources * ctx_rows, head_dim)

    def with_ones(vals):
        return jnp.concatenate([vals, jnp.ones_like(vals)], axis=1)

    def product(left, right):
        return lax.dot_general(
            left, right, (((1,), (1,)), ((), ())), preferred_element_type=jnp.float32
        )

    last = sections - 1
    ctx_tokens = sources * ctx_rows
    tokens = len(came_from[0]) * tok_rows
    blocks = [(step, s) for step in range(steps) for s in range(sections)]
    shared = [s == last and step + 1 < steps for step, s in blocks]
    allowed = [
        ctx_tokens + (step + is_shared) * tokens
        for (step, _), is_shared in zip(blocks, shared)
    ]
    every_task = []
    for head in range(heads):
        earlier = [(step, last, head) for step in range(steps - 1)]
        keys = jnp.concatenate([context(head, 0)] + [part(*e, 1) for e in earlier], axis=0)
        vals = jnp.concatenate([context(head, 1)] + [part(*e, 2) for e in earlier], axis=0)
        queries = [part(step, s, head, 0) for step, s in blocks]
        scores = product(jnp.concatenate(queries, axis=0), keys)
        lane = lax.broadcasted_iota(jnp.int32, (tokens, keys.shape[0]), 1)
        tasks = []
        for i, (step, s) in enumerate(blocks):
            common = scores[i * tokens : (i + 1) * tokens]
            if allowed[i] < keys.shape[0]:
                common = jnp.where(lane < allowed[i], common, -jnp.inf)
            own = None if shared[i] else product(queries[i], part(step, s, head, 1))
            tasks.append((common, own))
        every_task.append((tasks, vals))
    every_weight = []
    for tasks, _ in every_task:
        weights = []
        for common, own in tasks:
            top = jnp.max(common, axis=1, keepdims=True)
            if own is not None:
                top = jnp.maximum(top, jnp.max(own, axis=1, keepdims=True))
            weights.append(
                [
                    None if x is None else jnp.exp2((x - top) * log2_scale).astype(jnp.bfloat16)
                    for x in (common, own)
                ]
            )
        every_weight.append(weights)
    for head, (weights, (_, vals)) in enumerate(zip(every_weight, every_task)):
        mixed_all = jnp.dot(
            jnp.concatenate([common for common, _ in weights], axis=0),
            with_ones(vals),
            preferred_element_type=jnp.float32,
        )
        for i, (step, s) in enumerate(blocks):
            mixed = mixed_all[i * tokens : (i + 1) * tokens]
            if not shared[i]:
                mixed = mixed + jnp.dot(
                    weights[i][1],
                    with_ones(part(step, s, head, 2)),
                    preferred_element_type=jnp.float32,
                )
            done = (mixed[:, :head_dim] / mixed[:, head_dim:]).astype(jnp.bfloat16)
            base = (step * heads + head) * head_dim
            for slot, p in enumerate(goes_to[s]):
                out_ref[p, :, base : base + head_dim] = done[slot * tok_rows : (slot + 1) * tok_rows]


def pack_kernel(
    steps, block_of, heads, ctx_rows, head_dim, chunks, qkv_hbm, ctx_hbm, out_ref, qkv_ref, ctx_ref, sems, ctx_sem
):
    groups = len(block_of)
    width = heads * 3 * head_dim
    span = groups // chunks
    ctx_copy = pltpu.make_async_copy(ctx_hbm, ctx_ref, ctx_sem)
    copies = []
    for step in range(steps):
        for chunk in range(chunks):
            columns = pl.ds(chunk * span * width, span * width)
            copies.append(
                pltpu.make_async_copy(
                    qkv_hbm.at[step, 0, :, columns],
                    qkv_ref.at[step, :, columns],
                    sems.at[step, chunk],
                )
            )
    ctx_copy.start()
    for copy in copies:
        copy.start()
    base = steps * width
    ctx_copy.wait()
    for group in range(groups):
        for role in range(2):
            columns = [((group * heads + head) * 2 + role) * head_dim for head in range(heads)]
            block = [ctx_ref[:, c : c + head_dim] for c in columns]
            out_ref[block_of[group], :, base + role * head_dim : base + (role + 1) * head_dim] = (
                jnp.concatenate(block, axis=0)
            )
    for step in range(steps):
        for chunk in range(chunks):
            copies[step * chunks + chunk].wait()
            for group in range(chunk * span, (chunk + 1) * span):
                out_ref[block_of[group], :, step * width : (step + 1) * width] = qkv_ref[
                    step, :, group * width : (group + 1) * width
                ]


def exchange(blocks, order):
    return lax.all_to_all(
        blocks, AXES, split_axis=0, concat_axis=0, axis_index_groups=[order], tiled=True
    )


def send_orders(sections, per_section):
    peers = sections * per_section
    quarter = math.gcd(peers, 4)
    row = peers // quarter
    half = quarter // 2
    halves = list(range(half, quarter)) + list(range(half - 1, -1, -1))
    first = [z * row + i for z in halves for i in range(row - 1, -1, -1)]
    rows = list(range(half, quarter)) + list(range(half))
    second = [z * row + i for z in rows for i in range(row - 1, -1, -1)]
    return first, second


def shards(qkv_all, context_kv):
    sections = lax.axis_size("section")
    peers = sections * lax.axis_size("seq")
    groups = min(peers, HEADS)
    copies = peers // groups
    heads = HEADS // groups
    steps, _, tok_rows, width = qkv_all.shape
    head_dim = width // (3 * HEADS)
    ctx_rows = context_kv.shape[0]
    scale = head_dim ** (-0.5)
    if copies > 1 or heads * ctx_rows != tok_rows:
        return shards_copied(qkv_all, context_kv, sections, groups, copies, heads, scale)

    chunks = 1
    per_section = peers // sections
    first, second = send_orders(sections, per_section)
    devices = range(sections * per_section)
    block_of = [first.index(second[group]) for group in range(groups)]
    came_from = [[first.index(d) for d in devices if d % sections == s] for s in range(sections)]
    goes_to = [[second.index(d) for d in devices if d % sections == s] for s in range(sections)]
    in_vmem = pl.BlockSpec(memory_space=pltpu.VMEM)
    params = pltpu.CompilerParams(vmem_limit_bytes=32 * 1024 * 1024)
    sent = pl.pallas_call(
        functools.partial(pack_kernel, steps, block_of, heads, ctx_rows, head_dim, chunks),
        out_shape=jax.ShapeDtypeStruct(
            (groups, tok_rows, (steps * heads * 3 + 2) * head_dim), jnp.bfloat16
        ),
        in_specs=[pl.BlockSpec(memory_space=pltpu.HBM)] * 2,
        out_specs=in_vmem,
        scratch_shapes=[
            pltpu.VMEM((steps, tok_rows, width), jnp.bfloat16),
            pltpu.VMEM(context_kv.shape, jnp.bfloat16),
            pltpu.SemaphoreType.DMA((steps, chunks)),
            pltpu.SemaphoreType.DMA,
        ],
        compiler_params=params,
    )(*(pltpu.with_memory_space_constraint(x, pltpu.HBM) for x in (qkv_all, context_kv)))
    got = exchange(sent, first)
    mixed = pl.pallas_call(
        functools.partial(
            attend_kernel, steps, heads, tok_rows, ctx_rows, head_dim, scale, came_from, goes_to
        ),
        out_shape=jax.ShapeDtypeStruct((peers, tok_rows, steps * heads * head_dim), jnp.bfloat16),
        in_specs=[in_vmem],
        out_specs=in_vmem,
        compiler_params=params,
    )(got)
    back = exchange(mixed, second)
    back = back.reshape(groups, tok_rows, steps, heads * head_dim).transpose(2, 1, 0, 3)
    return back.reshape(steps, 1, tok_rows, HEADS * head_dim)


def shards_copied(qkv_all, context_kv, sections, groups, copies, heads, scale):
    steps, _, tok_rows, width = qkv_all.shape
    head_dim = width // (3 * HEADS)
    peers = groups * copies
    share = tok_rows // copies
    ctx_rows = context_kv.shape[0]
    frames = qkv_all[:, 0].reshape(steps, tok_rows, groups, heads, 3, head_dim)
    queries = frames[..., 0, :].reshape(steps, copies, share, groups, heads, head_dim)
    queries = queries.transpose(3, 1, 0, 4, 2, 5).reshape(peers, -1, head_dim)
    key_vals = frames[..., 1:, :].transpose(2, 0, 3, 4, 1, 5).reshape(groups, -1, head_dim)
    ctx = context_kv.reshape(ctx_rows, groups, heads, 2, head_dim)
    ctx = ctx.transpose(1, 2, 3, 0, 4).reshape(groups, -1, head_dim)
    shared = jnp.concatenate([key_vals, ctx], axis=1)
    shared = jnp.broadcast_to(shared[:, None], (groups, copies) + shared.shape[1:])
    shared = shared.reshape((peers,) + shared.shape[2:])
    sent = jnp.concatenate([queries, shared], axis=1)
    got = lax.all_to_all(sent, AXES, split_axis=0, concat_axis=0, tiled=True)
    per_section = peers // sections
    cut = steps * heads * share
    end = cut + steps * heads * 2 * tok_rows
    q = got[:, :cut].reshape(per_section, sections, steps, heads, share, head_dim)
    q = q.transpose(2, 1, 3, 0, 4, 5).reshape(steps, sections, heads, -1, head_dim)
    kv = got[:, cut:end].reshape(per_section, sections, steps, heads, 2, tok_rows, head_dim)
    kv = kv.transpose(2, 1, 4, 3, 0, 5, 6).reshape(steps, sections, 2, heads, -1, head_dim)
    ctx = got[:, end:].reshape(peers, heads, 2, ctx_rows, head_dim)
    earlier = [ctx.transpose(2, 1, 0, 3, 4).reshape(2, heads, -1, head_dim)]
    results = []
    for step in range(steps):
        for s in range(sections):
            keys, vals = jnp.concatenate(earlier + [kv[step, s]], axis=2)
            results.append(
                jnp.stack([softmax_mix(q[step, s, h], keys[h], vals[h], scale) for h in range(heads)])
            )
        earlier = earlier + [kv[step, sections - 1]]
    mixed = jnp.stack(results).reshape(steps, sections, heads, per_section, share, head_dim)
    mixed = mixed.transpose(3, 1, 0, 2, 4, 5).reshape(peers, -1, head_dim)
    back = lax.all_to_all(mixed, AXES, split_axis=0, concat_axis=0, tiled=True)
    back = back.reshape(groups, copies, steps, heads, share, head_dim)
    back = back.transpose(2, 1, 4, 0, 3, 5)
    return back.reshape(steps, 1, tok_rows, HEADS * head_dim)


def solution(mesh):
    in_specs = (P(None, "section", ("rep", "seq"), None), P(("rep", "section", "seq"), None))
    out_specs = P(None, "section", ("rep", "seq"), None)
    return jax.shard_map(shards, mesh=mesh, in_specs=in_specs, out_specs=out_specs, check_vma=False)
```

```python
import functools
import math

import jax
import jax.numpy as jnp
from jax import lax
from jax.experimental import pallas as pl
from jax.experimental.pallas import tpu as pltpu
from jax.sharding import PartitionSpec as P

HEADS = 32
AXES = ("seq", "section")


def softmax_mix(queries, keys, values, scale):
    scores = (
        lax.dot_general(
            queries, keys, (((1,), (1,)), ((), ())), preferred_element_type=jnp.float32
        )
        * scale
    )
    weights = jnp.exp(scores - jnp.max(scores, axis=1, keepdims=True))
    total = jnp.sum(weights, axis=1, keepdims=True)
    mixed = jnp.dot(weights.astype(jnp.bfloat16), values, preferred_element_type=jnp.float32)
    return (mixed / total).astype(jnp.bfloat16)


def attend_kernel(
    steps, heads, tok_rows, ctx_rows, head_dim, scale, came_from, goes_to, got_ref, out_ref
):
    sections = len(came_from)
    sources = got_ref.shape[0]
    ctx_base = steps * heads * 3 * head_dim
    log2_scale = scale * math.log2(math.e)

    def part(step, section, head, role):
        base = ((step * heads + head) * 3 + role) * head_dim
        return jnp.concatenate(
            [got_ref[p, :, base : base + head_dim] for p in came_from[section]], axis=0
        )

    def context(head, role):
        base = ctx_base + role * head_dim
        rows = slice(head * ctx_rows, (head + 1) * ctx_rows)
        return got_ref[:, rows, base : base + head_dim].reshape(sources * ctx_rows, head_dim)

    def with_ones(vals):
        return jnp.concatenate([vals, jnp.ones_like(vals)], axis=1)

    def product(left, right):
        return lax.dot_general(
            left, right, (((1,), (1,)), ((), ())), preferred_element_type=jnp.float32
        )

    last = sections - 1
    ctx_tokens = sources * ctx_rows
    tokens = len(came_from[0]) * tok_rows
    blocks = [(step, s) for step in range(steps) for s in range(sections)]
    shared = [s == last and step + 1 < steps for step, s in blocks]
    allowed = [
        ctx_tokens + (step + is_shared) * tokens
        for (step, _), is_shared in zip(blocks, shared)
    ]
    every_task = []
    for head in range(heads):
        earlier = [(step, last, head) for step in range(steps - 1)]
        keys = jnp.concatenate([context(head, 0)] + [part(*e, 1) for e in earlier], axis=0)
        vals = jnp.concatenate([context(head, 1)] + [part(*e, 2) for e in earlier], axis=0)
        queries = [part(step, s, head, 0) for step, s in blocks]
        scores = product(jnp.concatenate(queries, axis=0), keys)
        lane = lax.broadcasted_iota(jnp.int32, (tokens, keys.shape[0]), 1)
        tasks = []
        for i, (step, s) in enumerate(blocks):
            common = scores[i * tokens : (i + 1) * tokens]
            if allowed[i] < keys.shape[0]:
                common = jnp.where(lane < allowed[i], common, -jnp.inf)
            own = None if shared[i] else product(queries[i], part(step, s, head, 1))
            tasks.append((common, own))
        every_task.append((tasks, vals))
    every_weight = []
    for tasks, _ in every_task:
        weights = []
        for common, own in tasks:
            top = jnp.max(common, axis=1, keepdims=True)
            if own is not None:
                top = jnp.maximum(top, jnp.max(own, axis=1, keepdims=True))
            weights.append(
                [
                    None if x is None else jnp.exp2((x - top) * log2_scale).astype(jnp.bfloat16)
                    for x in (common, own)
                ]
            )
        every_weight.append(weights)
    for head, (weights, (_, vals)) in enumerate(zip(every_weight, every_task)):
        mixed_all = jnp.dot(
            jnp.concatenate([common for common, _ in weights], axis=0),
            with_ones(vals),
            preferred_element_type=jnp.float32,
        )
        for i, (step, s) in enumerate(blocks):
            mixed = mixed_all[i * tokens : (i + 1) * tokens]
            if not shared[i]:
                mixed = mixed + jnp.dot(
                    weights[i][1],
                    with_ones(part(step, s, head, 2)),
                    preferred_element_type=jnp.float32,
                )
            done = (mixed[:, :head_dim] / mixed[:, head_dim:]).astype(jnp.bfloat16)
            base = (step * heads + head) * head_dim
            for slot, p in enumerate(goes_to[s]):
                out_ref[p, :, base : base + head_dim] = done[slot * tok_rows : (slot + 1) * tok_rows]


def pack_kernel(
    steps, block_of, heads, ctx_rows, head_dim, chunks, qkv_hbm, ctx_hbm, out_ref, qkv_ref, ctx_ref, sems, ctx_sem
):
    groups = len(block_of)
    width = heads * 3 * head_dim
    span = groups // chunks
    ctx_copy = pltpu.make_async_copy(ctx_hbm, ctx_ref, ctx_sem)
    copies = []
    for step in range(steps):
        for chunk in range(chunks):
            columns = pl.ds(chunk * span * width, span * width)
            copies.append(
                pltpu.make_async_copy(
                    qkv_hbm.at[step, 0, :, columns],
                    qkv_ref.at[step, :, columns],
                    sems.at[step, chunk],
                )
            )
    ctx_copy.start()
    for copy in copies:
        copy.start()
    base = steps * width
    ctx_copy.wait()
    for group in range(groups):
        for role in range(2):
            columns = [((group * heads + head) * 2 + role) * head_dim for head in range(heads)]
            block = [ctx_ref[:, c : c + head_dim] for c in columns]
            out_ref[block_of[group], :, base + role * head_dim : base + (role + 1) * head_dim] = (
                jnp.concatenate(block, axis=0)
            )
    for step in range(steps):
        for chunk in range(chunks):
            copies[step * chunks + chunk].wait()
            for group in range(chunk * span, (chunk + 1) * span):
                out_ref[block_of[group], :, step * width : (step + 1) * width] = qkv_ref[
                    step, :, group * width : (group + 1) * width
                ]


def exchange(blocks, order):
    return lax.all_to_all(
        blocks, AXES, split_axis=0, concat_axis=0, axis_index_groups=[order], tiled=True
    )


def send_orders(sections, per_section):
    peers = sections * per_section
    quarter = math.gcd(peers, 4)
    row = peers // quarter
    turned = [z * row + i for z in range(quarter - 1, -1, -1) for i in range(row - 1, -1, -1)]
    first = turned[row:] + turned[:row]
    half = quarter // 2
    rows = list(range(half - 1, quarter)) + list(range(half - 1))
    second = [z * row + i for z in rows for i in range(row - 1, -1, -1)]
    return first, second


def shards(qkv_all, context_kv):
    sections = lax.axis_size("section")
    peers = sections * lax.axis_size("seq")
    groups = min(peers, HEADS)
    copies = peers // groups
    heads = HEADS // groups
    steps, _, tok_rows, width = qkv_all.shape
    head_dim = width // (3 * HEADS)
    ctx_rows = context_kv.shape[0]
    scale = head_dim ** (-0.5)
    if copies > 1 or heads * ctx_rows != tok_rows:
        return shards_copied(qkv_all, context_kv, sections, groups, copies, heads, scale)

    chunks = 1
    per_section = peers // sections
    first, second = send_orders(sections, per_section)
    devices = range(sections * per_section)
    block_of = [first.index(second[group]) for group in range(groups)]
    came_from = [[first.index(d) for d in devices if d % sections == s] for s in range(sections)]
    goes_to = [[second.index(d) for d in devices if d % sections == s] for s in range(sections)]
    in_vmem = pl.BlockSpec(memory_space=pltpu.VMEM)
    params = pltpu.CompilerParams(vmem_limit_bytes=32 * 1024 * 1024)
    sent = pl.pallas_call(
        functools.partial(pack_kernel, steps, block_of, heads, ctx_rows, head_dim, chunks),
        out_shape=jax.ShapeDtypeStruct(
            (groups, tok_rows, (steps * heads * 3 + 2) * head_dim), jnp.bfloat16
        ),
        in_specs=[pl.BlockSpec(memory_space=pltpu.HBM)] * 2,
        out_specs=in_vmem,
        scratch_shapes=[
            pltpu.VMEM((steps, tok_rows, width), jnp.bfloat16),
            pltpu.VMEM(context_kv.shape, jnp.bfloat16),
            pltpu.SemaphoreType.DMA((steps, chunks)),
            pltpu.SemaphoreType.DMA,
        ],
        compiler_params=params,
    )(*(pltpu.with_memory_space_constraint(x, pltpu.HBM) for x in (qkv_all, context_kv)))
    got = exchange(sent, first)
    mixed = pl.pallas_call(
        functools.partial(
            attend_kernel, steps, heads, tok_rows, ctx_rows, head_dim, scale, came_from, goes_to
        ),
        out_shape=jax.ShapeDtypeStruct((peers, tok_rows, steps * heads * head_dim), jnp.bfloat16),
        in_specs=[in_vmem],
        out_specs=in_vmem,
        compiler_params=params,
    )(got)
    back = exchange(mixed, second)
    back = back.reshape(groups, tok_rows, steps, heads * head_dim).transpose(2, 1, 0, 3)
    return back.reshape(steps, 1, tok_rows, HEADS * head_dim)


def shards_copied(qkv_all, context_kv, sections, groups, copies, heads, scale):
    steps, _, tok_rows, width = qkv_all.shape
    head_dim = width // (3 * HEADS)
    peers = groups * copies
    share = tok_rows // copies
    ctx_rows = context_kv.shape[0]
    frames = qkv_all[:, 0].reshape(steps, tok_rows, groups, heads, 3, head_dim)
    queries = frames[..., 0, :].reshape(steps, copies, share, groups, heads, head_dim)
    queries = queries.transpose(3, 1, 0, 4, 2, 5).reshape(peers, -1, head_dim)
    key_vals = frames[..., 1:, :].transpose(2, 0, 3, 4, 1, 5).reshape(groups, -1, head_dim)
    ctx = context_kv.reshape(ctx_rows, groups, heads, 2, head_dim)
    ctx = ctx.transpose(1, 2, 3, 0, 4).reshape(groups, -1, head_dim)
    shared = jnp.concatenate([key_vals, ctx], axis=1)
    shared = jnp.broadcast_to(shared[:, None], (groups, copies) + shared.shape[1:])
    shared = shared.reshape((peers,) + shared.shape[2:])
    sent = jnp.concatenate([queries, shared], axis=1)
    got = lax.all_to_all(sent, AXES, split_axis=0, concat_axis=0, tiled=True)
    per_section = peers // sections
    cut = steps * heads * share
    end = cut + steps * heads * 2 * tok_rows
    q = got[:, :cut].reshape(per_section, sections, steps, heads, share, head_dim)
    q = q.transpose(2, 1, 3, 0, 4, 5).reshape(steps, sections, heads, -1, head_dim)
    kv = got[:, cut:end].reshape(per_section, sections, steps, heads, 2, tok_rows, head_dim)
    kv = kv.transpose(2, 1, 4, 3, 0, 5, 6).reshape(steps, sections, 2, heads, -1, head_dim)
    ctx = got[:, end:].reshape(peers, heads, 2, ctx_rows, head_dim)
    earlier = [ctx.transpose(2, 1, 0, 3, 4).reshape(2, heads, -1, head_dim)]
    results = []
    for step in range(steps):
        for s in range(sections):
            keys, vals = jnp.concatenate(earlier + [kv[step, s]], axis=2)
            results.append(
                jnp.stack([softmax_mix(q[step, s, h], keys[h], vals[h], scale) for h in range(heads)])
            )
        earlier = earlier + [kv[step, sections - 1]]
    mixed = jnp.stack(results).reshape(steps, sections, heads, per_section, share, head_dim)
    mixed = mixed.transpose(3, 1, 0, 2, 4, 5).reshape(peers, -1, head_dim)
    back = lax.all_to_all(mixed, AXES, split_axis=0, concat_axis=0, tiled=True)
    back = back.reshape(groups, copies, steps, heads, share, head_dim)
    back = back.transpose(2, 1, 4, 0, 3, 5)
    return back.reshape(steps, 1, tok_rows, HEADS * head_dim)


def solution(mesh):
    in_specs = (P(None, "section", ("rep", "seq"), None), P(("rep", "section", "seq"), None))
    out_specs = P(None, "section", ("rep", "seq"), None)
    return jax.shard_map(shards, mesh=mesh, in_specs=in_specs, out_specs=out_specs, check_vma=False)
```

```python
import functools
import math

import jax
import jax.numpy as jnp
from jax import lax
from jax.experimental import pallas as pl
from jax.experimental.pallas import tpu as pltpu
from jax.sharding import PartitionSpec as P

HEADS = 32
AXES = ("seq", "section")


def softmax_mix(queries, keys, values, scale):
    scores = (
        lax.dot_general(
            queries, keys, (((1,), (1,)), ((), ())), preferred_element_type=jnp.float32
        )
        * scale
    )
    weights = jnp.exp(scores - jnp.max(scores, axis=1, keepdims=True))
    total = jnp.sum(weights, axis=1, keepdims=True)
    mixed = jnp.dot(weights.astype(jnp.bfloat16), values, preferred_element_type=jnp.float32)
    return (mixed / total).astype(jnp.bfloat16)


def attend_kernel(
    steps, heads, tok_rows, ctx_rows, head_dim, scale, came_from, goes_to, got_ref, out_ref
):
    sections = len(came_from)
    sources = got_ref.shape[0]
    ctx_base = steps * heads * 3 * head_dim
    log2_scale = scale * math.log2(math.e)

    def part(step, section, head, role):
        base = ((step * heads + head) * 3 + role) * head_dim
        return jnp.concatenate(
            [got_ref[p, :, base : base + head_dim] for p in came_from[section]], axis=0
        )

    def context(head, role):
        base = ctx_base + role * head_dim
        rows = slice(head * ctx_rows, (head + 1) * ctx_rows)
        return got_ref[:, rows, base : base + head_dim].reshape(sources * ctx_rows, head_dim)

    def with_ones(vals):
        return jnp.concatenate([vals, jnp.ones_like(vals)], axis=1)

    def product(left, right):
        return lax.dot_general(
            left, right, (((1,), (1,)), ((), ())), preferred_element_type=jnp.float32
        )

    last = sections - 1
    ctx_tokens = sources * ctx_rows
    tokens = len(came_from[0]) * tok_rows
    blocks = [(step, s) for step in range(steps) for s in range(sections)]
    shared = [s == last and step + 1 < steps for step, s in blocks]
    allowed = [
        ctx_tokens + (step + is_shared) * tokens
        for (step, _), is_shared in zip(blocks, shared)
    ]
    every_task = []
    for head in range(heads):
        earlier = [(step, last, head) for step in range(steps - 1)]
        keys = jnp.concatenate([context(head, 0)] + [part(*e, 1) for e in earlier], axis=0)
        vals = jnp.concatenate([context(head, 1)] + [part(*e, 2) for e in earlier], axis=0)
        queries = [part(step, s, head, 0) for step, s in blocks]
        scores = product(jnp.concatenate(queries, axis=0), keys)
        lane = lax.broadcasted_iota(jnp.int32, (tokens, keys.shape[0]), 1)
        tasks = []
        for i, (step, s) in enumerate(blocks):
            common = scores[i * tokens : (i + 1) * tokens]
            if allowed[i] < keys.shape[0]:
                common = jnp.where(lane < allowed[i], common, -jnp.inf)
            own = None if shared[i] else product(queries[i], part(step, s, head, 1))
            tasks.append((common, own))
        every_task.append((tasks, vals))
    every_weight = []
    for tasks, _ in every_task:
        weights = []
        for common, own in tasks:
            top = jnp.max(common, axis=1, keepdims=True)
            if own is not None:
                top = jnp.maximum(top, jnp.max(own, axis=1, keepdims=True))
            weights.append(
                [
                    None if x is None else jnp.exp2((x - top) * log2_scale).astype(jnp.bfloat16)
                    for x in (common, own)
                ]
            )
        every_weight.append(weights)
    for head, (weights, (_, vals)) in enumerate(zip(every_weight, every_task)):
        mixed_all = jnp.dot(
            jnp.concatenate([common for common, _ in weights], axis=0),
            with_ones(vals),
            preferred_element_type=jnp.float32,
        )
        for i, (step, s) in enumerate(blocks):
            mixed = mixed_all[i * tokens : (i + 1) * tokens]
            if not shared[i]:
                mixed = mixed + jnp.dot(
                    weights[i][1],
                    with_ones(part(step, s, head, 2)),
                    preferred_element_type=jnp.float32,
                )
            done = (mixed[:, :head_dim] / mixed[:, head_dim:]).astype(jnp.bfloat16)
            base = (step * heads + head) * head_dim
            for slot, p in enumerate(goes_to[s]):
                out_ref[p, :, base : base + head_dim] = done[slot * tok_rows : (slot + 1) * tok_rows]


def pack_kernel(
    steps, block_of, heads, ctx_rows, head_dim, chunks, qkv_hbm, ctx_hbm, out_ref, qkv_ref, ctx_ref, sems, ctx_sem
):
    groups = len(block_of)
    width = heads * 3 * head_dim
    span = groups // chunks
    ctx_copy = pltpu.make_async_copy(ctx_hbm, ctx_ref, ctx_sem)
    copies = []
    for step in range(steps):
        for chunk in range(chunks):
            columns = pl.ds(chunk * span * width, span * width)
            copies.append(
                pltpu.make_async_copy(
                    qkv_hbm.at[step, 0, :, columns],
                    qkv_ref.at[step, :, columns],
                    sems.at[step, chunk],
                )
            )
    ctx_copy.start()
    for copy in copies:
        copy.start()
    base = steps * width
    ctx_copy.wait()
    for group in range(groups):
        for role in range(2):
            columns = [((group * heads + head) * 2 + role) * head_dim for head in range(heads)]
            block = [ctx_ref[:, c : c + head_dim] for c in columns]
            out_ref[block_of[group], :, base + role * head_dim : base + (role + 1) * head_dim] = (
                jnp.concatenate(block, axis=0)
            )
    for step in range(steps):
        for chunk in range(chunks):
            copies[step * chunks + chunk].wait()
            for group in range(chunk * span, (chunk + 1) * span):
                out_ref[block_of[group], :, step * width : (step + 1) * width] = qkv_ref[
                    step, :, group * width : (group + 1) * width
                ]


def exchange(blocks, order):
    return lax.all_to_all(
        blocks, AXES, split_axis=0, concat_axis=0, axis_index_groups=[order], tiled=True
    )


def send_orders(sections, per_section):
    peers = sections * per_section
    quarter = math.gcd(peers, 4)
    row = peers // quarter
    turned = [z * row + i for z in range(quarter - 1, -1, -1) for i in range(row - 1, -1, -1)]
    first = turned[row:] + turned[:row]
    half = quarter // 2
    rows = [half] + list(range(half)) + list(range(half + 1, quarter))
    second = [z * row + i for z in rows for i in range(row - 1, -1, -1)]
    return first, second


def shards(qkv_all, context_kv):
    sections = lax.axis_size("section")
    peers = sections * lax.axis_size("seq")
    groups = min(peers, HEADS)
    copies = peers // groups
    heads = HEADS // groups
    steps, _, tok_rows, width = qkv_all.shape
    head_dim = width // (3 * HEADS)
    ctx_rows = context_kv.shape[0]
    scale = head_dim ** (-0.5)
    if copies > 1 or heads * ctx_rows != tok_rows:
        return shards_copied(qkv_all, context_kv, sections, groups, copies, heads, scale)

    chunks = 1
    per_section = peers // sections
    first, second = send_orders(sections, per_section)
    devices = range(sections * per_section)
    block_of = [first.index(second[group]) for group in range(groups)]
    came_from = [[first.index(d) for d in devices if d % sections == s] for s in range(sections)]
    goes_to = [[second.index(d) for d in devices if d % sections == s] for s in range(sections)]
    in_vmem = pl.BlockSpec(memory_space=pltpu.VMEM)
    params = pltpu.CompilerParams(vmem_limit_bytes=32 * 1024 * 1024)
    sent = pl.pallas_call(
        functools.partial(pack_kernel, steps, block_of, heads, ctx_rows, head_dim, chunks),
        out_shape=jax.ShapeDtypeStruct(
            (groups, tok_rows, (steps * heads * 3 + 2) * head_dim), jnp.bfloat16
        ),
        in_specs=[pl.BlockSpec(memory_space=pltpu.HBM)] * 2,
        out_specs=in_vmem,
        scratch_shapes=[
            pltpu.VMEM((steps, tok_rows, width), jnp.bfloat16),
            pltpu.VMEM(context_kv.shape, jnp.bfloat16),
            pltpu.SemaphoreType.DMA((steps, chunks)),
            pltpu.SemaphoreType.DMA,
        ],
        compiler_params=params,
    )(*(pltpu.with_memory_space_constraint(x, pltpu.HBM) for x in (qkv_all, context_kv)))
    got = exchange(sent, first)
    mixed = pl.pallas_call(
        functools.partial(
            attend_kernel, steps, heads, tok_rows, ctx_rows, head_dim, scale, came_from, goes_to
        ),
        out_shape=jax.ShapeDtypeStruct((peers, tok_rows, steps * heads * head_dim), jnp.bfloat16),
        in_specs=[in_vmem],
        out_specs=in_vmem,
        compiler_params=params,
    )(got)
    back = exchange(mixed, second)
    back = back.reshape(groups, tok_rows, steps, heads * head_dim).transpose(2, 1, 0, 3)
    return back.reshape(steps, 1, tok_rows, HEADS * head_dim)


def shards_copied(qkv_all, context_kv, sections, groups, copies, heads, scale):
    steps, _, tok_rows, width = qkv_all.shape
    head_dim = width // (3 * HEADS)
    peers = groups * copies
    share = tok_rows // copies
    ctx_rows = context_kv.shape[0]
    frames = qkv_all[:, 0].reshape(steps, tok_rows, groups, heads, 3, head_dim)
    queries = frames[..., 0, :].reshape(steps, copies, share, groups, heads, head_dim)
    queries = queries.transpose(3, 1, 0, 4, 2, 5).reshape(peers, -1, head_dim)
    key_vals = frames[..., 1:, :].transpose(2, 0, 3, 4, 1, 5).reshape(groups, -1, head_dim)
    ctx = context_kv.reshape(ctx_rows, groups, heads, 2, head_dim)
    ctx = ctx.transpose(1, 2, 3, 0, 4).reshape(groups, -1, head_dim)
    shared = jnp.concatenate([key_vals, ctx], axis=1)
    shared = jnp.broadcast_to(shared[:, None], (groups, copies) + shared.shape[1:])
    shared = shared.reshape((peers,) + shared.shape[2:])
    sent = jnp.concatenate([queries, shared], axis=1)
    got = lax.all_to_all(sent, AXES, split_axis=0, concat_axis=0, tiled=True)
    per_section = peers // sections
    cut = steps * heads * share
    end = cut + steps * heads * 2 * tok_rows
    q = got[:, :cut].reshape(per_section, sections, steps, heads, share, head_dim)
    q = q.transpose(2, 1, 3, 0, 4, 5).reshape(steps, sections, heads, -1, head_dim)
    kv = got[:, cut:end].reshape(per_section, sections, steps, heads, 2, tok_rows, head_dim)
    kv = kv.transpose(2, 1, 4, 3, 0, 5, 6).reshape(steps, sections, 2, heads, -1, head_dim)
    ctx = got[:, end:].reshape(peers, heads, 2, ctx_rows, head_dim)
    earlier = [ctx.transpose(2, 1, 0, 3, 4).reshape(2, heads, -1, head_dim)]
    results = []
    for step in range(steps):
        for s in range(sections):
            keys, vals = jnp.concatenate(earlier + [kv[step, s]], axis=2)
            results.append(
                jnp.stack([softmax_mix(q[step, s, h], keys[h], vals[h], scale) for h in range(heads)])
            )
        earlier = earlier + [kv[step, sections - 1]]
    mixed = jnp.stack(results).reshape(steps, sections, heads, per_section, share, head_dim)
    mixed = mixed.transpose(3, 1, 0, 2, 4, 5).reshape(peers, -1, head_dim)
    back = lax.all_to_all(mixed, AXES, split_axis=0, concat_axis=0, tiled=True)
    back = back.reshape(groups, copies, steps, heads, share, head_dim)
    back = back.transpose(2, 1, 4, 0, 3, 5)
    return back.reshape(steps, 1, tok_rows, HEADS * head_dim)


def solution(mesh):
    in_specs = (P(None, "section", ("rep", "seq"), None), P(("rep", "section", "seq"), None))
    out_specs = P(None, "section", ("rep", "seq"), None)
    return jax.shard_map(shards, mesh=mesh, in_specs=in_specs, out_specs=out_specs, check_vma=False)
```

```python
import functools
import math

import jax
import jax.numpy as jnp
from jax import lax
from jax.experimental import pallas as pl
from jax.experimental.pallas import tpu as pltpu
from jax.sharding import PartitionSpec as P

HEADS = 32
AXES = ("seq", "section")


def softmax_mix(queries, keys, values, scale):
    scores = (
        lax.dot_general(
            queries, keys, (((1,), (1,)), ((), ())), preferred_element_type=jnp.float32
        )
        * scale
    )
    weights = jnp.exp(scores - jnp.max(scores, axis=1, keepdims=True))
    total = jnp.sum(weights, axis=1, keepdims=True)
    mixed = jnp.dot(weights.astype(jnp.bfloat16), values, preferred_element_type=jnp.float32)
    return (mixed / total).astype(jnp.bfloat16)


def attend_kernel(
    steps, heads, tok_rows, ctx_rows, head_dim, scale, came_from, goes_to, got_ref, out_ref
):
    sections = len(came_from)
    sources = got_ref.shape[0]
    ctx_base = steps * heads * 3 * head_dim
    log2_scale = scale * math.log2(math.e)

    def part(step, section, head, role):
        base = ((step * heads + head) * 3 + role) * head_dim
        return jnp.concatenate(
            [got_ref[p, :, base : base + head_dim] for p in came_from[section]], axis=0
        )

    def context(head, role):
        base = ctx_base + role * head_dim
        rows = slice(head * ctx_rows, (head + 1) * ctx_rows)
        return got_ref[:, rows, base : base + head_dim].reshape(sources * ctx_rows, head_dim)

    def with_ones(vals):
        return jnp.concatenate([vals, jnp.ones_like(vals)], axis=1)

    def product(left, right):
        return lax.dot_general(
            left, right, (((1,), (1,)), ((), ())), preferred_element_type=jnp.float32
        )

    last = sections - 1
    ctx_tokens = sources * ctx_rows
    tokens = len(came_from[0]) * tok_rows
    blocks = [(step, s) for step in range(steps) for s in range(sections)]
    shared = [s == last and step + 1 < steps for step, s in blocks]
    allowed = [
        ctx_tokens + (step + is_shared) * tokens
        for (step, _), is_shared in zip(blocks, shared)
    ]
    every_task = []
    for head in range(heads):
        earlier = [(step, last, head) for step in range(steps - 1)]
        keys = jnp.concatenate([context(head, 0)] + [part(*e, 1) for e in earlier], axis=0)
        vals = jnp.concatenate([context(head, 1)] + [part(*e, 2) for e in earlier], axis=0)
        queries = [part(step, s, head, 0) for step, s in blocks]
        scores = product(jnp.concatenate(queries, axis=0), keys)
        lane = lax.broadcasted_iota(jnp.int32, (tokens, keys.shape[0]), 1)
        tasks = []
        for i, (step, s) in enumerate(blocks):
            common = scores[i * tokens : (i + 1) * tokens]
            if allowed[i] < keys.shape[0]:
                common = jnp.where(lane < allowed[i], common, -jnp.inf)
            own = None if shared[i] else product(queries[i], part(step, s, head, 1))
            tasks.append((common, own))
        every_task.append((tasks, vals))
    every_weight = []
    for tasks, _ in every_task:
        weights = []
        for common, own in tasks:
            top = jnp.max(common, axis=1, keepdims=True)
            if own is not None:
                top = jnp.maximum(top, jnp.max(own, axis=1, keepdims=True))
            weights.append(
                [
                    None if x is None else jnp.exp2((x - top) * log2_scale).astype(jnp.bfloat16)
                    for x in (common, own)
                ]
            )
        every_weight.append(weights)
    for head, (weights, (_, vals)) in enumerate(zip(every_weight, every_task)):
        mixed_all = jnp.dot(
            jnp.concatenate([common for common, _ in weights], axis=0),
            with_ones(vals),
            preferred_element_type=jnp.float32,
        )
        for i, (step, s) in enumerate(blocks):
            mixed = mixed_all[i * tokens : (i + 1) * tokens]
            if not shared[i]:
                mixed = mixed + jnp.dot(
                    weights[i][1],
                    with_ones(part(step, s, head, 2)),
                    preferred_element_type=jnp.float32,
                )
            done = (mixed[:, :head_dim] / mixed[:, head_dim:]).astype(jnp.bfloat16)
            base = (step * heads + head) * head_dim
            for slot, p in enumerate(goes_to[s]):
                out_ref[p, :, base : base + head_dim] = done[slot * tok_rows : (slot + 1) * tok_rows]


def pack_kernel(
    steps, block_of, heads, ctx_rows, head_dim, chunks, qkv_hbm, ctx_hbm, out_ref, qkv_ref, ctx_ref, sems, ctx_sem
):
    groups = len(block_of)
    width = heads * 3 * head_dim
    span = groups // chunks
    ctx_copy = pltpu.make_async_copy(ctx_hbm, ctx_ref, ctx_sem)
    copies = []
    for step in range(steps):
        for chunk in range(chunks):
            columns = pl.ds(chunk * span * width, span * width)
            copies.append(
                pltpu.make_async_copy(
                    qkv_hbm.at[step, 0, :, columns],
                    qkv_ref.at[step, :, columns],
                    sems.at[step, chunk],
                )
            )
    ctx_copy.start()
    for copy in copies:
        copy.start()
    base = steps * width
    ctx_copy.wait()
    for group in range(groups):
        for role in range(2):
            columns = [((group * heads + head) * 2 + role) * head_dim for head in range(heads)]
            block = [ctx_ref[:, c : c + head_dim] for c in columns]
            out_ref[block_of[group], :, base + role * head_dim : base + (role + 1) * head_dim] = (
                jnp.concatenate(block, axis=0)
            )
    for step in range(steps):
        for chunk in range(chunks):
            copies[step * chunks + chunk].wait()
            for group in range(chunk * span, (chunk + 1) * span):
                out_ref[block_of[group], :, step * width : (step + 1) * width] = qkv_ref[
                    step, :, group * width : (group + 1) * width
                ]


def exchange(blocks, order):
    return lax.all_to_all(
        blocks, AXES, split_axis=0, concat_axis=0, axis_index_groups=[order], tiled=True
    )


def send_orders(sections, per_section):
    peers = sections * per_section
    quarter = math.gcd(peers, 4)
    row = peers // quarter
    turned = [z * row + i for z in range(quarter - 1, -1, -1) for i in range(row - 1, -1, -1)]
    first = turned[row:] + turned[:row]
    half = quarter // 2
    rows = sorted(range(quarter), key=lambda z: (abs(z - half) > 1, abs(z - half), z))
    rows = [z for z in rows if z <= half and z] + [z for z in rows if z > half] + [0]
    second = [z * row + i for z in rows for i in range(row - 1, -1, -1)]
    return first, second


def shards(qkv_all, context_kv):
    sections = lax.axis_size("section")
    peers = sections * lax.axis_size("seq")
    groups = min(peers, HEADS)
    copies = peers // groups
    heads = HEADS // groups
    steps, _, tok_rows, width = qkv_all.shape
    head_dim = width // (3 * HEADS)
    ctx_rows = context_kv.shape[0]
    scale = head_dim ** (-0.5)
    if copies > 1 or heads * ctx_rows != tok_rows:
        return shards_copied(qkv_all, context_kv, sections, groups, copies, heads, scale)

    chunks = 1
    per_section = peers // sections
    first, second = send_orders(sections, per_section)
    devices = range(sections * per_section)
    block_of = [first.index(second[group]) for group in range(groups)]
    came_from = [[first.index(d) for d in devices if d % sections == s] for s in range(sections)]
    goes_to = [[second.index(d) for d in devices if d % sections == s] for s in range(sections)]
    in_vmem = pl.BlockSpec(memory_space=pltpu.VMEM)
    params = pltpu.CompilerParams(vmem_limit_bytes=32 * 1024 * 1024)
    sent = pl.pallas_call(
        functools.partial(pack_kernel, steps, block_of, heads, ctx_rows, head_dim, chunks),
        out_shape=jax.ShapeDtypeStruct(
            (groups, tok_rows, (steps * heads * 3 + 2) * head_dim), jnp.bfloat16
        ),
        in_specs=[pl.BlockSpec(memory_space=pltpu.HBM)] * 2,
        out_specs=in_vmem,
        scratch_shapes=[
            pltpu.VMEM((steps, tok_rows, width), jnp.bfloat16),
            pltpu.VMEM(context_kv.shape, jnp.bfloat16),
            pltpu.SemaphoreType.DMA((steps, chunks)),
            pltpu.SemaphoreType.DMA,
        ],
        compiler_params=params,
    )(*(pltpu.with_memory_space_constraint(x, pltpu.HBM) for x in (qkv_all, context_kv)))
    got = exchange(sent, first)
    mixed = pl.pallas_call(
        functools.partial(
            attend_kernel, steps, heads, tok_rows, ctx_rows, head_dim, scale, came_from, goes_to
        ),
        out_shape=jax.ShapeDtypeStruct((peers, tok_rows, steps * heads * head_dim), jnp.bfloat16),
        in_specs=[in_vmem],
        out_specs=in_vmem,
        compiler_params=params,
    )(got)
    back = exchange(mixed, second)
    back = back.reshape(groups, tok_rows, steps, heads * head_dim).transpose(2, 1, 0, 3)
    return back.reshape(steps, 1, tok_rows, HEADS * head_dim)


def shards_copied(qkv_all, context_kv, sections, groups, copies, heads, scale):
    steps, _, tok_rows, width = qkv_all.shape
    head_dim = width // (3 * HEADS)
    peers = groups * copies
    share = tok_rows // copies
    ctx_rows = context_kv.shape[0]
    frames = qkv_all[:, 0].reshape(steps, tok_rows, groups, heads, 3, head_dim)
    queries = frames[..., 0, :].reshape(steps, copies, share, groups, heads, head_dim)
    queries = queries.transpose(3, 1, 0, 4, 2, 5).reshape(peers, -1, head_dim)
    key_vals = frames[..., 1:, :].transpose(2, 0, 3, 4, 1, 5).reshape(groups, -1, head_dim)
    ctx = context_kv.reshape(ctx_rows, groups, heads, 2, head_dim)
    ctx = ctx.transpose(1, 2, 3, 0, 4).reshape(groups, -1, head_dim)
    shared = jnp.concatenate([key_vals, ctx], axis=1)
    shared = jnp.broadcast_to(shared[:, None], (groups, copies) + shared.shape[1:])
    shared = shared.reshape((peers,) + shared.shape[2:])
    sent = jnp.concatenate([queries, shared], axis=1)
    got = lax.all_to_all(sent, AXES, split_axis=0, concat_axis=0, tiled=True)
    per_section = peers // sections
    cut = steps * heads * share
    end = cut + steps * heads * 2 * tok_rows
    q = got[:, :cut].reshape(per_section, sections, steps, heads, share, head_dim)
    q = q.transpose(2, 1, 3, 0, 4, 5).reshape(steps, sections, heads, -1, head_dim)
    kv = got[:, cut:end].reshape(per_section, sections, steps, heads, 2, tok_rows, head_dim)
    kv = kv.transpose(2, 1, 4, 3, 0, 5, 6).reshape(steps, sections, 2, heads, -1, head_dim)
    ctx = got[:, end:].reshape(peers, heads, 2, ctx_rows, head_dim)
    earlier = [ctx.transpose(2, 1, 0, 3, 4).reshape(2, heads, -1, head_dim)]
    results = []
    for step in range(steps):
        for s in range(sections):
            keys, vals = jnp.concatenate(earlier + [kv[step, s]], axis=2)
            results.append(
                jnp.stack([softmax_mix(q[step, s, h], keys[h], vals[h], scale) for h in range(heads)])
            )
        earlier = earlier + [kv[step, sections - 1]]
    mixed = jnp.stack(results).reshape(steps, sections, heads, per_section, share, head_dim)
    mixed = mixed.transpose(3, 1, 0, 2, 4, 5).reshape(peers, -1, head_dim)
    back = lax.all_to_all(mixed, AXES, split_axis=0, concat_axis=0, tiled=True)
    back = back.reshape(groups, copies, steps, heads, share, head_dim)
    back = back.transpose(2, 1, 4, 0, 3, 5)
    return back.reshape(steps, 1, tok_rows, HEADS * head_dim)


def solution(mesh):
    in_specs = (P(None, "section", ("rep", "seq"), None), P(("rep", "section", "seq"), None))
    out_specs = P(None, "section", ("rep", "seq"), None)
    return jax.shard_map(shards, mesh=mesh, in_specs=in_specs, out_specs=out_specs, check_vma=False)
```

```python
import functools
import math

import jax
import jax.numpy as jnp
from jax import lax
from jax.experimental import pallas as pl
from jax.experimental.pallas import tpu as pltpu
from jax.sharding import PartitionSpec as P

HEADS = 32
AXES = ("seq", "section")


def softmax_mix(queries, keys, values, scale):
    scores = (
        lax.dot_general(
            queries, keys, (((1,), (1,)), ((), ())), preferred_element_type=jnp.float32
        )
        * scale
    )
    weights = jnp.exp(scores - jnp.max(scores, axis=1, keepdims=True))
    total = jnp.sum(weights, axis=1, keepdims=True)
    mixed = jnp.dot(weights.astype(jnp.bfloat16), values, preferred_element_type=jnp.float32)
    return (mixed / total).astype(jnp.bfloat16)


def attend_kernel(
    steps, heads, tok_rows, ctx_rows, head_dim, scale, came_from, goes_to, got_ref, out_ref
):
    sections = len(came_from)
    sources = got_ref.shape[0]
    ctx_base = steps * heads * 3 * head_dim
    log2_scale = scale * math.log2(math.e)

    def part(step, section, head, role):
        base = ((step * heads + head) * 3 + role) * head_dim
        return jnp.concatenate(
            [got_ref[p, :, base : base + head_dim] for p in came_from[section]], axis=0
        )

    def context(head, role):
        base = ctx_base + role * head_dim
        rows = slice(head * ctx_rows, (head + 1) * ctx_rows)
        return got_ref[:, rows, base : base + head_dim].reshape(sources * ctx_rows, head_dim)

    def with_ones(vals):
        return jnp.concatenate([vals, jnp.ones_like(vals)], axis=1)

    def product(left, right):
        return lax.dot_general(
            left, right, (((1,), (1,)), ((), ())), preferred_element_type=jnp.float32
        )

    last = sections - 1
    ctx_tokens = sources * ctx_rows
    tokens = len(came_from[0]) * tok_rows
    blocks = [(step, s) for step in range(steps) for s in range(sections)]
    shared = [s == last and step + 1 < steps for step, s in blocks]
    allowed = [
        ctx_tokens + (step + is_shared) * tokens
        for (step, _), is_shared in zip(blocks, shared)
    ]
    every_task = []
    for head in range(heads):
        earlier = [(step, last, head) for step in range(steps - 1)]
        keys = jnp.concatenate([context(head, 0)] + [part(*e, 1) for e in earlier], axis=0)
        vals = jnp.concatenate([context(head, 1)] + [part(*e, 2) for e in earlier], axis=0)
        queries = [part(step, s, head, 0) for step, s in blocks]
        scores = product(jnp.concatenate(queries, axis=0), keys)
        lane = lax.broadcasted_iota(jnp.int32, (tokens, keys.shape[0]), 1)
        tasks = []
        for i, (step, s) in enumerate(blocks):
            common = scores[i * tokens : (i + 1) * tokens]
            if allowed[i] < keys.shape[0]:
                common = jnp.where(lane < allowed[i], common, -jnp.inf)
            own = None if shared[i] else product(queries[i], part(step, s, head, 1))
            tasks.append((common, own))
        every_task.append((tasks, vals))
    every_weight = []
    for tasks, _ in every_task:
        weights = []
        for common, own in tasks:
            top = jnp.max(common, axis=1, keepdims=True)
            if own is not None:
                top = jnp.maximum(top, jnp.max(own, axis=1, keepdims=True))
            weights.append(
                [
                    None if x is None else jnp.exp2((x - top) * log2_scale).astype(jnp.bfloat16)
                    for x in (common, own)
                ]
            )
        every_weight.append(weights)
    for head, (weights, (_, vals)) in enumerate(zip(every_weight, every_task)):
        mixed_all = jnp.dot(
            jnp.concatenate([common for common, _ in weights], axis=0),
            with_ones(vals),
            preferred_element_type=jnp.float32,
        )
        for i, (step, s) in enumerate(blocks):
            mixed = mixed_all[i * tokens : (i + 1) * tokens]
            if not shared[i]:
                mixed = mixed + jnp.dot(
                    weights[i][1],
                    with_ones(part(step, s, head, 2)),
                    preferred_element_type=jnp.float32,
                )
            done = (mixed[:, :head_dim] / mixed[:, head_dim:]).astype(jnp.bfloat16)
            base = (step * heads + head) * head_dim
            for slot, p in enumerate(goes_to[s]):
                out_ref[p, :, base : base + head_dim] = done[slot * tok_rows : (slot + 1) * tok_rows]


def pack_kernel(
    steps, block_of, heads, ctx_rows, head_dim, chunks, qkv_hbm, ctx_hbm, out_ref, qkv_ref, ctx_ref, sems, ctx_sem
):
    groups = len(block_of)
    width = heads * 3 * head_dim
    span = groups // chunks
    ctx_copy = pltpu.make_async_copy(ctx_hbm, ctx_ref, ctx_sem)
    copies = []
    for step in range(steps):
        for chunk in range(chunks):
            columns = pl.ds(chunk * span * width, span * width)
            copies.append(
                pltpu.make_async_copy(
                    qkv_hbm.at[step, 0, :, columns],
                    qkv_ref.at[step, :, columns],
                    sems.at[step, chunk],
                )
            )
    ctx_copy.start()
    for copy in copies:
        copy.start()
    base = steps * width
    ctx_copy.wait()
    for group in range(groups):
        for role in range(2):
            columns = [((group * heads + head) * 2 + role) * head_dim for head in range(heads)]
            block = [ctx_ref[:, c : c + head_dim] for c in columns]
            out_ref[block_of[group], :, base + role * head_dim : base + (role + 1) * head_dim] = (
                jnp.concatenate(block, axis=0)
            )
    for step in range(steps):
        for chunk in range(chunks):
            copies[step * chunks + chunk].wait()
            for group in range(chunk * span, (chunk + 1) * span):
                out_ref[block_of[group], :, step * width : (step + 1) * width] = qkv_ref[
                    step, :, group * width : (group + 1) * width
                ]


def exchange(blocks, order):
    return lax.all_to_all(
        blocks, AXES, split_axis=0, concat_axis=0, axis_index_groups=[order], tiled=True
    )


def send_orders(sections, per_section):
    peers = sections * per_section
    quarter = math.gcd(peers, 4)
    row = peers // quarter
    half = quarter // 2
    spread = [half] + list(range(half)) + list(range(half + 1, quarter))
    first = [z * row + i for z in spread for i in range(row - 1, -1, -1)]
    rows = list(range(half, quarter)) + list(range(half))
    second = [z * row + i for z in rows for i in range(row - 1, -1, -1)]
    return first, second


def shards(qkv_all, context_kv):
    sections = lax.axis_size("section")
    peers = sections * lax.axis_size("seq")
    groups = min(peers, HEADS)
    copies = peers // groups
    heads = HEADS // groups
    steps, _, tok_rows, width = qkv_all.shape
    head_dim = width // (3 * HEADS)
    ctx_rows = context_kv.shape[0]
    scale = head_dim ** (-0.5)
    if copies > 1 or heads * ctx_rows != tok_rows:
        return shards_copied(qkv_all, context_kv, sections, groups, copies, heads, scale)

    chunks = 1
    per_section = peers // sections
    first, second = send_orders(sections, per_section)
    devices = range(sections * per_section)
    block_of = [first.index(second[group]) for group in range(groups)]
    came_from = [[first.index(d) for d in devices if d % sections == s] for s in range(sections)]
    goes_to = [[second.index(d) for d in devices if d % sections == s] for s in range(sections)]
    in_vmem = pl.BlockSpec(memory_space=pltpu.VMEM)
    params = pltpu.CompilerParams(vmem_limit_bytes=32 * 1024 * 1024)
    sent = pl.pallas_call(
        functools.partial(pack_kernel, steps, block_of, heads, ctx_rows, head_dim, chunks),
        out_shape=jax.ShapeDtypeStruct(
            (groups, tok_rows, (steps * heads * 3 + 2) * head_dim), jnp.bfloat16
        ),
        in_specs=[pl.BlockSpec(memory_space=pltpu.HBM)] * 2,
        out_specs=in_vmem,
        scratch_shapes=[
            pltpu.VMEM((steps, tok_rows, width), jnp.bfloat16),
            pltpu.VMEM(context_kv.shape, jnp.bfloat16),
            pltpu.SemaphoreType.DMA((steps, chunks)),
            pltpu.SemaphoreType.DMA,
        ],
        compiler_params=params,
    )(*(pltpu.with_memory_space_constraint(x, pltpu.HBM) for x in (qkv_all, context_kv)))
    got = exchange(sent, first)
    mixed = pl.pallas_call(
        functools.partial(
            attend_kernel, steps, heads, tok_rows, ctx_rows, head_dim, scale, came_from, goes_to
        ),
        out_shape=jax.ShapeDtypeStruct((peers, tok_rows, steps * heads * head_dim), jnp.bfloat16),
        in_specs=[in_vmem],
        out_specs=in_vmem,
        compiler_params=params,
    )(got)
    back = exchange(mixed, second)
    back = back.reshape(groups, tok_rows, steps, heads * head_dim).transpose(2, 1, 0, 3)
    return back.reshape(steps, 1, tok_rows, HEADS * head_dim)


def shards_copied(qkv_all, context_kv, sections, groups, copies, heads, scale):
    steps, _, tok_rows, width = qkv_all.shape
    head_dim = width // (3 * HEADS)
    peers = groups * copies
    share = tok_rows // copies
    ctx_rows = context_kv.shape[0]
    frames = qkv_all[:, 0].reshape(steps, tok_rows, groups, heads, 3, head_dim)
    queries = frames[..., 0, :].reshape(steps, copies, share, groups, heads, head_dim)
    queries = queries.transpose(3, 1, 0, 4, 2, 5).reshape(peers, -1, head_dim)
    key_vals = frames[..., 1:, :].transpose(2, 0, 3, 4, 1, 5).reshape(groups, -1, head_dim)
    ctx = context_kv.reshape(ctx_rows, groups, heads, 2, head_dim)
    ctx = ctx.transpose(1, 2, 3, 0, 4).reshape(groups, -1, head_dim)
    shared = jnp.concatenate([key_vals, ctx], axis=1)
    shared = jnp.broadcast_to(shared[:, None], (groups, copies) + shared.shape[1:])
    shared = shared.reshape((peers,) + shared.shape[2:])
    sent = jnp.concatenate([queries, shared], axis=1)
    got = lax.all_to_all(sent, AXES, split_axis=0, concat_axis=0, tiled=True)
    per_section = peers // sections
    cut = steps * heads * share
    end = cut + steps * heads * 2 * tok_rows
    q = got[:, :cut].reshape(per_section, sections, steps, heads, share, head_dim)
    q = q.transpose(2, 1, 3, 0, 4, 5).reshape(steps, sections, heads, -1, head_dim)
    kv = got[:, cut:end].reshape(per_section, sections, steps, heads, 2, tok_rows, head_dim)
    kv = kv.transpose(2, 1, 4, 3, 0, 5, 6).reshape(steps, sections, 2, heads, -1, head_dim)
    ctx = got[:, end:].reshape(peers, heads, 2, ctx_rows, head_dim)
    earlier = [ctx.transpose(2, 1, 0, 3, 4).reshape(2, heads, -1, head_dim)]
    results = []
    for step in range(steps):
        for s in range(sections):
            keys, vals = jnp.concatenate(earlier + [kv[step, s]], axis=2)
            results.append(
                jnp.stack([softmax_mix(q[step, s, h], keys[h], vals[h], scale) for h in range(heads)])
            )
        earlier = earlier + [kv[step, sections - 1]]
    mixed = jnp.stack(results).reshape(steps, sections, heads, per_section, share, head_dim)
    mixed = mixed.transpose(3, 1, 0, 2, 4, 5).reshape(peers, -1, head_dim)
    back = lax.all_to_all(mixed, AXES, split_axis=0, concat_axis=0, tiled=True)
    back = back.reshape(groups, copies, steps, heads, share, head_dim)
    back = back.transpose(2, 1, 4, 0, 3, 5)
    return back.reshape(steps, 1, tok_rows, HEADS * head_dim)


def solution(mesh):
    in_specs = (P(None, "section", ("rep", "seq"), None), P(("rep", "section", "seq"), None))
    out_specs = P(None, "section", ("rep", "seq"), None)
    return jax.shard_map(shards, mesh=mesh, in_specs=in_specs, out_specs=out_specs, check_vma=False)
```

```python
import functools
import math

import jax
import jax.numpy as jnp
from jax import lax
from jax.experimental import pallas as pl
from jax.experimental.pallas import tpu as pltpu
from jax.sharding import PartitionSpec as P

HEADS = 32
AXES = ("seq", "section")


def softmax_mix(queries, keys, values, scale):
    scores = (
        lax.dot_general(
            queries, keys, (((1,), (1,)), ((), ())), preferred_element_type=jnp.float32
        )
        * scale
    )
    weights = jnp.exp(scores - jnp.max(scores, axis=1, keepdims=True))
    total = jnp.sum(weights, axis=1, keepdims=True)
    mixed = jnp.dot(weights.astype(jnp.bfloat16), values, preferred_element_type=jnp.float32)
    return (mixed / total).astype(jnp.bfloat16)


def attend_kernel(
    steps, heads, tok_rows, ctx_rows, head_dim, scale, came_from, goes_to, got_ref, out_ref
):
    sections = len(came_from)
    sources = got_ref.shape[0]
    ctx_base = steps * heads * 3 * head_dim
    log2_scale = scale * math.log2(math.e)

    def part(step, section, head, role):
        base = ((step * heads + head) * 3 + role) * head_dim
        return jnp.concatenate(
            [got_ref[p, :, base : base + head_dim] for p in came_from[section]], axis=0
        )

    def context(head, role):
        base = ctx_base + role * head_dim
        rows = slice(head * ctx_rows, (head + 1) * ctx_rows)
        return got_ref[:, rows, base : base + head_dim].reshape(sources * ctx_rows, head_dim)

    def with_ones(vals):
        return jnp.concatenate([vals, jnp.ones_like(vals)], axis=1)

    def product(left, right):
        return lax.dot_general(
            left, right, (((1,), (1,)), ((), ())), preferred_element_type=jnp.float32
        )

    last = sections - 1
    ctx_tokens = sources * ctx_rows
    tokens = len(came_from[0]) * tok_rows
    blocks = [(step, s) for step in range(steps) for s in range(sections)]
    shared = [s == last and step + 1 < steps for step, s in blocks]
    allowed = [
        ctx_tokens + (step + is_shared) * tokens
        for (step, _), is_shared in zip(blocks, shared)
    ]
    every_task = []
    for head in range(heads):
        earlier = [(step, last, head) for step in range(steps - 1)]
        keys = jnp.concatenate([context(head, 0)] + [part(*e, 1) for e in earlier], axis=0)
        vals = jnp.concatenate([context(head, 1)] + [part(*e, 2) for e in earlier], axis=0)
        queries = [part(step, s, head, 0) for step, s in blocks]
        scores = product(jnp.concatenate(queries, axis=0), keys)
        lane = lax.broadcasted_iota(jnp.int32, (tokens, keys.shape[0]), 1)
        tasks = []
        for i, (step, s) in enumerate(blocks):
            common = scores[i * tokens : (i + 1) * tokens]
            if allowed[i] < keys.shape[0]:
                common = jnp.where(lane < allowed[i], common, -jnp.inf)
            own = None if shared[i] else product(queries[i], part(step, s, head, 1))
            tasks.append((common, own))
        every_task.append((tasks, vals))
    every_weight = []
    for tasks, _ in every_task:
        weights = []
        for common, own in tasks:
            top = jnp.max(common, axis=1, keepdims=True)
            if own is not None:
                top = jnp.maximum(top, jnp.max(own, axis=1, keepdims=True))
            weights.append(
                [
                    None if x is None else jnp.exp2((x - top) * log2_scale).astype(jnp.bfloat16)
                    for x in (common, own)
                ]
            )
        every_weight.append(weights)
    for head, (weights, (_, vals)) in enumerate(zip(every_weight, every_task)):
        mixed_all = jnp.dot(
            jnp.concatenate([common for common, _ in weights], axis=0),
            with_ones(vals),
            preferred_element_type=jnp.float32,
        )
        for i, (step, s) in enumerate(blocks):
            mixed = mixed_all[i * tokens : (i + 1) * tokens]
            if not shared[i]:
                mixed = mixed + jnp.dot(
                    weights[i][1],
                    with_ones(part(step, s, head, 2)),
                    preferred_element_type=jnp.float32,
                )
            done = (mixed[:, :head_dim] * (1.0 / mixed[:, head_dim:])).astype(jnp.bfloat16)
            base = (step * heads + head) * head_dim
            for slot, p in enumerate(goes_to[s]):
                out_ref[p, :, base : base + head_dim] = done[slot * tok_rows : (slot + 1) * tok_rows]


def pack_kernel(
    steps, block_of, heads, ctx_rows, head_dim, chunks, qkv_hbm, ctx_hbm, out_ref, qkv_ref, ctx_ref, sems, ctx_sem
):
    groups = len(block_of)
    width = heads * 3 * head_dim
    span = groups // chunks
    ctx_copy = pltpu.make_async_copy(ctx_hbm, ctx_ref, ctx_sem)
    copies = []
    for step in range(steps):
        for chunk in range(chunks):
            columns = pl.ds(chunk * span * width, span * width)
            copies.append(
                pltpu.make_async_copy(
                    qkv_hbm.at[step, 0, :, columns],
                    qkv_ref.at[step, :, columns],
                    sems.at[step, chunk],
                )
            )
    for copy in copies:
        copy.start()
    ctx_copy.start()
    base = steps * width
    ctx_copy.wait()
    for group in range(groups):
        for role in range(2):
            columns = [((group * heads + head) * 2 + role) * head_dim for head in range(heads)]
            block = [ctx_ref[:, c : c + head_dim] for c in columns]
            out_ref[block_of[group], :, base + role * head_dim : base + (role + 1) * head_dim] = (
                jnp.concatenate(block, axis=0)
            )
    for step in range(steps):
        for chunk in range(chunks):
            copies[step * chunks + chunk].wait()
            for group in range(chunk * span, (chunk + 1) * span):
                out_ref[block_of[group], :, step * width : (step + 1) * width] = qkv_ref[
                    step, :, group * width : (group + 1) * width
                ]


def exchange(blocks, order):
    return lax.all_to_all(
        blocks, AXES, split_axis=0, concat_axis=0, axis_index_groups=[order], tiled=True
    )


def send_orders(sections, per_section):
    peers = sections * per_section
    quarter = math.gcd(peers, 4)
    row = peers // quarter
    turned = [z * row + i for z in range(quarter - 1, -1, -1) for i in range(row - 1, -1, -1)]
    first = turned[row:] + turned[:row]
    half = quarter // 2
    rows = sorted(range(quarter), key=lambda z: (abs(z - half) > 1, abs(z - half), z))
    rows = [z for z in rows if z <= half and z] + [z for z in rows if z > half] + [0]
    second = [z * row + i for z in rows for i in range(row - 1, -1, -1)]
    return first, second


def shards(qkv_all, context_kv):
    sections = lax.axis_size("section")
    peers = sections * lax.axis_size("seq")
    groups = min(peers, HEADS)
    copies = peers // groups
    heads = HEADS // groups
    steps, _, tok_rows, width = qkv_all.shape
    head_dim = width // (3 * HEADS)
    ctx_rows = context_kv.shape[0]
    scale = head_dim ** (-0.5)
    if copies > 1 or heads * ctx_rows != tok_rows:
        return shards_copied(qkv_all, context_kv, sections, groups, copies, heads, scale)

    chunks = 1
    per_section = peers // sections
    first, second = send_orders(sections, per_section)
    devices = range(sections * per_section)
    block_of = [first.index(second[group]) for group in range(groups)]
    came_from = [[first.index(d) for d in devices if d % sections == s] for s in range(sections)]
    goes_to = [[second.index(d) for d in devices if d % sections == s] for s in range(sections)]
    in_vmem = pl.BlockSpec(memory_space=pltpu.VMEM)
    params = pltpu.CompilerParams(vmem_limit_bytes=32 * 1024 * 1024)
    sent = pl.pallas_call(
        functools.partial(pack_kernel, steps, block_of, heads, ctx_rows, head_dim, chunks),
        out_shape=jax.ShapeDtypeStruct(
            (groups, tok_rows, (steps * heads * 3 + 2) * head_dim), jnp.bfloat16
        ),
        in_specs=[pl.BlockSpec(memory_space=pltpu.HBM)] * 2,
        out_specs=in_vmem,
        scratch_shapes=[
            pltpu.VMEM((steps, tok_rows, width), jnp.bfloat16),
            pltpu.VMEM(context_kv.shape, jnp.bfloat16),
            pltpu.SemaphoreType.DMA((steps, chunks)),
            pltpu.SemaphoreType.DMA,
        ],
        compiler_params=params,
    )(*(pltpu.with_memory_space_constraint(x, pltpu.HBM) for x in (qkv_all, context_kv)))
    got = exchange(sent, first)
    mixed = pl.pallas_call(
        functools.partial(
            attend_kernel, steps, heads, tok_rows, ctx_rows, head_dim, scale, came_from, goes_to
        ),
        out_shape=jax.ShapeDtypeStruct((peers, tok_rows, steps * heads * head_dim), jnp.bfloat16),
        in_specs=[in_vmem],
        out_specs=in_vmem,
        compiler_params=params,
    )(got)
    back = exchange(mixed, second)
    back = back.reshape(groups, tok_rows, steps, heads * head_dim).transpose(2, 1, 0, 3)
    return back.reshape(steps, 1, tok_rows, HEADS * head_dim)


def shards_copied(qkv_all, context_kv, sections, groups, copies, heads, scale):
    steps, _, tok_rows, width = qkv_all.shape
    head_dim = width // (3 * HEADS)
    peers = groups * copies
    share = tok_rows // copies
    ctx_rows = context_kv.shape[0]
    frames = qkv_all[:, 0].reshape(steps, tok_rows, groups, heads, 3, head_dim)
    queries = frames[..., 0, :].reshape(steps, copies, share, groups, heads, head_dim)
    queries = queries.transpose(3, 1, 0, 4, 2, 5).reshape(peers, -1, head_dim)
    key_vals = frames[..., 1:, :].transpose(2, 0, 3, 4, 1, 5).reshape(groups, -1, head_dim)
    ctx = context_kv.reshape(ctx_rows, groups, heads, 2, head_dim)
    ctx = ctx.transpose(1, 2, 3, 0, 4).reshape(groups, -1, head_dim)
    shared = jnp.concatenate([key_vals, ctx], axis=1)
    shared = jnp.broadcast_to(shared[:, None], (groups, copies) + shared.shape[1:])
    shared = shared.reshape((peers,) + shared.shape[2:])
    sent = jnp.concatenate([queries, shared], axis=1)
    got = lax.all_to_all(sent, AXES, split_axis=0, concat_axis=0, tiled=True)
    per_section = peers // sections
    cut = steps * heads * share
    end = cut + steps * heads * 2 * tok_rows
    q = got[:, :cut].reshape(per_section, sections, steps, heads, share, head_dim)
    q = q.transpose(2, 1, 3, 0, 4, 5).reshape(steps, sections, heads, -1, head_dim)
    kv = got[:, cut:end].reshape(per_section, sections, steps, heads, 2, tok_rows, head_dim)
    kv = kv.transpose(2, 1, 4, 3, 0, 5, 6).reshape(steps, sections, 2, heads, -1, head_dim)
    ctx = got[:, end:].reshape(peers, heads, 2, ctx_rows, head_dim)
    earlier = [ctx.transpose(2, 1, 0, 3, 4).reshape(2, heads, -1, head_dim)]
    results = []
    for step in range(steps):
        for s in range(sections):
            keys, vals = jnp.concatenate(earlier + [kv[step, s]], axis=2)
            results.append(
                jnp.stack([softmax_mix(q[step, s, h], keys[h], vals[h], scale) for h in range(heads)])
            )
        earlier = earlier + [kv[step, sections - 1]]
    mixed = jnp.stack(results).reshape(steps, sections, heads, per_section, share, head_dim)
    mixed = mixed.transpose(3, 1, 0, 2, 4, 5).reshape(peers, -1, head_dim)
    back = lax.all_to_all(mixed, AXES, split_axis=0, concat_axis=0, tiled=True)
    back = back.reshape(groups, copies, steps, heads, share, head_dim)
    back = back.transpose(2, 1, 4, 0, 3, 5)
    return back.reshape(steps, 1, tok_rows, HEADS * head_dim)


def solution(mesh):
    in_specs = (P(None, "section", ("rep", "seq"), None), P(("rep", "section", "seq"), None))
    out_specs = P(None, "section", ("rep", "seq"), None)
    return jax.shard_map(shards, mesh=mesh, in_specs=in_specs, out_specs=out_specs, check_vma=False)
```

```python
import functools
import math

import jax
import jax.numpy as jnp
from jax import lax
from jax.experimental import pallas as pl
from jax.experimental.pallas import tpu as pltpu
from jax.sharding import PartitionSpec as P

HEADS = 32
AXES = ("seq", "section")


def softmax_mix(queries, keys, values, scale):
    scores = (
        lax.dot_general(
            queries, keys, (((1,), (1,)), ((), ())), preferred_element_type=jnp.float32
        )
        * scale
    )
    weights = jnp.exp(scores - jnp.max(scores, axis=1, keepdims=True))
    total = jnp.sum(weights, axis=1, keepdims=True)
    mixed = jnp.dot(weights.astype(jnp.bfloat16), values, preferred_element_type=jnp.float32)
    return (mixed / total).astype(jnp.bfloat16)


def attend_kernel(
    steps, heads, tok_rows, ctx_rows, head_dim, scale, came_from, goes_to, got_ref, out_ref
):
    sections = len(came_from)
    sources = got_ref.shape[0]
    ctx_base = steps * heads * 3 * head_dim
    log2_scale = scale * math.log2(math.e)

    def part(step, section, head, role):
        base = ((step * heads + head) * 3 + role) * head_dim
        return jnp.concatenate(
            [got_ref[p, :, base : base + head_dim] for p in came_from[section]], axis=0
        )

    def context(head, role):
        base = ctx_base + role * head_dim
        rows = slice(head * ctx_rows, (head + 1) * ctx_rows)
        return got_ref[:, rows, base : base + head_dim].reshape(sources * ctx_rows, head_dim)

    def with_ones(vals):
        return jnp.concatenate([vals, jnp.ones_like(vals)], axis=1)

    def product(left, right):
        return lax.dot_general(
            left, right, (((1,), (1,)), ((), ())), preferred_element_type=jnp.float32
        )

    last = sections - 1
    ctx_tokens = sources * ctx_rows
    tokens = len(came_from[0]) * tok_rows
    blocks = [(step, s) for step in range(steps) for s in range(sections)]
    shared = [s == last and step + 1 < steps for step, s in blocks]
    allowed = [
        ctx_tokens + (step + is_shared) * tokens
        for (step, _), is_shared in zip(blocks, shared)
    ]
    every_task = []
    for head in range(heads):
        earlier = [(step, last, head) for step in range(steps - 1)]
        keys = jnp.concatenate([context(head, 0)] + [part(*e, 1) for e in earlier], axis=0)
        vals = jnp.concatenate([context(head, 1)] + [part(*e, 2) for e in earlier], axis=0)
        queries = [part(step, s, head, 0) for step, s in blocks]
        scores = product(jnp.concatenate(queries, axis=0), keys)
        lane = lax.broadcasted_iota(jnp.int32, (tokens, keys.shape[0]), 1)
        tasks = []
        for i, (step, s) in enumerate(blocks):
            common = scores[i * tokens : (i + 1) * tokens]
            if allowed[i] < keys.shape[0]:
                common = jnp.where(lane < allowed[i], common, -jnp.inf)
            own = None if shared[i] else product(queries[i], part(step, s, head, 1))
            tasks.append((common, own))
        every_task.append((tasks, vals))
    every_weight = []
    for tasks, _ in every_task:
        weights = []
        for common, own in tasks:
            top = jnp.max(common, axis=1, keepdims=True)
            if own is not None:
                top = jnp.maximum(top, jnp.max(own, axis=1, keepdims=True))
            weights.append(
                [
                    None if x is None else jnp.exp2((x - top) * log2_scale).astype(jnp.bfloat16)
                    for x in (common, own)
                ]
            )
        every_weight.append(weights)
    for head, (weights, (_, vals)) in enumerate(zip(every_weight, every_task)):
        mixed_all = jnp.dot(
            jnp.concatenate([common for common, _ in weights], axis=0),
            with_ones(vals),
            preferred_element_type=jnp.float32,
        )
        for i, (step, s) in enumerate(blocks):
            mixed = mixed_all[i * tokens : (i + 1) * tokens]
            if not shared[i]:
                mixed = mixed + jnp.dot(
                    weights[i][1],
                    with_ones(part(step, s, head, 2)),
                    preferred_element_type=jnp.float32,
                )
            done = (mixed[:, :head_dim] * (1.0 / mixed[:, head_dim:])).astype(jnp.bfloat16)
            base = (step * heads + head) * head_dim
            for slot, p in enumerate(goes_to[s]):
                out_ref[p, :, base : base + head_dim] = done[slot * tok_rows : (slot + 1) * tok_rows]


def pack_kernel(
    steps, block_of, heads, ctx_rows, head_dim, chunks, qkv_hbm, ctx_hbm, out_ref, qkv_ref, ctx_ref, sems, ctx_sem
):
    groups = len(block_of)
    width = heads * 3 * head_dim
    span = groups // chunks
    ctx_copy = pltpu.make_async_copy(ctx_hbm, ctx_ref, ctx_sem)
    copies = []
    for step in range(steps):
        for chunk in range(chunks):
            columns = pl.ds(chunk * span * width, span * width)
            copies.append(
                pltpu.make_async_copy(
                    qkv_hbm.at[step, 0, :, columns],
                    qkv_ref.at[step, :, columns],
                    sems.at[step, chunk],
                )
            )
    for copy in copies:
        copy.start()
    ctx_copy.start()
    base = steps * width
    ctx_copy.wait()
    for group in range(groups):
        for role in range(2):
            columns = [((group * heads + head) * 2 + role) * head_dim for head in range(heads)]
            block = [ctx_ref[:, c : c + head_dim] for c in columns]
            out_ref[block_of[group], :, base + role * head_dim : base + (role + 1) * head_dim] = (
                jnp.concatenate(block, axis=0)
            )
    for step in range(steps):
        for chunk in range(chunks):
            copies[step * chunks + chunk].wait()
            for group in range(chunk * span, (chunk + 1) * span):
                out_ref[block_of[group], :, step * width : (step + 1) * width] = qkv_ref[
                    step, :, group * width : (group + 1) * width
                ]


def exchange(blocks, order):
    return lax.all_to_all(
        blocks, AXES, split_axis=0, concat_axis=0, axis_index_groups=[order], tiled=True
    )


def send_orders(sections, per_section):
    peers = sections * per_section
    quarter = math.gcd(peers, 4)
    row = peers // quarter
    turned = [z * row + i for z in range(quarter - 1, -1, -1) for i in range(row - 1, -1, -1)]
    first = turned[row:] + turned[:row]
    half = quarter // 2
    rows = list(range(half, quarter)) + list(range(half))
    second = [z * row + i for z in rows for i in range(row - 1, -1, -1)]
    return first, second


def shards(qkv_all, context_kv):
    sections = lax.axis_size("section")
    peers = sections * lax.axis_size("seq")
    groups = min(peers, HEADS)
    copies = peers // groups
    heads = HEADS // groups
    steps, _, tok_rows, width = qkv_all.shape
    head_dim = width // (3 * HEADS)
    ctx_rows = context_kv.shape[0]
    scale = head_dim ** (-0.5)
    if copies > 1 or heads * ctx_rows != tok_rows:
        return shards_copied(qkv_all, context_kv, sections, groups, copies, heads, scale)

    chunks = 1
    per_section = peers // sections
    first, second = send_orders(sections, per_section)
    devices = range(sections * per_section)
    block_of = [first.index(second[group]) for group in range(groups)]
    came_from = [[first.index(d) for d in devices if d % sections == s] for s in range(sections)]
    goes_to = [[second.index(d) for d in devices if d % sections == s] for s in range(sections)]
    in_vmem = pl.BlockSpec(memory_space=pltpu.VMEM)
    params = pltpu.CompilerParams(vmem_limit_bytes=32 * 1024 * 1024)
    sent = pl.pallas_call(
        functools.partial(pack_kernel, steps, block_of, heads, ctx_rows, head_dim, chunks),
        out_shape=jax.ShapeDtypeStruct(
            (groups, tok_rows, (steps * heads * 3 + 2) * head_dim), jnp.bfloat16
        ),
        in_specs=[pl.BlockSpec(memory_space=pltpu.HBM)] * 2,
        out_specs=in_vmem,
        scratch_shapes=[
            pltpu.VMEM((steps, tok_rows, width), jnp.bfloat16),
            pltpu.VMEM(context_kv.shape, jnp.bfloat16),
            pltpu.SemaphoreType.DMA((steps, chunks)),
            pltpu.SemaphoreType.DMA,
        ],
        compiler_params=params,
    )(*(pltpu.with_memory_space_constraint(x, pltpu.HBM) for x in (qkv_all, context_kv)))
    got = exchange(sent, first)
    mixed = pl.pallas_call(
        functools.partial(
            attend_kernel, steps, heads, tok_rows, ctx_rows, head_dim, scale, came_from, goes_to
        ),
        out_shape=jax.ShapeDtypeStruct((peers, tok_rows, steps * heads * head_dim), jnp.bfloat16),
        in_specs=[in_vmem],
        out_specs=in_vmem,
        compiler_params=params,
    )(got)
    back = exchange(mixed, second)
    back = back.reshape(groups, tok_rows, steps, heads * head_dim).transpose(2, 1, 0, 3)
    return back.reshape(steps, 1, tok_rows, HEADS * head_dim)


def shards_copied(qkv_all, context_kv, sections, groups, copies, heads, scale):
    steps, _, tok_rows, width = qkv_all.shape
    head_dim = width // (3 * HEADS)
    peers = groups * copies
    share = tok_rows // copies
    ctx_rows = context_kv.shape[0]
    frames = qkv_all[:, 0].reshape(steps, tok_rows, groups, heads, 3, head_dim)
    queries = frames[..., 0, :].reshape(steps, copies, share, groups, heads, head_dim)
    queries = queries.transpose(3, 1, 0, 4, 2, 5).reshape(peers, -1, head_dim)
    key_vals = frames[..., 1:, :].transpose(2, 0, 3, 4, 1, 5).reshape(groups, -1, head_dim)
    ctx = context_kv.reshape(ctx_rows, groups, heads, 2, head_dim)
    ctx = ctx.transpose(1, 2, 3, 0, 4).reshape(groups, -1, head_dim)
    shared = jnp.concatenate([key_vals, ctx], axis=1)
    shared = jnp.broadcast_to(shared[:, None], (groups, copies) + shared.shape[1:])
    shared = shared.reshape((peers,) + shared.shape[2:])
    sent = jnp.concatenate([queries, shared], axis=1)
    got = lax.all_to_all(sent, AXES, split_axis=0, concat_axis=0, tiled=True)
    per_section = peers // sections
    cut = steps * heads * share
    end = cut + steps * heads * 2 * tok_rows
    q = got[:, :cut].reshape(per_section, sections, steps, heads, share, head_dim)
    q = q.transpose(2, 1, 3, 0, 4, 5).reshape(steps, sections, heads, -1, head_dim)
    kv = got[:, cut:end].reshape(per_section, sections, steps, heads, 2, tok_rows, head_dim)
    kv = kv.transpose(2, 1, 4, 3, 0, 5, 6).reshape(steps, sections, 2, heads, -1, head_dim)
    ctx = got[:, end:].reshape(peers, heads, 2, ctx_rows, head_dim)
    earlier = [ctx.transpose(2, 1, 0, 3, 4).reshape(2, heads, -1, head_dim)]
    results = []
    for step in range(steps):
        for s in range(sections):
            keys, vals = jnp.concatenate(earlier + [kv[step, s]], axis=2)
            results.append(
                jnp.stack([softmax_mix(q[step, s, h], keys[h], vals[h], scale) for h in range(heads)])
            )
        earlier = earlier + [kv[step, sections - 1]]
    mixed = jnp.stack(results).reshape(steps, sections, heads, per_section, share, head_dim)
    mixed = mixed.transpose(3, 1, 0, 2, 4, 5).reshape(peers, -1, head_dim)
    back = lax.all_to_all(mixed, AXES, split_axis=0, concat_axis=0, tiled=True)
    back = back.reshape(groups, copies, steps, heads, share, head_dim)
    back = back.transpose(2, 1, 4, 0, 3, 5)
    return back.reshape(steps, 1, tok_rows, HEADS * head_dim)


def solution(mesh):
    in_specs = (P(None, "section", ("rep", "seq"), None), P(("rep", "section", "seq"), None))
    out_specs = P(None, "section", ("rep", "seq"), None)
    return jax.shard_map(shards, mesh=mesh, in_specs=in_specs, out_specs=out_specs, check_vma=False)
```
